32 devices in a mesh: ctx: 4 (over y, x), tp: 2 (over core), dp: 4 (over z).
Axes of the slice: x: 2, y: 2, z: 4, core: 2. Of those that a mesh axis runs over, the one named last changes fastest.
Arguments:
- queries: bfloat16 [2048, 8192], P(('dp', 'ctx'), 'tp'), parts along dimension 0
- key_rows: bfloat16 [2048, 1024], P(('dp', 'ctx'), 'tp'), parts along dimension 0
- value_rows: bfloat16 [2048, 1024], P(('dp', 'ctx'), 'tp'), parts along dimension 0, may hold values from -6 to 6
- doc_lengths: int32 [32], P('dp'), parts along dimension 0, may hold values from 1 to 256, 512 in all
- unit_source: int32 [64], P('dp'), parts along dimension 0, may hold values from 0 to 15, as said below
- w_out: bfloat16 [8192, 16384], P('tp', 'ctx'), may hold values from -0.0625 to 0.0625
Outputs:
- projected: bfloat16 [2048, 16384], P(('dp', 'tp'), 'ctx'), parts along dimension 0
The draws below stay inside these ranges and needn't reach their ends.
There are 4 independent parts, one for each index of `dp`. The reference program is written for one: setup_inputs(seed, part) draws one part's arguments, and reference() takes and returns one part's arrays. A program takes and returns all parts, laid end to end along the dimension named above; an argument that names none is the same for every part. Nothing has to cross between parts.
Inputs may be any that keep to these rules, and one draw needn't show every extreme that they name: `unit_source`: each run of 4 slots (one device's units in the balanced order) holds exactly one unit from every run of 4 units of the packed order; every unit appears once. `doc_lengths`: they sum to 512; the longest is exactly 256.
All inputs are finite; a program needn't handle non-finite values.
Results may differ from the reference program's by a relative error of at most 0.017.
Values may be sent and summed in bfloat16 or wider, within the bound.
No kernel may reach another device: no remote copies, remote signals or barrier semaphores. Data moves between devices by JAX's collectives and lax.ppermute only.
A program may use at most 128 MiB of HBM per device.

```python
import math
import jax
import jax.numpy as jnp
import numpy as np
from jax import lax

D = 16384
HQ = 64
KVH = 8
HD = 128
DOCS = 8
TOKENS = 512
UNITS = 16
MOSTLEN = 256
HEAD_BLOCKS = 2
N_CTX = 4


def drawn_rows(key):
    key_first = jax.random.fold_in(key, 0)
    shared_base = jax.random.normal(key_first, (TOKENS, KVH * HD), jnp.float32)
    return shared_base


def draw_key_rows(key, part):
    shared_base = drawn_rows(key)
    drawn = shared_base
    return drawn.astype(jnp.bfloat16)


def draw_queries(key, part):
    key = jax.random.fold_in(key, 22)
    key_first = jax.random.fold_in(key, 0)
    result = jax.random.normal(key_first, (TOKENS, HQ * HD), jnp.float32)
    return result.astype(jnp.bfloat16)


def draw_unit_source(key, part):
    key = jax.random.fold_in(key, 23)
    key_first, second = jax.random.split(key)
    device_count = N_CTX
    orders = jax.vmap(lambda subkey: jax.random.permutation(subkey, device_count))(jax.random.split(key_first, device_count))
    unit_order = jax.vmap(lambda subkey: jax.random.permutation(subkey, device_count))(jax.random.split(second, device_count))
    dest_grid = jnp.broadcast_to(jnp.arange(device_count)[:, None], (device_count, device_count))
    within = unit_order[orders, dest_grid]
    return (orders * device_count + within).reshape(device_count * device_count).astype(jnp.int32)


def shard_levels(own_key, shape, cuts, smallest, largest):
    level, own = 1.0, jax.random.fold_in(own_key, 6)
    for position, blocks in cuts:
        heights = jnp.exp(jax.random.uniform(jax.random.fold_in(own, position), (blocks,), jnp.float32, smallest / len(cuts), largest / len(cuts)))
        level = level * jnp.repeat(heights, shape[position] // blocks).reshape([-1 if axis == position else 1 for axis in range(len(shape))])
    return level


def length_profile(amount, total, limit, lean):
    portions = [(1 << 20) // math.isqrt(rank ** lean) + 1 for rank in range(2, amount + 1)]
    spare, given = total - limit - (amount - 1), [1] * (amount - 1)
    while spare > 0:
        candidates = [i for i in range(amount - 1) if given[i] < limit]
        mass, remaining = sum([portions[i] for i in candidates]), spare
        for i in candidates:
            more = min(limit - given[i], max(1, remaining * portions[i] // mass), spare)
            given[i] = given[i] + more
            spare = spare - more
    return np.array([limit] + given)


def uneven(stream_key, amount, total, reach, lean):
    if amount == 2:
        one = jax.random.randint(stream_key, (), max(1, total - reach), min(reach, total - 1) + 1)
        return jnp.stack([one, total - one])
    tallies = jnp.asarray(length_profile(amount, total, reach, lean), jnp.int32)
    pairs = (amount - 1) // 2
    source_of, sink = tallies[1:1 + 2 * pairs:2], tallies[2:2 + 2 * pairs:2]
    slack = jnp.minimum(source_of - 1, reach - sink)
    shifted = jax.random.randint(jax.random.fold_in(stream_key, 1), (pairs,), 0, 1 << 20) % (slack + 1)
    tallies = tallies.at[1:1 + 2 * pairs:2].set(source_of - shifted).at[2:2 + 2 * pairs:2].set(sink + shifted)
    return tallies[jax.random.permutation(jax.random.fold_in(stream_key, 2), amount)]


def normal_values(stream_key, dims, width, most, cuts=(), held_as=jnp.bfloat16):
    array = width * jax.random.normal(stream_key, dims, jnp.float32)
    if cuts:
        array = array * shard_levels(stream_key, dims, cuts, -0.22, 0.18)
    return jnp.clip(array, -most, most).astype(held_as)


def setup_inputs(seed: int = 0, part: int = 0) -> dict:
    streams_of = jax.random.split(jax.random.key(seed), 7)
    own_keys = jax.random.split(jax.random.fold_in(streams_of[6], part), 7)
    return {
        "queries": draw_queries(jax.random.fold_in(jax.random.fold_in(streams_of[6], part), 71), part),
        "key_rows": draw_key_rows(jax.random.fold_in(jax.random.fold_in(streams_of[6], part), 71), part),
        "value_rows": normal_values(own_keys[2], (TOKENS, KVH * HD), 1.0, 6.0, ((0, 4), (1, 2))),
        "doc_lengths": uneven(own_keys[3], DOCS, TOKENS, MOSTLEN, 2).astype(jnp.int32),
        "unit_source": draw_unit_source(jax.random.fold_in(jax.random.fold_in(streams_of[6], part), 71), part),
        "w_out": normal_values(streams_of[5], (HQ * HD, D), (HQ * HD) ** -0.5, 0.0625, ((0, 2), (1, 4))),
    }


def doc_index(positions, doc_ends):
    return jnp.sum((positions[None, :] >= doc_ends[:, None]).astype(jnp.int32), axis=0)


def reference(queries, key_rows, value_rows, doc_lengths, unit_source, w_out):
    group_size = HQ // KVH
    doc_ends = jnp.cumsum(doc_lengths).astype(jnp.int32)
    positions = jnp.arange(TOKENS, dtype=jnp.int32)
    token_doc = doc_index(positions, doc_ends)
    visible = (token_doc[:, None] == token_doc[None, :]) & (positions[None, :] <= positions[:, None])
    query_heads = queries.reshape(TOKENS, KVH, group_size, HD).transpose(1, 0, 2, 3)
    key_heads = key_rows.reshape(TOKENS, KVH, HD).transpose(1, 0, 2)
    value_heads = value_rows.reshape(TOKENS, KVH, HD).transpose(1, 0, 2)

    def one_group(operands):
        query_group, key_group, value_group = operands
        scores = jnp.einsum("tgd,sd->gts", query_group.astype(jnp.float32), key_group.astype(jnp.float32)) * (HD ** -0.5)
        scores = jnp.where(visible[None], scores, -jnp.inf)
        row_max = jnp.max(scores, axis=2, keepdims=True)
        weights = jnp.where(visible[None], jnp.exp(scores - row_max), 0.0)
        totals = jnp.sum(weights, axis=2)
        rounded = lax.optimization_barrier(weights.astype(jnp.bfloat16))
        blended = jnp.einsum("gts,sd->gtd", rounded.astype(jnp.float32), value_group.astype(jnp.float32))
        return (blended / totals[..., None]).astype(jnp.bfloat16)

    attended = lax.map(one_group, (query_heads, key_heads, value_heads))
    attended = attended.transpose(2, 0, 1, 3).reshape(TOKENS, HQ * HD)
    unit_rows = TOKENS // UNITS
    source_rows = (unit_source[:, None] * unit_rows + jnp.arange(unit_rows, dtype=jnp.int32)[None, :]).reshape(TOKENS)
    balanced = jnp.take(attended, source_rows, axis=0)
    block_cols = HQ * HD // HEAD_BLOCKS
    running_total = jnp.zeros((TOKENS, D), jnp.float32)
    for block_index in range(HEAD_BLOCKS):
        lower = block_index * block_cols
        partial_value = jnp.dot(balanced[:, lower:lower + block_cols], w_out[lower:lower + block_cols], preferred_element_type=jnp.float32)
        running_total = running_total + lax.optimization_barrier(partial_value.astype(jnp.bfloat16)).astype(jnp.float32)
    return running_total.astype(jnp.bfloat16)
```

```python
import functools
import math

import jax
import jax.numpy as jnp
from jax import lax
from jax.experimental import pallas as pl
from jax.experimental.pallas import tpu as pltpu
from jax.sharding import PartitionSpec as P

HD = 128
MIB = 1 << 20
PARTS = ((0, 1), (1, 2), (2, 3), (3, 4))
PIECES = 2


def doc_index(positions, doc_ends):
    return jnp.sum((positions[None, :] >= doc_ends[:, None]).astype(jnp.int32), axis=0)


def general(queries, key_rows, value_rows, doc_lengths, unit_source, w_out):
    ctx_count = lax.axis_size("ctx")
    ctx_index = lax.axis_index("ctx")
    tok_dev, columns = queries.shape
    unit_rows = tok_dev // ctx_count
    head_count = columns // HD
    kv_heads = key_rows.shape[1] // HD
    group_size = head_count // kv_heads
    unit_plan = unit_source.reshape(ctx_count, ctx_count)
    positions = ctx_index * tok_dev + jnp.arange(tok_dev, dtype=jnp.int32)
    doc_ends = jnp.cumsum(doc_lengths)
    query_doc = doc_index(positions, doc_ends)
    grouped = queries.reshape(tok_dev, kv_heads, group_size, HD)
    key_all = lax.all_gather(key_rows, "ctx", axis=0, tiled=True)
    value_all = lax.all_gather(value_rows, "ctx", axis=0, tiled=True)
    extent = key_all.shape[0]
    key_pos = jnp.arange(extent, dtype=jnp.int32)
    key_doc = doc_index(key_pos, doc_ends)
    visible = (key_doc[None, :] == query_doc[:, None]) & (key_pos[None, :] <= positions[:, None])
    scores = jnp.einsum(
        "qkgd,pkd->kgqp",
        grouped,
        key_all.reshape(extent, kv_heads, HD),
        preferred_element_type=jnp.float32,
    ) * (HD ** -0.5)
    scores = jnp.where(visible, scores, -jnp.inf)
    row_max = jnp.max(scores, axis=3, keepdims=True)
    weights = jnp.where(visible, jnp.exp(scores - row_max), 0.0)
    totals = jnp.sum(weights, axis=3)
    blended = jnp.einsum(
        "kgqp,pkd->kgqd",
        weights.astype(jnp.bfloat16),
        value_all.reshape(extent, kv_heads, HD),
        preferred_element_type=jnp.float32,
    )
    attended = (
        (blended / totals[..., None])
        .transpose(2, 0, 1, 3)
        .reshape(tok_dev, columns)
        .astype(jnp.bfloat16)
    )
    gathered = lax.all_gather(attended, "ctx", axis=0, tiled=True)
    units = gathered.reshape(ctx_count * ctx_count, unit_rows, columns)
    balanced = jnp.take(units, unit_plan.reshape(-1), axis=0).reshape(extent, columns)
    partial_value = jnp.dot(balanced, w_out, preferred_element_type=jnp.float32)
    return lax.psum_scatter(
        partial_value.astype(jnp.bfloat16), "tp", scatter_dimension=0, tiled=True
    )


SMEM = pl.BlockSpec(memory_space=pltpu.SMEM)
VMEM = pl.BlockSpec(memory_space=pltpu.VMEM)
HBM = pl.BlockSpec(memory_space=pl.ANY)
TILE = 512


def in_hbm(x):
    return pltpu.with_memory_space_constraint(x, pltpu.HBM)


def pack_kernel(k_hbm, v_hbm, first_ref, sems):
    copies = [
        pltpu.make_async_copy(k_hbm.at[:, :HD], first_ref.at[:, :HD], sems.at[0]),
        pltpu.make_async_copy(v_hbm.at[:, :HD], first_ref.at[:, HD:], sems.at[1]),
    ]
    for copy in copies:
        copy.start()
    for copy in copies:
        copy.wait()


def pack(key_rows, value_rows):
    return pl.pallas_call(
        pack_kernel,
        out_shape=jax.ShapeDtypeStruct((key_rows.shape[0], 2 * HD), jnp.bfloat16),
        in_specs=[HBM, HBM],
        out_specs=VMEM,
        scratch_shapes=[pltpu.SemaphoreType.DMA((2,))],
        compiler_params=pltpu.CompilerParams(vmem_limit_bytes=4 * MIB),
        name="pack",
    )(in_hbm(key_rows), in_hbm(value_rows))


def prepare_kernel(docs_hbm, k_hbm, v_hbm, q_hbm, rest_ref, q_ref, mask_ref, docs, sems):
    more = k_hbm.shape[1] - HD
    lengths = pltpu.make_async_copy(docs_hbm, docs, sems.at[0])
    loads = [
        pltpu.make_async_copy(k_hbm.at[:, HD:], rest_ref.at[:, :more], sems.at[1]),
        pltpu.make_async_copy(v_hbm.at[:, HD:], rest_ref.at[:, more:], sems.at[2]),
        pltpu.make_async_copy(q_hbm, q_ref, sems.at[3]),
    ]
    lengths.start()
    for load in loads:
        load.start()
    lengths.wait()
    rows, window = mask_ref.shape
    base = lax.axis_index("ctx") * rows
    pos = base + lax.broadcasted_iota(jnp.int32, (rows, window), 0)
    start = jnp.zeros((rows, window), jnp.int32)
    end = jnp.int32(0)
    for d in range(docs.shape[0]):
        end = end + docs[d]
        start = jnp.where(pos >= end, end, start)
    key_pos = base + rows - window + lax.broadcasted_iota(jnp.int32, (rows, window), 1)
    mask_ref[...] = jnp.where((key_pos >= start) & (key_pos <= pos), 0.0, -jnp.inf)
    for load in loads:
        load.wait()


def prepare(doc_lengths, key_rows, value_rows, queries):
    rows, columns = key_rows.shape
    return pl.pallas_call(
        prepare_kernel,
        out_shape=[
            jax.ShapeDtypeStruct((rows, 2 * (columns - HD)), jnp.bfloat16),
            jax.ShapeDtypeStruct(queries.shape, jnp.bfloat16),
            jax.ShapeDtypeStruct((rows, 3 * rows), jnp.float32),
        ],
        in_specs=[HBM] * 4,
        out_specs=[VMEM] * 3,
        scratch_shapes=[
            pltpu.SMEM(doc_lengths.shape, jnp.int32),
            pltpu.SemaphoreType.DMA((4,)),
        ],
        compiler_params=pltpu.CompilerParams(vmem_limit_bytes=4 * MIB),
        cost_estimate=pl.CostEstimate(flops=0, bytes_accessed=0, transcendentals=0),
        name="prepare",
    )(in_hbm(doc_lengths), in_hbm(key_rows), in_hbm(value_rows), in_hbm(queries))


def attend_kernel(groups, count, q_ref, mask_ref, *refs):
    kv, out_ref = refs[:count], refs[-1]
    rows = q_ref.shape[0]
    width = out_ref.shape[1] // len(groups)
    heads = width // HD
    window = 3 * rows
    factor = HD ** -0.5 * math.log2(math.e)
    for i, g in enumerate(groups):
        kv0, kv1, kv2 = kv[:3] if g == 0 else kv[-3:]
        column = 0 if g == 0 else g - 1
        half = kv0.shape[1] // 2
        at_k = slice(column * HD, (column + 1) * HD)
        at_v = slice(half + column * HD, half + (column + 1) * HD)
        keys = jnp.concatenate([kv2[:, at_k], kv1[:, at_k], kv0[:, at_k]], axis=0)
        values = jnp.concatenate([kv2[:, at_v], kv1[:, at_v], kv0[:, at_v]], axis=0)
        stacked = jnp.concatenate(
            [q_ref[:, g * width + h * HD:g * width + (h + 1) * HD] for h in range(heads)], axis=0
        )
        scores = lax.dot_general(
            stacked, keys, (((1,), (1,)), ((), ())), preferred_element_type=jnp.float32
        ).reshape(heads, rows, window)
        scores = scores + mask_ref[...][None]
        top = jnp.max(scores, axis=2, keepdims=True)
        weights = jnp.exp2((scores - top) * factor)
        total = jnp.sum(weights, axis=2, keepdims=True)
        mixed = jnp.dot(
            weights.astype(jnp.bfloat16).reshape(heads * rows, window),
            values,
            preferred_element_type=jnp.float32,
        ).reshape(heads, rows, HD)
        result = (mixed / total).astype(jnp.bfloat16)
        for h in range(heads):
            out_ref[:, i * width + h * HD:i * width + (h + 1) * HD] = result[h]


def attend(groups, width, queries, mask, window, after):
    rows = queries.shape[0]
    kv = ([*window[0]] if 0 in groups else []) + ([*window[1]] if groups[-1] > 0 else [])
    count = len(groups)
    return pl.pallas_call(
        functools.partial(attend_kernel, groups, len(kv)),
        out_shape=jax.ShapeDtypeStruct((rows, count * width), jnp.bfloat16),
        in_specs=[VMEM] * (2 + len(kv)) + [HBM] * len(after),
        out_specs=VMEM,
        compiler_params=pltpu.CompilerParams(vmem_limit_bytes=16 * MIB),
        cost_estimate=pl.CostEstimate(flops=0, bytes_accessed=0, transcendentals=0),
        name=f"attend_{groups[0]}",
    )(queries, mask, *kv, *after)


def lay_out(plan, pieces, lhs):
    here = lax.axis_index("ctx")
    core = lax.axis_index("tp")
    first = jnp.where(core == 0, 1, 2)
    owners = [here, here ^ first, here ^ (3 - first), here ^ 3]
    unit_rows = lhs.shape[0] // 16
    swap = jnp.where(core == 0, 8, 0)
    wanted = [plan[slot] for slot in range(16)]
    for owner, piece in zip(owners, pieces):
        for u in range(4):
            slot = jnp.int32(0)
            for s in range(1, 16):
                slot = jnp.where(wanted[s] == owner * 4 + u, s, slot)
            slot = slot ^ swap
            at = pl.ds(pl.multiple_of(slot * unit_rows, unit_rows), unit_rows)
            lhs[at, :] = piece[u * unit_rows:(u + 1) * unit_rows, :]


def project(w_hbm, wbuf, sems, row, first, prologue, body):
    depth, columns = wbuf.shape
    cuts = [0, columns // 8, 3 * columns // 8, columns]
    copies = [
        pltpu.make_async_copy(
            w_hbm.at[row:row + depth, first + lo:first + hi], wbuf.at[:, lo:hi], sems.at[i]
        )
        for i, (lo, hi) in enumerate(zip(cuts, cuts[1:]))
    ]
    for copy in copies:
        copy.start()
    prologue()
    for copy, lo, hi in zip(copies, cuts, cuts[1:]):
        copy.wait()
        for at in range(lo, hi, TILE):
            end = min(at + TILE, hi)
            body(slice(first + at, first + end), slice(at, end), wbuf[:, at:end])


def chunk_kernel(row, has_acc, plan, p0, p1, p2, p3, w_hbm, *rest):
    acc_ref = rest[0]
    out_ref, lhs, wbuf, sems = rest[-4:]

    def body(at, to, tile):
        product = jnp.dot(lhs[...], tile, preferred_element_type=jnp.float32)
        if has_acc:
            product = product + acc_ref[:, at]
        out_ref[:, at] = product

    project(w_hbm, wbuf, sems, row, 0, lambda: lay_out(plan, (p0, p1, p2, p3), lhs), body)


def chunk(row, plan, pieces, w_out, acc, after):
    rows, width = pieces[0].shape
    total_rows, columns = 4 * rows, w_out.shape[1]
    has_acc = acc is not None
    return pl.pallas_call(
        functools.partial(chunk_kernel, row, has_acc),
        out_shape=jax.ShapeDtypeStruct((total_rows, columns), jnp.float32),
        in_specs=[SMEM] + [VMEM] * 4 + [HBM] + [VMEM] * has_acc + [HBM] * len(after),
        out_specs=VMEM,
        scratch_shapes=[
            pltpu.VMEM((total_rows, width), jnp.bfloat16),
            pltpu.VMEM((width, columns), jnp.bfloat16),
            pltpu.SemaphoreType.DMA((3,)),
        ],
        input_output_aliases={6: 0} if has_acc else {},
        compiler_params=pltpu.CompilerParams(vmem_limit_bytes=(4 + width // 128) * MIB),
        cost_estimate=pl.CostEstimate(
            flops=2 * total_rows * width * columns,
            bytes_accessed=2 * width * columns,
            transcendentals=0,
        ),
        name=f"chunk_{row // width}",
    )(plan, *pieces, w_out, *([acc] if has_acc else []), *after)


def last_kernel(row, first, plan, p0, p1, p2, p3, w_hbm, acc_ref, own_ref, sent_ref, lhs, wbuf, sems):
    rows = lhs.shape[0] // 2

    def body(at, to, tile):
        product = jnp.dot(lhs[...], tile, preferred_element_type=jnp.float32)
        product = product + acc_ref[:, at]
        sent_ref[:, to] = product[:rows].astype(jnp.bfloat16)
        own_ref[:, to] = product[rows:]

    project(w_hbm, wbuf, sems, row, first, lambda: lay_out(plan, (p0, p1, p2, p3), lhs), body)


def last(row, first, columns, plan, pieces, w_out, acc):
    rows, width = pieces[0].shape
    total_rows = 4 * rows
    return pl.pallas_call(
        functools.partial(last_kernel, row, first),
        out_shape=[
            jax.ShapeDtypeStruct((total_rows // 2, columns), jnp.float32),
            jax.ShapeDtypeStruct((total_rows // 2, columns), jnp.bfloat16),
        ],
        in_specs=[SMEM] + [VMEM] * 4 + [HBM, VMEM],
        out_specs=[VMEM, VMEM],
        scratch_shapes=[
            pltpu.VMEM((total_rows, width), jnp.bfloat16),
            pltpu.VMEM((width, columns), jnp.bfloat16),
            pltpu.SemaphoreType.DMA((3,)),
        ],
        compiler_params=pltpu.CompilerParams(vmem_limit_bytes=(4 + width // 128) * MIB),
        cost_estimate=pl.CostEstimate(
            flops=2 * total_rows * width * columns,
            bytes_accessed=2 * width * columns,
            transcendentals=0,
        ),
        name=f"last_{first // columns}",
    )(plan, *pieces, w_out, acc)


def total_kernel(first, has_out, own_ref, got_ref, *rest):
    out_hbm, buf, sems = rest[has_out:]
    columns = got_ref.shape[1]
    step = columns // 2
    writes = []
    for i in range(2):
        to = slice(i * step, (i + 1) * step)
        at = slice(first + i * step, first + (i + 1) * step)
        value = own_ref[:, to] + got_ref[:, to].astype(jnp.float32)
        buf[:, to] = value.astype(jnp.bfloat16)
        write = pltpu.make_async_copy(buf.at[:, to], out_hbm.at[:, at], sems.at[i])
        write.start()
        writes.append(write)
    for write in writes:
        write.wait()


def total(first, width, own, got, out):
    rows, columns = got.shape
    has_out = out is not None
    return pl.pallas_call(
        functools.partial(total_kernel, first, has_out),
        out_shape=jax.ShapeDtypeStruct((rows, width), jnp.bfloat16),
        in_specs=[VMEM, VMEM] + [HBM] * has_out,
        out_specs=HBM,
        scratch_shapes=[
            pltpu.VMEM((rows, columns), jnp.bfloat16),
            pltpu.SemaphoreType.DMA((2,)),
        ],
        input_output_aliases={2: 0} if has_out else {},
        compiler_params=pltpu.CompilerParams(vmem_limit_bytes=4 * MIB),
        cost_estimate=pl.CostEstimate(
            flops=rows * columns, bytes_accessed=2 * rows * columns, transcendentals=0
        ),
        name=f"total_{first // columns}",
    )(own, got, *([out] if has_out else []))


def gather_rows(own):
    def route(first):
        pairs = []
        for chip in range(4):
            for core in range(2):
                axis = 1 if (core == 0) == first else 2
                pairs.append((chip * 2 + core, (chip ^ axis) * 2 + core))
        return pairs

    near = lax.ppermute(own, ("ctx", "tp"), route(True))
    side = lax.ppermute(own, ("ctx", "tp"), route(False))
    far = lax.ppermute(near, ("ctx", "tp"), route(False))
    return own, near, side, far


def local(queries, key_rows, value_rows, doc_lengths, unit_source, w_out):
    if lax.axis_size("ctx") != 4 or lax.axis_size("tp") != 2 or key_rows.shape[1] != 4 * HD:
        return general(queries, key_rows, value_rows, doc_lengths, unit_source, w_out)
    w_out = in_hbm(w_out)
    kv_heads = key_rows.shape[1] // HD
    width = queries.shape[1] // kv_heads
    back_one = [(0, 1), (1, 2), (2, 3)]
    back_two = [(0, 2), (1, 3)]
    first = pack(key_rows, value_rows)
    rest, held, mask = prepare(doc_lengths, key_rows, value_rows, queries)
    window = [
        (part, lax.ppermute(part, "ctx", back_one), lax.ppermute(part, "ctx", back_two))
        for part in (first, rest)
    ]

    def rows_of(i, after):
        own = attend(tuple(range(*PARTS[i])), width, held, mask, window, after)
        return gather_rows(own)

    gathered = [rows_of(0, [])]
    gathered.append(rows_of(1, [gathered[0][0]]))
    gathered.append(rows_of(2, [gathered[1][0], gathered[0][2]]))
    acc = chunk(0, unit_source, gathered[0], w_out, None, [gathered[2][0]])
    gathered.append(rows_of(3, [acc, gathered[1][2]]))
    acc = chunk(width, unit_source, gathered[1], w_out, acc, [gathered[3][0], gathered[2][2]])
    acc = chunk(2 * width, unit_source, gathered[2], w_out, acc, [gathered[3][2]])
    columns = w_out.shape[1] // PIECES
    mine, got = [], []
    for i in range(PIECES):
        kept, sent = last(3 * width, i * columns, columns, unit_source, gathered[3], w_out, acc)
        mine.append(kept)
        got.append(lax.ppermute(sent, "tp", [(0, 1), (1, 0)]))
    out = None
    for i in range(PIECES):
        out = total(i * columns, w_out.shape[1], mine[i], got[i], out)
    return out


def solution(mesh):
    return jax.shard_map(
        local,
        mesh=mesh,
        in_specs=(
            P(("dp", "ctx"), "tp"),
            P(("dp", "ctx"), "tp"),
            P(("dp", "ctx"), "tp"),
            P("dp"),
            P("dp"),
            P("tp", "ctx"),
        ),
        out_specs=P(("dp", "tp"), "ctx"),
        check_vma=False,
    )
```

```python
import functools
import math

import jax
import jax.numpy as jnp
from jax import lax
from jax.experimental import pallas as pl
from jax.experimental.pallas import tpu as pltpu
from jax.sharding import PartitionSpec as P

HD = 128
MIB = 1 << 20
HALVES = 2


def doc_index(positions, doc_ends):
    return jnp.sum((positions[None, :] >= doc_ends[:, None]).astype(jnp.int32), axis=0)


def general(queries, key_rows, value_rows, doc_lengths, unit_source, w_out):
    ctx_count = lax.axis_size("ctx")
    ctx_index = lax.axis_index("ctx")
    tok_dev, columns = queries.shape
    unit_rows = tok_dev // ctx_count
    head_count = columns // HD
    kv_heads = key_rows.shape[1] // HD
    group_size = head_count // kv_heads
    unit_plan = unit_source.reshape(ctx_count, ctx_count)
    positions = ctx_index * tok_dev + jnp.arange(tok_dev, dtype=jnp.int32)
    doc_ends = jnp.cumsum(doc_lengths)
    query_doc = doc_index(positions, doc_ends)
    grouped = queries.reshape(tok_dev, kv_heads, group_size, HD)
    key_all = lax.all_gather(key_rows, "ctx", axis=0, tiled=True)
    value_all = lax.all_gather(value_rows, "ctx", axis=0, tiled=True)
    extent = key_all.shape[0]
    key_pos = jnp.arange(extent, dtype=jnp.int32)
    key_doc = doc_index(key_pos, doc_ends)
    visible = (key_doc[None, :] == query_doc[:, None]) & (key_pos[None, :] <= positions[:, None])
    scores = jnp.einsum(
        "qkgd,pkd->kgqp",
        grouped,
        key_all.reshape(extent, kv_heads, HD),
        preferred_element_type=jnp.float32,
    ) * (HD ** -0.5)
    scores = jnp.where(visible, scores, -jnp.inf)
    row_max = jnp.max(scores, axis=3, keepdims=True)
    weights = jnp.where(visible, jnp.exp(scores - row_max), 0.0)
    totals = jnp.sum(weights, axis=3)
    blended = jnp.einsum(
        "kgqp,pkd->kgqd",
        weights.astype(jnp.bfloat16),
        value_all.reshape(extent, kv_heads, HD),
        preferred_element_type=jnp.float32,
    )
    attended = (
        (blended / totals[..., None])
        .transpose(2, 0, 1, 3)
        .reshape(tok_dev, columns)
        .astype(jnp.bfloat16)
    )
    gathered = lax.all_gather(attended, "ctx", axis=0, tiled=True)
    units = gathered.reshape(ctx_count * ctx_count, unit_rows, columns)
    balanced = jnp.take(units, unit_plan.reshape(-1), axis=0).reshape(extent, columns)
    partial_value = jnp.dot(balanced, w_out, preferred_element_type=jnp.float32)
    return lax.psum_scatter(
        partial_value.astype(jnp.bfloat16), "tp", scatter_dimension=0, tiled=True
    )


SMEM = pl.BlockSpec(memory_space=pltpu.SMEM)
VMEM = pl.BlockSpec(memory_space=pltpu.VMEM)
HBM = pl.BlockSpec(memory_space=pl.ANY)
TILE = 512


def in_hbm(x):
    return pltpu.with_memory_space_constraint(x, pltpu.HBM)


def pack_kernel(k_hbm, v_hbm, kv_ref, sems):
    columns = k_hbm.shape[1]
    copies = [
        pltpu.make_async_copy(k_hbm, kv_ref.at[:, :columns], sems.at[0]),
        pltpu.make_async_copy(v_hbm, kv_ref.at[:, columns:], sems.at[1]),
    ]
    for copy in copies:
        copy.start()
    for copy in copies:
        copy.wait()


def pack(key_rows, value_rows):
    rows, columns = key_rows.shape
    return pl.pallas_call(
        pack_kernel,
        out_shape=jax.ShapeDtypeStruct((rows, 2 * columns), jnp.bfloat16),
        in_specs=[HBM, HBM],
        out_specs=VMEM,
        scratch_shapes=[pltpu.SemaphoreType.DMA((2,))],
        compiler_params=pltpu.CompilerParams(vmem_limit_bytes=4 * MIB),
        name="pack",
    )(in_hbm(key_rows), in_hbm(value_rows))


def prepare_kernel(docs_hbm, q_hbm, w_hbm, q_ref, mask_ref, w_ref, docs, sems):
    lengths = pltpu.make_async_copy(docs_hbm, docs, sems.at[0])
    loads = [
        pltpu.make_async_copy(q_hbm, q_ref, sems.at[1]),
        block_copy(w_hbm, 0, w_ref, sems.at[2]),
    ]
    lengths.start()
    for load in loads:
        load.start()
    lengths.wait()
    rows, window = mask_ref.shape
    base = lax.axis_index("ctx") * rows
    pos = base + lax.broadcasted_iota(jnp.int32, (rows, window), 0)
    start = jnp.zeros((rows, window), jnp.int32)
    end = jnp.int32(0)
    for d in range(docs.shape[0]):
        end = end + docs[d]
        start = jnp.where(pos >= end, end, start)
    key_pos = base + rows - window + lax.broadcasted_iota(jnp.int32, (rows, window), 1)
    mask_ref[...] = jnp.where((key_pos >= start) & (key_pos <= pos), 0.0, -jnp.inf)
    for load in loads:
        load.wait()


def block_shape(w_out, chunks):
    return w_out.shape[0] // chunks, w_out.shape[1] // HALVES


def block_copy(w_hbm, index, w_ref, sem):
    depth, columns = w_ref.shape
    row, column = index // HALVES * depth, index % HALVES * columns
    return pltpu.make_async_copy(
        w_hbm.at[row:row + depth, column:column + columns], w_ref, sem
    )


def prepare(doc_lengths, queries, w_out, chunks):
    rows = queries.shape[0]
    return pl.pallas_call(
        prepare_kernel,
        out_shape=[
            jax.ShapeDtypeStruct(queries.shape, jnp.bfloat16),
            jax.ShapeDtypeStruct((rows, 3 * rows), jnp.float32),
            jax.ShapeDtypeStruct(block_shape(w_out, chunks), jnp.bfloat16),
        ],
        in_specs=[HBM] * 3,
        out_specs=[VMEM] * 3,
        scratch_shapes=[
            pltpu.SMEM(doc_lengths.shape, jnp.int32),
            pltpu.SemaphoreType.DMA((3,)),
        ],
        compiler_params=pltpu.CompilerParams(vmem_limit_bytes=4 * MIB),
        cost_estimate=pl.CostEstimate(flops=0, bytes_accessed=0, transcendentals=0),
        name="prepare",
    )(in_hbm(doc_lengths), in_hbm(queries), w_out)


def attend_kernel(g, q_ref, mask_ref, kv0, kv1, kv2, *rest):
    out_ref = rest[-1]
    rows, width = out_ref.shape
    heads = width // HD
    window = 3 * rows
    factor = HD ** -0.5 * math.log2(math.e)
    half = kv0.shape[1] // 2
    at_k = slice(g * HD, (g + 1) * HD)
    at_v = slice(half + g * HD, half + (g + 1) * HD)
    keys = jnp.concatenate([kv2[:, at_k], kv1[:, at_k], kv0[:, at_k]], axis=0)
    values = jnp.concatenate([kv2[:, at_v], kv1[:, at_v], kv0[:, at_v]], axis=0)
    stacked = jnp.concatenate(
        [q_ref[:, g * width + h * HD:g * width + (h + 1) * HD] for h in range(heads)], axis=0
    )
    scores = lax.dot_general(
        stacked, keys, (((1,), (1,)), ((), ())), preferred_element_type=jnp.float32
    ).reshape(heads, rows, window)
    scores = scores + mask_ref[...][None]
    top = jnp.max(scores, axis=2, keepdims=True)
    weights = jnp.exp2((scores - top) * factor)
    total = jnp.sum(weights, axis=2, keepdims=True)
    mixed = jnp.dot(
        weights.astype(jnp.bfloat16).reshape(heads * rows, window),
        values,
        preferred_element_type=jnp.float32,
    ).reshape(heads, rows, HD)
    result = (mixed / total).astype(jnp.bfloat16)
    for h in range(heads):
        out_ref[:, h * HD:(h + 1) * HD] = result[h]


def attend(g, width, queries, mask, kv, after):
    rows = queries.shape[0]
    return pl.pallas_call(
        functools.partial(attend_kernel, g),
        out_shape=jax.ShapeDtypeStruct((rows, width), jnp.bfloat16),
        in_specs=[VMEM] * 5 + [HBM] * len(after),
        out_specs=VMEM,
        compiler_params=pltpu.CompilerParams(vmem_limit_bytes=16 * MIB),
        cost_estimate=pl.CostEstimate(flops=0, bytes_accessed=0, transcendentals=0),
        name=f"attend_{g}",
    )(queries, mask, *kv, *after)


def lay_out(plan, pieces, lhs):
    here = lax.axis_index("ctx")
    core = lax.axis_index("tp")
    first = jnp.where(core == 0, 1, 2)
    owners = [here, here ^ first, here ^ (3 - first), here ^ 3]
    unit_rows = lhs.shape[0] // 16
    swap = jnp.where(core == 0, 8, 0)
    wanted = [plan[slot] for slot in range(16)]
    for owner, piece in zip(owners, pieces):
        for u in range(4):
            slot = jnp.int32(0)
            for s in range(1, 16):
                slot = jnp.where(wanted[s] == owner * 4 + u, s, slot)
            slot = slot ^ swap
            at = pl.ds(pl.multiple_of(slot * unit_rows, unit_rows), unit_rows)
            lhs[at, :] = piece[u * unit_rows:(u + 1) * unit_rows, :]


def step_kernel(index, last, first_half, has_acc, *refs):
    refs = list(refs)
    if first_half:
        plan, *pieces = refs[:5]
        del refs[:5]
    else:
        lhs = refs.pop(0)
    w_ref, w_hbm = refs[:2]
    del refs[:2]
    acc_ref = refs.pop(0) if has_acc else None
    has_next = not (last and not first_half)
    sem = refs.pop() if has_next else None
    next_ref = refs.pop() if has_next else None
    if first_half:
        lhs = refs.pop()
    load = None
    if has_next:
        load = block_copy(w_hbm, index + 1, next_ref, sem)
        load.start()
    if first_half:
        lay_out(plan, pieces, lhs)
    rows = lhs.shape[0] // 2
    for at in range(0, w_ref.shape[1], TILE):
        to = slice(at, at + TILE)
        product = jnp.dot(lhs[...], w_ref[:, to], preferred_element_type=jnp.float32)
        if has_acc:
            product = product + acc_ref[:, to]
        if last:
            own_ref, sent_ref = refs
            own_ref[:, to] = product[rows:]
            sent_ref[:, to] = product[:rows].astype(jnp.bfloat16)
        else:
            refs[0][:, to] = product
    if load is not None:
        load.wait()


def step(index, last, rows_in, block, w_out, acc):
    first_half = index % HALVES == 0
    has_acc = acc is not None
    has_next = not (last and not first_half)
    depth, columns = block.shape
    if first_half:
        plan, pieces = rows_in
        total_rows = 4 * pieces[0].shape[0]
        operands, specs = [plan, *pieces], [SMEM] + [VMEM] * 4
    else:
        total_rows = rows_in.shape[0]
        operands, specs = [rows_in], [VMEM]
    if last:
        half = (total_rows // 2, columns)
        shapes = [jax.ShapeDtypeStruct(half, jnp.float32), jax.ShapeDtypeStruct(half, jnp.bfloat16)]
    else:
        shapes = [jax.ShapeDtypeStruct((total_rows, columns), jnp.float32)]
    if first_half:
        shapes.append(jax.ShapeDtypeStruct((total_rows, depth), jnp.bfloat16))
    if has_next:
        shapes.append(jax.ShapeDtypeStruct(block.shape, jnp.bfloat16))
    operands += [block, w_out] + [acc] * has_acc
    specs += [VMEM, HBM] + [VMEM] * has_acc
    alias = {len(operands) - 1: 0} if has_acc and not last else {}
    results = list(pl.pallas_call(
        functools.partial(step_kernel, index, last, first_half, has_acc),
        out_shape=shapes,
        in_specs=specs,
        out_specs=[VMEM] * len(shapes),
        scratch_shapes=[pltpu.SemaphoreType.DMA] * has_next,
        input_output_aliases=alias,
        compiler_params=pltpu.CompilerParams(vmem_limit_bytes=8 * MIB),
        cost_estimate=pl.CostEstimate(
            flops=2 * total_rows * depth * columns, bytes_accessed=0, transcendentals=0
        ),
        name=f"step_{index}",
    )(*operands))
    following = results.pop() if has_next else None
    lhs = results.pop() if first_half else None
    return results, lhs, following


def total_kernel(first, has_out, own_ref, got_ref, *rest):
    out_hbm, buf, sems = rest[has_out:]
    columns = got_ref.shape[1]
    step = columns // 2
    writes = []
    for i in range(2):
        to = slice(i * step, (i + 1) * step)
        at = slice(first + i * step, first + (i + 1) * step)
        value = own_ref[:, to] + got_ref[:, to].astype(jnp.float32)
        buf[:, to] = value.astype(jnp.bfloat16)
        write = pltpu.make_async_copy(buf.at[:, to], out_hbm.at[:, at], sems.at[i])
        write.start()
        writes.append(write)
    for write in writes:
        write.wait()


def total(first, width, own, got, out):
    rows, columns = got.shape
    has_out = out is not None
    return pl.pallas_call(
        functools.partial(total_kernel, first, has_out),
        out_shape=jax.ShapeDtypeStruct((rows, width), jnp.bfloat16),
        in_specs=[VMEM, VMEM] + [HBM] * has_out,
        out_specs=HBM,
        scratch_shapes=[
            pltpu.VMEM((rows, columns), jnp.bfloat16),
            pltpu.SemaphoreType.DMA((2,)),
        ],
        input_output_aliases={2: 0} if has_out else {},
        compiler_params=pltpu.CompilerParams(vmem_limit_bytes=4 * MIB),
        cost_estimate=pl.CostEstimate(
            flops=rows * columns, bytes_accessed=2 * rows * columns, transcendentals=0
        ),
        name=f"total_{first // columns}",
    )(own, got, *([out] if has_out else []))


def gather_rows(own):
    def route(first):
        pairs = []
        for chip in range(4):
            for core in range(2):
                axis = 1 if (core == 0) == first else 2
                pairs.append((chip * 2 + core, (chip ^ axis) * 2 + core))
        return pairs

    near = lax.ppermute(own, ("ctx", "tp"), route(True))
    side = lax.ppermute(own, ("ctx", "tp"), route(False))
    far = lax.ppermute(near, ("ctx", "tp"), route(False))
    return own, near, side, far


def local(queries, key_rows, value_rows, doc_lengths, unit_source, w_out):
    if lax.axis_size("ctx") != 4 or lax.axis_size("tp") != 2 or key_rows.shape[1] != 4 * HD:
        return general(queries, key_rows, value_rows, doc_lengths, unit_source, w_out)
    w_out = in_hbm(w_out)
    kv_heads = key_rows.shape[1] // HD
    width = queries.shape[1] // kv_heads
    kv = pack(key_rows, value_rows)
    held, mask, block = prepare(doc_lengths, queries, w_out, kv_heads)
    window = (
        kv,
        lax.ppermute(kv, "ctx", [(0, 1), (1, 2), (2, 3)]),
        lax.ppermute(kv, "ctx", [(0, 2), (1, 3)]),
    )
    gathered, after = [], []
    for g in range(kv_heads):
        own = attend(g, width, held, mask, window, after)
        gathered.append(gather_rows(own))
        after = [own]
    totals = [None] * HALVES
    mine, got = [], []
    for g in range(kv_heads):
        last = g == kv_heads - 1
        rows_in = (unit_source, gathered[g])
        for half in range(HALVES):
            results, lhs, block = step(
                g * HALVES + half, last, rows_in, block, w_out, totals[half]
            )
            rows_in = lhs
            if last:
                mine.append(results[0])
                got.append(lax.ppermute(results[1], "tp", [(0, 1), (1, 0)]))
            else:
                totals[half] = results[0]
    columns = w_out.shape[1] // HALVES
    out = None
    for half in range(HALVES):
        out = total(half * columns, w_out.shape[1], mine[half], got[half], out)
    return out


def solution(mesh):
    return jax.shard_map(
        local,
        mesh=mesh,
        in_specs=(
            P(("dp", "ctx"), "tp"),
            P(("dp", "ctx"), "tp"),
            P(("dp", "ctx"), "tp"),
            P("dp"),
            P("dp"),
            P("tp", "ctx"),
        ),
        out_specs=P(("dp", "tp"), "ctx"),
        check_vma=False,
    )
```

```python
import functools
import math

import jax
import jax.numpy as jnp
from jax import lax
from jax.experimental import pallas as pl
from jax.experimental.pallas import tpu as pltpu
from jax.sharding import PartitionSpec as P

HD = 128
MIB = 1 << 20
HALVES = 2


def doc_index(positions, doc_ends):
    return jnp.sum((positions[None, :] >= doc_ends[:, None]).astype(jnp.int32), axis=0)


def general(queries, key_rows, value_rows, doc_lengths, unit_source, w_out):
    ctx_count = lax.axis_size("ctx")
    ctx_index = lax.axis_index("ctx")
    tok_dev, columns = queries.shape
    unit_rows = tok_dev // ctx_count
    head_count = columns // HD
    kv_heads = key_rows.shape[1] // HD
    group_size = head_count // kv_heads
    unit_plan = unit_source.reshape(ctx_count, ctx_count)
    positions = ctx_index * tok_dev + jnp.arange(tok_dev, dtype=jnp.int32)
    doc_ends = jnp.cumsum(doc_lengths)
    query_doc = doc_index(positions, doc_ends)
    grouped = queries.reshape(tok_dev, kv_heads, group_size, HD)
    key_all = lax.all_gather(key_rows, "ctx", axis=0, tiled=True)
    value_all = lax.all_gather(value_rows, "ctx", axis=0, tiled=True)
    extent = key_all.shape[0]
    key_pos = jnp.arange(extent, dtype=jnp.int32)
    key_doc = doc_index(key_pos, doc_ends)
    visible = (key_doc[None, :] == query_doc[:, None]) & (key_pos[None, :] <= positions[:, None])
    scores = jnp.einsum(
        "qkgd,pkd->kgqp",
        grouped,
        key_all.reshape(extent, kv_heads, HD),
        preferred_element_type=jnp.float32,
    ) * (HD ** -0.5)
    scores = jnp.where(visible, scores, -jnp.inf)
    row_max = jnp.max(scores, axis=3, keepdims=True)
    weights = jnp.where(visible, jnp.exp(scores - row_max), 0.0)
    totals = jnp.sum(weights, axis=3)
    blended = jnp.einsum(
        "kgqp,pkd->kgqd",
        weights.astype(jnp.bfloat16),
        value_all.reshape(extent, kv_heads, HD),
        preferred_element_type=jnp.float32,
    )
    attended = (
        (blended / totals[..., None])
        .transpose(2, 0, 1, 3)
        .reshape(tok_dev, columns)
        .astype(jnp.bfloat16)
    )
    gathered = lax.all_gather(attended, "ctx", axis=0, tiled=True)
    units = gathered.reshape(ctx_count * ctx_count, unit_rows, columns)
    balanced = jnp.take(units, unit_plan.reshape(-1), axis=0).reshape(extent, columns)
    partial_value = jnp.dot(balanced, w_out, preferred_element_type=jnp.float32)
    return lax.psum_scatter(
        partial_value.astype(jnp.bfloat16), "tp", scatter_dimension=0, tiled=True
    )


SMEM = pl.BlockSpec(memory_space=pltpu.SMEM)
VMEM = pl.BlockSpec(memory_space=pltpu.VMEM)
HBM = pl.BlockSpec(memory_space=pl.ANY)
TILE = 512


def in_hbm(x):
    return pltpu.with_memory_space_constraint(x, pltpu.HBM)


TOKEN = jax.ShapeDtypeStruct((8, 128), jnp.float32)


def block_shape(w_out, chunks):
    return w_out.shape[0] // chunks, w_out.shape[1] // HALVES


def block_copy(w_hbm, index, w_ref, sem):
    depth, columns = w_ref.shape
    row, column = index // HALVES * depth, index % HALVES * columns
    return pltpu.make_async_copy(
        w_hbm.at[row:row + depth, column:column + columns], w_ref, sem
    )


def prepare_kernel(docs_hbm, k_hbm, v_hbm, q_hbm, w_hbm, after, k_ref, v_ref, q_ref, mask_ref, w_ref, docs, sems):
    lengths = pltpu.make_async_copy(docs_hbm, docs, sems.at[0])
    loads = [
        pltpu.make_async_copy(k_hbm, k_ref, sems.at[1]),
        pltpu.make_async_copy(v_hbm, v_ref, sems.at[2]),
        pltpu.make_async_copy(q_hbm, q_ref, sems.at[3]),
        block_copy(w_hbm, 0, w_ref, sems.at[4]),
    ]
    lengths.start()
    for load in loads:
        load.start()
    lengths.wait()
    rows, window = mask_ref.shape
    base = lax.axis_index("ctx") * rows
    pos = base + lax.broadcasted_iota(jnp.int32, (rows, window), 0)
    start = jnp.zeros((rows, window), jnp.int32)
    end = jnp.int32(0)
    for d in range(docs.shape[0]):
        end = end + docs[d]
        start = jnp.where(pos >= end, end, start)
    key_pos = base + rows - window + lax.broadcasted_iota(jnp.int32, (rows, window), 1)
    mask_ref[...] = jnp.where((key_pos >= start) & (key_pos <= pos), 0.0, -jnp.inf)
    for load in loads:
        load.wait()


def prepare(doc_lengths, key_rows, value_rows, queries, w_out, chunks, after):
    rows = queries.shape[0]
    return pl.pallas_call(
        prepare_kernel,
        out_shape=[
            jax.ShapeDtypeStruct(key_rows.shape, jnp.bfloat16),
            jax.ShapeDtypeStruct(value_rows.shape, jnp.bfloat16),
            jax.ShapeDtypeStruct(queries.shape, jnp.bfloat16),
            jax.ShapeDtypeStruct((rows, 3 * rows), jnp.float32),
            jax.ShapeDtypeStruct(block_shape(w_out, chunks), jnp.bfloat16),
        ],
        in_specs=[HBM] * 6,
        out_specs=[VMEM] * 5,
        scratch_shapes=[
            pltpu.SMEM(doc_lengths.shape, jnp.int32),
            pltpu.SemaphoreType.DMA((5,)),
        ],
        compiler_params=pltpu.CompilerParams(vmem_limit_bytes=4 * MIB),
        cost_estimate=pl.CostEstimate(
            flops=0, bytes_accessed=w_out.size // chunks, transcendentals=0
        ),
        name="prepare",
    )(
        in_hbm(doc_lengths), in_hbm(key_rows), in_hbm(value_rows), in_hbm(queries), w_out, after
    )


def load_kernel(indexes, after, w_hbm, *refs):
    *w_refs, token, sems = refs
    loads = [
        block_copy(w_hbm, index, w_ref, sems.at[i])
        for i, (index, w_ref) in enumerate(zip(indexes, w_refs))
    ]
    for load in loads:
        load.start()
    token[...] = jnp.zeros_like(token)
    for load in loads:
        load.wait()


def load_blocks(indexes, w_out, chunks, after):
    shape = block_shape(w_out, chunks)
    *blocks, token = pl.pallas_call(
        functools.partial(load_kernel, indexes),
        out_shape=[jax.ShapeDtypeStruct(shape, jnp.bfloat16)] * len(indexes) + [TOKEN],
        in_specs=[HBM, HBM],
        out_specs=[VMEM] * (len(indexes) + 1),
        scratch_shapes=[pltpu.SemaphoreType.DMA((len(indexes),))],
        compiler_params=pltpu.CompilerParams(vmem_limit_bytes=1 * MIB),
        cost_estimate=pl.CostEstimate(
            flops=0, bytes_accessed=4 * len(indexes) * shape[0] * shape[1], transcendentals=0
        ),
        name=f"load_{indexes[0]}",
    )(after, w_out)
    return blocks, token


def attend_kernel(groups, q_ref, mask_ref, k0, k_near, k_far, k2, v0, v_near, v_far, v2, *rest):
    out_ref = rest[-1]
    rows = out_ref.shape[0]
    width = out_ref.shape[1] // len(groups)
    heads = width // HD
    window = 3 * rows
    factor = HD ** -0.5 * math.log2(math.e)
    across = lax.axis_index("ctx") == 2
    for i, g in enumerate(groups):
        at = slice(g * HD, (g + 1) * HD)
        k1 = jnp.where(across, k_far[:, at], k_near[:, at])
        v1 = jnp.where(across, v_far[:, at], v_near[:, at])
        keys = jnp.concatenate([k2[:, at], k1, k0[:, at]], axis=0)
        values = jnp.concatenate([v2[:, at], v1, v0[:, at]], axis=0)
        stacked = jnp.concatenate(
            [q_ref[:, g * width + h * HD:g * width + (h + 1) * HD] for h in range(heads)], axis=0
        )
        scores = lax.dot_general(
            stacked, keys, (((1,), (1,)), ((), ())), preferred_element_type=jnp.float32
        ).reshape(heads, rows, window)
        scores = scores + mask_ref[...][None]
        top = jnp.max(scores, axis=2, keepdims=True)
        weights = jnp.exp2((scores - top) * factor)
        total = jnp.sum(weights, axis=2, keepdims=True)
        mixed = jnp.dot(
            weights.astype(jnp.bfloat16).reshape(heads * rows, window),
            values,
            preferred_element_type=jnp.float32,
        ).reshape(heads, rows, HD)
        result = (mixed / total).astype(jnp.bfloat16)
        for h in range(heads):
            out_ref[:, i * width + h * HD:i * width + (h + 1) * HD] = result[h]


def attend(groups, width, queries, mask, keys, values, after):
    rows = queries.shape[0]
    return pl.pallas_call(
        functools.partial(attend_kernel, groups),
        out_shape=jax.ShapeDtypeStruct((rows, len(groups) * width), jnp.bfloat16),
        in_specs=[VMEM] * 10 + [HBM] * len(after),
        out_specs=VMEM,
        compiler_params=pltpu.CompilerParams(vmem_limit_bytes=8 * MIB),
        cost_estimate=pl.CostEstimate(flops=0, bytes_accessed=0, transcendentals=0),
        name=f"attend_{groups[0]}",
    )(queries, mask, *keys, *values, *after)


def lay_out(plan, pieces, column, lhs):
    here = lax.axis_index("ctx")
    core = lax.axis_index("tp")
    first = jnp.where(core == 0, 1, 2)
    owners = [here, here ^ first, here ^ (3 - first), here ^ 3]
    unit_rows = lhs.shape[0] // 16
    swap = jnp.where(core == 0, 8, 0)
    wanted = [plan[slot] for slot in range(16)]
    for owner, piece in zip(owners, pieces):
        for u in range(4):
            slot = jnp.int32(0)
            for s in range(1, 16):
                slot = jnp.where(wanted[s] == owner * 4 + u, s, slot)
            slot = slot ^ swap
            at = pl.ds(pl.multiple_of(slot * unit_rows, unit_rows), unit_rows)
            lhs[at, :] = piece[u * unit_rows:(u + 1) * unit_rows, column:column + lhs.shape[1]]


def step_kernel(index, last, column, has_acc, has_after, *refs):
    refs = list(refs)[has_after:]
    first_half = index % HALVES == 0
    load = None
    if first_half:
        plan, *pieces = refs[:5]
        w_hbm = refs[5]
        del refs[:6]
        sem = refs.pop()
        token = refs.pop()
        next_ref = refs.pop()
        lhs = refs.pop()
        load = block_copy(w_hbm, index + 1, next_ref, sem)
        load.start()
        lay_out(plan, pieces, column, lhs)
    else:
        token = refs.pop()
        lhs = refs.pop(0)
    token[...] = jnp.zeros_like(token)
    w_ref = refs.pop(0)
    acc_ref = refs.pop(0) if has_acc else None
    rows = lhs.shape[0] // 2
    for at in range(0, w_ref.shape[1], TILE):
        to = slice(at, at + TILE)
        product = jnp.dot(lhs[...], w_ref[:, to], preferred_element_type=jnp.float32)
        if has_acc:
            product = product + acc_ref[:, to]
        if last:
            own_ref, sent_ref = refs
            own_ref[:, to] = product[rows:]
            sent_ref[:, to] = product[:rows].astype(jnp.bfloat16)
        else:
            refs[0][:, to] = product
    if load is not None:
        load.wait()


def step(index, last, rows_in, column, block, w_out, acc, after):
    first_half = index % HALVES == 0
    has_acc, has_after = acc is not None, after is not None
    depth, columns = block.shape
    if first_half:
        plan, pieces = rows_in
        total_rows = 4 * pieces[0].shape[0]
        operands, specs = [plan, *pieces, w_out], [SMEM] + [VMEM] * 4 + [HBM]
    else:
        total_rows = rows_in.shape[0]
        operands, specs = [rows_in], [VMEM]
    if last:
        part = (total_rows // 2, columns)
        shapes = [jax.ShapeDtypeStruct(part, jnp.float32), jax.ShapeDtypeStruct(part, jnp.bfloat16)]
    else:
        shapes = [jax.ShapeDtypeStruct((total_rows, columns), jnp.float32)]
    if first_half:
        shapes.append(jax.ShapeDtypeStruct((total_rows, depth), jnp.bfloat16))
        shapes.append(jax.ShapeDtypeStruct(block.shape, jnp.bfloat16))
    shapes.append(TOKEN)
    operands = [after] * has_after + operands + [block] + [acc] * has_acc
    specs = [HBM] * has_after + specs + [VMEM] * (1 + has_acc)
    results = list(pl.pallas_call(
        functools.partial(step_kernel, index, last, column, has_acc, has_after),
        out_shape=shapes,
        in_specs=specs,
        out_specs=[VMEM] * len(shapes),
        scratch_shapes=[pltpu.SemaphoreType.DMA] * first_half,
        input_output_aliases={len(operands) - 1: 0} if has_acc and not last else {},
        compiler_params=pltpu.CompilerParams(vmem_limit_bytes=6 * MIB),
        cost_estimate=pl.CostEstimate(
            flops=2 * total_rows * depth * columns, bytes_accessed=0, transcendentals=0
        ),
        name=f"step_{index}",
    )(*operands))
    token = results.pop()
    following = results.pop() if first_half else None
    lhs = results.pop() if first_half else None
    return results, lhs, following, token


def total_kernel(first, has_out, own_ref, got_ref, *rest):
    out_hbm, buf, sems = rest[has_out:]
    columns = got_ref.shape[1]
    step = columns // 2
    writes = []
    for i in range(2):
        to = slice(i * step, (i + 1) * step)
        at = slice(first + i * step, first + (i + 1) * step)
        value = own_ref[:, to] + got_ref[:, to].astype(jnp.float32)
        buf[:, to] = value.astype(jnp.bfloat16)
        write = pltpu.make_async_copy(buf.at[:, to], out_hbm.at[:, at], sems.at[i])
        write.start()
        writes.append(write)
    for write in writes:
        write.wait()


def total(first, width, own, got, out):
    rows, columns = got.shape
    has_out = out is not None
    return pl.pallas_call(
        functools.partial(total_kernel, first, has_out),
        out_shape=jax.ShapeDtypeStruct((rows, width), jnp.bfloat16),
        in_specs=[VMEM, VMEM] + [HBM] * has_out,
        out_specs=HBM,
        scratch_shapes=[
            pltpu.VMEM((rows, columns), jnp.bfloat16),
            pltpu.SemaphoreType.DMA((2,)),
        ],
        input_output_aliases={2: 0} if has_out else {},
        compiler_params=pltpu.CompilerParams(vmem_limit_bytes=4 * MIB),
        cost_estimate=pl.CostEstimate(
            flops=rows * columns, bytes_accessed=2 * rows * columns, transcendentals=0
        ),
        name=f"total_{first // columns}",
    )(own, got, *([out] if has_out else []))


def gather_rows(own):
    def route(first):
        pairs = []
        for chip in range(4):
            for core in range(2):
                axis = 1 if (core == 0) == first else 2
                pairs.append((chip * 2 + core, (chip ^ axis) * 2 + core))
        return pairs

    near = lax.ppermute(own, ("ctx", "tp"), route(True))
    side = lax.ppermute(own, ("ctx", "tp"), route(False))
    far = lax.ppermute(near, ("ctx", "tp"), route(False))
    return own, near, side, far


def local(queries, key_rows, value_rows, doc_lengths, unit_source, w_out):
    if lax.axis_size("ctx") != 4 or lax.axis_size("tp") != 2 or key_rows.shape[1] != 4 * HD:
        return general(queries, key_rows, value_rows, doc_lengths, unit_source, w_out)
    w_out = in_hbm(w_out)
    kv_heads = key_rows.shape[1] // HD
    width = queries.shape[1] // kv_heads
    two = [(0, 2), (1, 3)]
    value_two = lax.ppermute(value_rows, "ctx", two)
    key_two = lax.ppermute(key_rows, "ctx", two)
    key_near = lax.ppermute(key_rows, "ctx", [(0, 1), (1, 2), (2, 3)])
    value_near = lax.ppermute(value_rows, "ctx", [(0, 1), (2, 3)])
    value_far = lax.ppermute(value_two, "ctx", [(3, 2)])
    own_keys, own_values, held, mask, block = prepare(
        doc_lengths, key_rows, value_rows, queries, w_out, kv_heads, value_two
    )
    keys = (own_keys, key_near, key_near, key_two)
    values = (own_values, value_near, value_far, value_two)
    state = {"blocks": {0: block}, "totals": [None] * HALVES, "before": None}
    gathered, mine, got = [], [], []

    def rows_of(g, after):
        own = attend((g,), width, held, mask, keys, values, after)
        gathered.append(gather_rows(own))
        return own

    def load(wanted, after):
        loaded, token = load_blocks([g * HALVES for g in wanted], w_out, kv_heads, after)
        state["blocks"].update(zip(wanted, loaded))
        return token

    def steps(g):
        last = g == kv_heads - 1
        rows_in, block = (unit_source, gathered[g]), state["blocks"][g]
        for half in range(HALVES):
            results, rows_in, block, state["before"] = step(
                g * HALVES + half, last, rows_in, 0, block, w_out,
                state["totals"][half], state["before"],
            )
            if last:
                mine.append(results[0])
                got.append(lax.ppermute(results[1], "tp", [(0, 1), (1, 0)]))
            else:
                state["totals"][half] = results[0]
        return state["before"]

    own = rows_of(0, [])
    own = rows_of(1, [load((1,), own)])
    own = rows_of(2, [load((2, 3), own), *gathered[0][1:2]])
    done = steps(0)
    rows_of(3, [own, done])
    for g in range(1, kv_heads):
        steps(g)
    columns = w_out.shape[1] // HALVES
    out = None
    for half in range(HALVES):
        out = total(half * columns, w_out.shape[1], mine[half], got[half], out)
    return out


def solution(mesh):
    return jax.shard_map(
        local,
        mesh=mesh,
        in_specs=(
            P(("dp", "ctx"), "tp"),
            P(("dp", "ctx"), "tp"),
            P(("dp", "ctx"), "tp"),
            P("dp"),
            P("dp"),
            P("tp", "ctx"),
        ),
        out_specs=P(("dp", "tp"), "ctx"),
        check_vma=False,
    )
```

```python
import functools
import math

import jax
import jax.numpy as jnp
from jax import lax
from jax.experimental import pallas as pl
from jax.experimental.pallas import tpu as pltpu
from jax.sharding import PartitionSpec as P

HD = 128
MIB = 1 << 20
HALVES = 2


def doc_index(positions, doc_ends):
    return jnp.sum((positions[None, :] >= doc_ends[:, None]).astype(jnp.int32), axis=0)


def general(queries, key_rows, value_rows, doc_lengths, unit_source, w_out):
    ctx_count = lax.axis_size("ctx")
    ctx_index = lax.axis_index("ctx")
    tok_dev, columns = queries.shape
    unit_rows = tok_dev // ctx_count
    head_count = columns // HD
    kv_heads = key_rows.shape[1] // HD
    group_size = head_count // kv_heads
    unit_plan = unit_source.reshape(ctx_count, ctx_count)
    positions = ctx_index * tok_dev + jnp.arange(tok_dev, dtype=jnp.int32)
    doc_ends = jnp.cumsum(doc_lengths)
    query_doc = doc_index(positions, doc_ends)
    grouped = queries.reshape(tok_dev, kv_heads, group_size, HD)
    key_all = lax.all_gather(key_rows, "ctx", axis=0, tiled=True)
    value_all = lax.all_gather(value_rows, "ctx", axis=0, tiled=True)
    extent = key_all.shape[0]
    key_pos = jnp.arange(extent, dtype=jnp.int32)
    key_doc = doc_index(key_pos, doc_ends)
    visible = (key_doc[None, :] == query_doc[:, None]) & (key_pos[None, :] <= positions[:, None])
    scores = jnp.einsum(
        "qkgd,pkd->kgqp",
        grouped,
        key_all.reshape(extent, kv_heads, HD),
        preferred_element_type=jnp.float32,
    ) * (HD ** -0.5)
    scores = jnp.where(visible, scores, -jnp.inf)
    row_max = jnp.max(scores, axis=3, keepdims=True)
    weights = jnp.where(visible, jnp.exp(scores - row_max), 0.0)
    totals = jnp.sum(weights, axis=3)
    blended = jnp.einsum(
        "kgqp,pkd->kgqd",
        weights.astype(jnp.bfloat16),
        value_all.reshape(extent, kv_heads, HD),
        preferred_element_type=jnp.float32,
    )
    attended = (
        (blended / totals[..., None])
        .transpose(2, 0, 1, 3)
        .reshape(tok_dev, columns)
        .astype(jnp.bfloat16)
    )
    gathered = lax.all_gather(attended, "ctx", axis=0, tiled=True)
    units = gathered.reshape(ctx_count * ctx_count, unit_rows, columns)
    balanced = jnp.take(units, unit_plan.reshape(-1), axis=0).reshape(extent, columns)
    partial_value = jnp.dot(balanced, w_out, preferred_element_type=jnp.float32)
    return lax.psum_scatter(
        partial_value.astype(jnp.bfloat16), "tp", scatter_dimension=0, tiled=True
    )


SMEM = pl.BlockSpec(memory_space=pltpu.SMEM)
VMEM = pl.BlockSpec(memory_space=pltpu.VMEM)
HBM = pl.BlockSpec(memory_space=pl.ANY)
TILE = 512


def in_hbm(x):
    return pltpu.with_memory_space_constraint(x, pltpu.HBM)


TOKEN = jax.ShapeDtypeStruct((8, 128), jnp.float32)


def block_shape(w_out, chunks):
    return w_out.shape[0] // chunks, w_out.shape[1] // HALVES


def block_copy(w_hbm, index, w_ref, sem):
    depth, columns = w_ref.shape
    row, column = index // HALVES * depth, index % HALVES * columns
    return pltpu.make_async_copy(
        w_hbm.at[row:row + depth, column:column + columns], w_ref, sem
    )


def prepare_kernel(docs_hbm, k_hbm, v_hbm, q_hbm, w_hbm, after, k_ref, v_ref, q_ref, mask_ref, left_ref, right_ref, docs, sems):
    lengths = pltpu.make_async_copy(docs_hbm, docs, sems.at[0])
    loads = [
        pltpu.make_async_copy(k_hbm, k_ref, sems.at[1]),
        pltpu.make_async_copy(v_hbm, v_ref, sems.at[2]),
        pltpu.make_async_copy(q_hbm, q_ref, sems.at[3]),
        block_copy(w_hbm, 0, left_ref, sems.at[4]),
        block_copy(w_hbm, 1, right_ref, sems.at[5]),
    ]
    lengths.start()
    for load in loads:
        load.start()
    lengths.wait()
    rows, window = mask_ref.shape
    base = lax.axis_index("ctx") * rows
    pos = base + lax.broadcasted_iota(jnp.int32, (rows, window), 0)
    start = jnp.zeros((rows, window), jnp.int32)
    end = jnp.int32(0)
    for d in range(docs.shape[0]):
        end = end + docs[d]
        start = jnp.where(pos >= end, end, start)
    key_pos = base + rows - window + lax.broadcasted_iota(jnp.int32, (rows, window), 1)
    mask_ref[...] = jnp.where((key_pos >= start) & (key_pos <= pos), 0.0, -jnp.inf)
    for load in loads:
        load.wait()


def prepare(doc_lengths, key_rows, value_rows, queries, w_out, chunks, after):
    rows = queries.shape[0]
    return pl.pallas_call(
        prepare_kernel,
        out_shape=[
            jax.ShapeDtypeStruct(key_rows.shape, jnp.bfloat16),
            jax.ShapeDtypeStruct(value_rows.shape, jnp.bfloat16),
            jax.ShapeDtypeStruct(queries.shape, jnp.bfloat16),
            jax.ShapeDtypeStruct((rows, 3 * rows), jnp.float32),
            jax.ShapeDtypeStruct(block_shape(w_out, chunks), jnp.bfloat16),
            jax.ShapeDtypeStruct(block_shape(w_out, chunks), jnp.bfloat16),
        ],
        in_specs=[HBM] * 6,
        out_specs=[VMEM] * 6,
        scratch_shapes=[
            pltpu.SMEM(doc_lengths.shape, jnp.int32),
            pltpu.SemaphoreType.DMA((6,)),
        ],
        compiler_params=pltpu.CompilerParams(vmem_limit_bytes=4 * MIB),
        cost_estimate=pl.CostEstimate(
            flops=0, bytes_accessed=2 * w_out.size // chunks, transcendentals=0
        ),
        name="prepare",
    )(
        in_hbm(doc_lengths), in_hbm(key_rows), in_hbm(value_rows), in_hbm(queries), w_out, after
    )


def load_kernel(indexes, after, w_hbm, *refs):
    *w_refs, token, sems = refs
    loads = [
        block_copy(w_hbm, index, w_ref, sems.at[i])
        for i, (index, w_ref) in enumerate(zip(indexes, w_refs))
    ]
    for load in loads:
        load.start()
    token[...] = jnp.zeros_like(token)
    for load in loads:
        load.wait()


def load_blocks(indexes, w_out, chunks, after):
    shape = block_shape(w_out, chunks)
    *blocks, token = pl.pallas_call(
        functools.partial(load_kernel, indexes),
        out_shape=[jax.ShapeDtypeStruct(shape, jnp.bfloat16)] * len(indexes) + [TOKEN],
        in_specs=[HBM, HBM],
        out_specs=[VMEM] * (len(indexes) + 1),
        scratch_shapes=[pltpu.SemaphoreType.DMA((len(indexes),))],
        compiler_params=pltpu.CompilerParams(vmem_limit_bytes=1 * MIB),
        cost_estimate=pl.CostEstimate(
            flops=0, bytes_accessed=4 * len(indexes) * shape[0] * shape[1], transcendentals=0
        ),
        name=f"load_{indexes[0]}",
    )(after, w_out)
    return blocks, token


def attend_kernel(groups, q_ref, mask_ref, k0, k_near, k_far, k2, v0, v_near, v_far, v2, *rest):
    out_ref = rest[-1]
    rows = out_ref.shape[0]
    width = out_ref.shape[1] // len(groups)
    heads = width // HD
    window = 3 * rows
    factor = HD ** -0.5 * math.log2(math.e)
    across = lax.axis_index("ctx") == 2
    for i, g in enumerate(groups):
        at = slice(g * HD, (g + 1) * HD)
        k1 = jnp.where(across, k_far[:, at], k_near[:, at])
        v1 = jnp.where(across, v_far[:, at], v_near[:, at])
        keys = jnp.concatenate([k2[:, at], k1, k0[:, at]], axis=0)
        values = jnp.concatenate([v2[:, at], v1, v0[:, at]], axis=0)
        stacked = jnp.concatenate(
            [q_ref[:, g * width + h * HD:g * width + (h + 1) * HD] for h in range(heads)], axis=0
        )
        scores = lax.dot_general(
            stacked, keys, (((1,), (1,)), ((), ())), preferred_element_type=jnp.float32
        ).reshape(heads, rows, window)
        scores = scores + mask_ref[...][None]
        top = jnp.max(scores, axis=2, keepdims=True)
        weights = jnp.exp2((scores - top) * factor)
        total = jnp.sum(weights, axis=2, keepdims=True)
        mixed = jnp.dot(
            weights.astype(jnp.bfloat16).reshape(heads * rows, window),
            values,
            preferred_element_type=jnp.float32,
        ).reshape(heads, rows, HD)
        result = (mixed / total).astype(jnp.bfloat16)
        for h in range(heads):
            out_ref[:, i * width + h * HD:i * width + (h + 1) * HD] = result[h]


def attend(groups, width, queries, mask, keys, values, after):
    rows = queries.shape[0]
    return pl.pallas_call(
        functools.partial(attend_kernel, groups),
        out_shape=jax.ShapeDtypeStruct((rows, len(groups) * width), jnp.bfloat16),
        in_specs=[VMEM] * 10 + [HBM] * len(after),
        out_specs=VMEM,
        compiler_params=pltpu.CompilerParams(vmem_limit_bytes=8 * MIB),
        cost_estimate=pl.CostEstimate(flops=0, bytes_accessed=0, transcendentals=0),
        name=f"attend_{groups[0]}",
    )(queries, mask, *keys, *values, *after)


def lay_out(plan, pieces, column, lhs):
    here = lax.axis_index("ctx")
    core = lax.axis_index("tp")
    first = jnp.where(core == 0, 1, 2)
    owners = [here, here ^ first, here ^ (3 - first), here ^ 3]
    unit_rows = lhs.shape[0] // 16
    swap = jnp.where(core == 0, 8, 0)
    wanted = [plan[slot] for slot in range(16)]
    for owner, piece in zip(owners, pieces):
        for u in range(4):
            slot = jnp.int32(0)
            for s in range(1, 16):
                slot = jnp.where(wanted[s] == owner * 4 + u, s, slot)
            slot = slot ^ swap
            at = pl.ds(pl.multiple_of(slot * unit_rows, unit_rows), unit_rows)
            lhs[at, :] = piece[u * unit_rows:(u + 1) * unit_rows, column:column + lhs.shape[1]]


def step_kernel(index, last, column, first, columns, has_acc, has_after, has_load, *refs):
    refs = list(refs)[has_after:]
    first_half = index % HALVES == 0
    load = None
    if has_load:
        sem = refs.pop()
    token = refs.pop()
    if has_load:
        load = block_copy(refs.pop(0), index + 1, refs.pop(), sem)
        load.start()
    if first_half:
        plan, *pieces = refs[:5]
        del refs[:5]
        lhs = refs.pop()
        lay_out(plan, pieces, column, lhs)
    else:
        lhs = refs.pop(0)
    token[...] = jnp.zeros_like(token)
    w_ref = refs.pop(0)
    acc_ref = refs.pop(0) if has_acc else None
    rows = lhs.shape[0] // 2
    for start in range(0, columns, TILE):
        to = slice(start, start + TILE)
        at = slice(first + start, first + start + TILE)
        product = jnp.dot(lhs[...], w_ref[:, at], preferred_element_type=jnp.float32)
        if has_acc:
            product = product + acc_ref[:, at]
        if last:
            own_ref, sent_ref = refs
            own_ref[:, to] = product[rows:]
            sent_ref[:, to] = product[:rows].astype(jnp.bfloat16)
        else:
            refs[0][:, to] = product
    if load is not None:
        load.wait()


def step(index, last, rows_in, column, block, first, columns, w_out, acc, after):
    first_half = index % HALVES == 0
    has_acc, has_after, has_load = acc is not None, after is not None, w_out is not None
    depth = block.shape[0]
    if first_half:
        plan, pieces = rows_in
        total_rows = 4 * pieces[0].shape[0]
        operands, specs = [plan, *pieces], [SMEM] + [VMEM] * 4
    else:
        total_rows = rows_in.shape[0]
        operands, specs = [rows_in], [VMEM]
    if last:
        part = (total_rows // 2, columns)
        shapes = [jax.ShapeDtypeStruct(part, jnp.float32), jax.ShapeDtypeStruct(part, jnp.bfloat16)]
    else:
        shapes = [jax.ShapeDtypeStruct((total_rows, columns), jnp.float32)]
    if first_half:
        shapes.append(jax.ShapeDtypeStruct((total_rows, depth), jnp.bfloat16))
    if has_load:
        shapes.append(jax.ShapeDtypeStruct(block.shape, jnp.bfloat16))
    shapes.append(TOKEN)
    operands = [after] * has_after + [w_out] * has_load + operands + [block] + [acc] * has_acc
    specs = [HBM] * (has_after + has_load) + specs + [VMEM] * (1 + has_acc)
    results = list(pl.pallas_call(
        functools.partial(
            step_kernel, index, last, column, first, columns, has_acc, has_after, has_load
        ),
        out_shape=shapes,
        in_specs=specs,
        out_specs=[VMEM] * len(shapes),
        scratch_shapes=[pltpu.SemaphoreType.DMA] * has_load,
        input_output_aliases={len(operands) - 1: 0} if has_acc and not last else {},
        compiler_params=pltpu.CompilerParams(vmem_limit_bytes=6 * MIB),
        cost_estimate=pl.CostEstimate(
            flops=2 * total_rows * depth * columns, bytes_accessed=0, transcendentals=0
        ),
        name=f"step_{index}_{first // columns}",
    )(*operands))
    token = results.pop()
    following = results.pop() if has_load else None
    lhs = results.pop() if first_half else rows_in
    return results, lhs, following, token


def total_kernel(first, count, has_out, *refs):
    own_refs, got_refs = refs[:count], refs[count:2 * count]
    out_hbm, buf, sems = refs[2 * count + has_out:]
    writes, at = [], 0
    for own_ref, got_ref in zip(own_refs, got_refs):
        columns = own_ref.shape[1]
        for start in range(0, columns, 2 * TILE):
            to = slice(start, start + 2 * TILE)
            value = own_ref[:, to] + got_ref[:, to].astype(jnp.float32)
            here = slice(at + start, at + start + 2 * TILE)
            there = slice(first + at + start, first + at + start + 2 * TILE)
            buf[:, here] = value.astype(jnp.bfloat16)
            write = pltpu.make_async_copy(buf.at[:, here], out_hbm.at[:, there], sems.at[len(writes)])
            write.start()
            writes.append(write)
        at += columns
    for write in writes:
        write.wait()


def total(first, width, own, got, out):
    rows = own[0].shape[0]
    columns = sum(x.shape[1] for x in own)
    count, has_out = len(own), out is not None
    return pl.pallas_call(
        functools.partial(total_kernel, first, count, has_out),
        out_shape=jax.ShapeDtypeStruct((rows, width), jnp.bfloat16),
        in_specs=[VMEM] * (2 * count) + [HBM] * has_out,
        out_specs=HBM,
        scratch_shapes=[
            pltpu.VMEM((rows, columns), jnp.bfloat16),
            pltpu.SemaphoreType.DMA((columns // (2 * TILE),)),
        ],
        input_output_aliases={2 * count: 0} if has_out else {},
        compiler_params=pltpu.CompilerParams(vmem_limit_bytes=4 * MIB),
        cost_estimate=pl.CostEstimate(
            flops=rows * columns, bytes_accessed=2 * rows * columns, transcendentals=0
        ),
        name=f"total_{first}",
    )(*own, *got, *([out] if has_out else []))


def gate_kernel(x, after, out):
    pass


def gate(x, after):
    return pl.pallas_call(
        gate_kernel,
        out_shape=jax.ShapeDtypeStruct(x.shape, x.dtype),
        in_specs=[HBM, HBM],
        out_specs=HBM,
        input_output_aliases={0: 0},
        compiler_params=pltpu.CompilerParams(vmem_limit_bytes=1 * MIB),
        cost_estimate=pl.CostEstimate(flops=0, bytes_accessed=0, transcendentals=0),
        name="gate",
    )(x, after)


def gather_rows(own):
    def route(first):
        pairs = []
        for chip in range(4):
            for core in range(2):
                axis = 1 if (core == 0) == first else 2
                pairs.append((chip * 2 + core, (chip ^ axis) * 2 + core))
        return pairs

    near = lax.ppermute(own, ("ctx", "tp"), route(True))
    side = lax.ppermute(own, ("ctx", "tp"), route(False))

    def forward(after):
        first = near if after is None else gate(near, after)
        return own, first, side, lax.ppermute(first, ("ctx", "tp"), route(False))

    return near, side, forward


def local(queries, key_rows, value_rows, doc_lengths, unit_source, w_out):
    if lax.axis_size("ctx") != 4 or lax.axis_size("tp") != 2 or key_rows.shape[1] != 4 * HD:
        return general(queries, key_rows, value_rows, doc_lengths, unit_source, w_out)
    w_out = in_hbm(w_out)
    kv_heads = key_rows.shape[1] // HD
    width = queries.shape[1] // kv_heads
    two = [(0, 2), (1, 3)]
    value_two = lax.ppermute(value_rows, "ctx", two)
    key_two = lax.ppermute(key_rows, "ctx", two)
    key_near = lax.ppermute(key_rows, "ctx", [(0, 1), (1, 2), (2, 3)])
    value_near = lax.ppermute(value_rows, "ctx", [(0, 1), (2, 3)])
    value_far = lax.ppermute(value_two, "ctx", [(3, 2)])
    own_keys, own_values, held, mask, left, right = prepare(
        doc_lengths, key_rows, value_rows, queries, w_out, kv_heads, value_two
    )
    keys = (own_keys, key_near, key_near, key_two)
    values = (own_values, value_near, value_far, value_two)
    half_columns = w_out.shape[1] // HALVES
    state = {"left": {0: left}, "right": {0: right}, "totals": [None] * HALVES, "before": None}
    rows, mine, got = {}, [], []

    def rows_of(groups, after):
        own = attend(groups, width, held, mask, keys, values, after)
        near, side, forward = gather_rows(own)

        def arrive(after):
            pieces = forward(after)
            for i, g in enumerate(groups):
                rows[g] = (pieces, i * width)
            return pieces[1]

        return own, arrive

    def load(wanted, after):
        loaded, token = load_blocks([g * HALVES for g in wanted], w_out, kv_heads, after)
        state["left"].update(zip(wanted, loaded))
        return token

    def steps(g):
        last = g == kv_heads - 1
        pieces, column = rows[g]
        loads = g not in state["right"]
        first, lhs, following, state["before"] = step(
            g * HALVES, last, (unit_source, pieces), column, state["left"][g], 0, half_columns,
            w_out if loads else None, state["totals"][0], state["before"],
        )
        if loads:
            state["right"][g] = following
        parts = 1
        seconds = []
        for i in range(parts):
            second, lhs, _, state["before"] = step(
                g * HALVES + 1, last, lhs, column, state["right"][g],
                i * half_columns // parts, half_columns // parts, None,
                state["totals"][1], state["before"],
            )
            seconds.append(second)
        if last:
            for kept, sent in [first, *seconds]:
                mine.append(kept)
                got.append(lax.ppermute(sent, "tp", [(0, 1), (1, 0)]))
        else:
            state["totals"] = [first[0], seconds[0][0]]
        return state["before"]

    own, arrive = rows_of((0,), [])
    near = arrive(load((1, 2), own))
    own, arrive = rows_of((1, 2), [near])
    done = steps(0)
    near = arrive(done)
    _, arrive = rows_of((3,), [load((3,), near), done])
    arrive(steps(1))
    for g in range(2, kv_heads):
        steps(g)
    out = total(0, w_out.shape[1], mine[:1], got[:1], None)
    return total(half_columns, w_out.shape[1], mine[1:], got[1:], out)


def solution(mesh):
    return jax.shard_map(
        local,
        mesh=mesh,
        in_specs=(
            P(("dp", "ctx"), "tp"),
            P(("dp", "ctx"), "tp"),
            P(("dp", "ctx"), "tp"),
            P("dp"),
            P("dp"),
            P("tp", "ctx"),
        ),
        out_specs=P(("dp", "tp"), "ctx"),
        check_vma=False,
    )
```

```python
import functools
import math

import jax
import jax.numpy as jnp
from jax import lax
from jax.experimental import pallas as pl
from jax.experimental.pallas import tpu as pltpu
from jax.sharding import PartitionSpec as P

HD = 128
MIB = 1 << 20
HALVES = 2


def doc_index(positions, doc_ends):
    return jnp.sum((positions[None, :] >= doc_ends[:, None]).astype(jnp.int32), axis=0)


def general(queries, key_rows, value_rows, doc_lengths, unit_source, w_out):
    ctx_count = lax.axis_size("ctx")
    ctx_index = lax.axis_index("ctx")
    tok_dev, columns = queries.shape
    unit_rows = tok_dev // ctx_count
    head_count = columns // HD
    kv_heads = key_rows.shape[1] // HD
    group_size = head_count // kv_heads
    unit_plan = unit_source.reshape(ctx_count, ctx_count)
    positions = ctx_index * tok_dev + jnp.arange(tok_dev, dtype=jnp.int32)
    doc_ends = jnp.cumsum(doc_lengths)
    query_doc = doc_index(positions, doc_ends)
    grouped = queries.reshape(tok_dev, kv_heads, group_size, HD)
    key_all = lax.all_gather(key_rows, "ctx", axis=0, tiled=True)
    value_all = lax.all_gather(value_rows, "ctx", axis=0, tiled=True)
    extent = key_all.shape[0]
    key_pos = jnp.arange(extent, dtype=jnp.int32)
    key_doc = doc_index(key_pos, doc_ends)
    visible = (key_doc[None, :] == query_doc[:, None]) & (key_pos[None, :] <= positions[:, None])
    scores = jnp.einsum(
        "qkgd,pkd->kgqp",
        grouped,
        key_all.reshape(extent, kv_heads, HD),
        preferred_element_type=jnp.float32,
    ) * (HD ** -0.5)
    scores = jnp.where(visible, scores, -jnp.inf)
    row_max = jnp.max(scores, axis=3, keepdims=True)
    weights = jnp.where(visible, jnp.exp(scores - row_max), 0.0)
    totals = jnp.sum(weights, axis=3)
    blended = jnp.einsum(
        "kgqp,pkd->kgqd",
        weights.astype(jnp.bfloat16),
        value_all.reshape(extent, kv_heads, HD),
        preferred_element_type=jnp.float32,
    )
    attended = (
        (blended / totals[..., None])
        .transpose(2, 0, 1, 3)
        .reshape(tok_dev, columns)
        .astype(jnp.bfloat16)
    )
    gathered = lax.all_gather(attended, "ctx", axis=0, tiled=True)
    units = gathered.reshape(ctx_count * ctx_count, unit_rows, columns)
    balanced = jnp.take(units, unit_plan.reshape(-1), axis=0).reshape(extent, columns)
    partial_value = jnp.dot(balanced, w_out, preferred_element_type=jnp.float32)
    return lax.psum_scatter(
        partial_value.astype(jnp.bfloat16), "tp", scatter_dimension=0, tiled=True
    )


SMEM = pl.BlockSpec(memory_space=pltpu.SMEM)
VMEM = pl.BlockSpec(memory_space=pltpu.VMEM)
HBM = pl.BlockSpec(memory_space=pl.ANY)
TILE = 512


def in_hbm(x):
    return pltpu.with_memory_space_constraint(x, pltpu.HBM)


TOKEN = jax.ShapeDtypeStruct((8, 128), jnp.float32)


def block_shape(w_out, chunks):
    return w_out.shape[0] // chunks, w_out.shape[1] // HALVES


def block_copy(w_hbm, index, w_ref, sem):
    depth, columns = w_ref.shape
    row, column = index // HALVES * depth, index % HALVES * columns
    return pltpu.make_async_copy(
        w_hbm.at[row:row + depth, column:column + columns], w_ref, sem
    )


def prepare_kernel(docs_hbm, k_hbm, v_hbm, q_hbm, w_hbm, k_ref, v_ref, q_ref, mask_ref, left_ref, right_ref, docs, sems):
    lengths = pltpu.make_async_copy(docs_hbm, docs, sems.at[0])
    loads = [
        pltpu.make_async_copy(k_hbm, k_ref, sems.at[1]),
        pltpu.make_async_copy(v_hbm, v_ref, sems.at[2]),
        pltpu.make_async_copy(q_hbm, q_ref, sems.at[3]),
        block_copy(w_hbm, 0, left_ref, sems.at[4]),
        block_copy(w_hbm, 1, right_ref, sems.at[5]),
    ]
    lengths.start()
    for load in loads:
        load.start()
    lengths.wait()
    rows, window = mask_ref.shape
    base = lax.axis_index("ctx") * rows
    pos = base + lax.broadcasted_iota(jnp.int32, (rows, window), 0)
    start = jnp.zeros((rows, window), jnp.int32)
    end = jnp.int32(0)
    for d in range(docs.shape[0]):
        end = end + docs[d]
        start = jnp.where(pos >= end, end, start)
    key_pos = base + rows - window + lax.broadcasted_iota(jnp.int32, (rows, window), 1)
    mask_ref[...] = jnp.where((key_pos >= start) & (key_pos <= pos), 0.0, -jnp.inf)
    for load in loads:
        load.wait()


def prepare(doc_lengths, key_rows, value_rows, queries, w_out, chunks):
    rows = queries.shape[0]
    return pl.pallas_call(
        prepare_kernel,
        out_shape=[
            jax.ShapeDtypeStruct(key_rows.shape, jnp.bfloat16),
            jax.ShapeDtypeStruct(value_rows.shape, jnp.bfloat16),
            jax.ShapeDtypeStruct(queries.shape, jnp.bfloat16),
            jax.ShapeDtypeStruct((rows, 3 * rows), jnp.float32),
            jax.ShapeDtypeStruct(block_shape(w_out, chunks), jnp.bfloat16),
            jax.ShapeDtypeStruct(block_shape(w_out, chunks), jnp.bfloat16),
        ],
        in_specs=[HBM] * 5,
        out_specs=[VMEM] * 6,
        scratch_shapes=[
            pltpu.SMEM(doc_lengths.shape, jnp.int32),
            pltpu.SemaphoreType.DMA((6,)),
        ],
        compiler_params=pltpu.CompilerParams(vmem_limit_bytes=4 * MIB),
        cost_estimate=pl.CostEstimate(
            flops=0, bytes_accessed=2 * w_out.size // chunks, transcendentals=0
        ),
        name="prepare",
    )(
        in_hbm(doc_lengths), in_hbm(key_rows), in_hbm(value_rows), in_hbm(queries), w_out
    )


def load_kernel(indexes, after, w_hbm, *refs):
    *w_refs, token, sems = refs
    loads = [
        block_copy(w_hbm, index, w_ref, sems.at[i])
        for i, (index, w_ref) in enumerate(zip(indexes, w_refs))
    ]
    for load in loads:
        load.start()
    token[...] = jnp.zeros_like(token)
    for load in loads:
        load.wait()


def load_blocks(indexes, w_out, chunks, after):
    shape = block_shape(w_out, chunks)
    *blocks, token = pl.pallas_call(
        functools.partial(load_kernel, indexes),
        out_shape=[jax.ShapeDtypeStruct(shape, jnp.bfloat16)] * len(indexes) + [TOKEN],
        in_specs=[HBM, HBM],
        out_specs=[VMEM] * (len(indexes) + 1),
        scratch_shapes=[pltpu.SemaphoreType.DMA((len(indexes),))],
        compiler_params=pltpu.CompilerParams(vmem_limit_bytes=1 * MIB),
        cost_estimate=pl.CostEstimate(
            flops=0, bytes_accessed=4 * len(indexes) * shape[0] * shape[1], transcendentals=0
        ),
        name=f"load_{indexes[0]}",
    )(after, w_out)
    return blocks, token


def attend_kernel(groups, q_ref, mask_ref, k0, k_near, k_far, k2, v0, v_near, v_far, v2, *rest):
    out_ref = rest[-1]
    rows = out_ref.shape[0]
    width = out_ref.shape[1] // len(groups)
    heads = width // HD
    window = 3 * rows
    factor = HD ** -0.5 * math.log2(math.e)
    across = lax.axis_index("ctx") == 2
    for i, g in enumerate(groups):
        at = slice(g * HD, (g + 1) * HD)
        k1 = jnp.where(across, k_far[:, at], k_near[:, at])
        v1 = jnp.where(across, v_far[:, at], v_near[:, at])
        keys = jnp.concatenate([k2[:, at], k1, k0[:, at]], axis=0)
        values = jnp.concatenate([v2[:, at], v1, v0[:, at]], axis=0)
        stacked = jnp.concatenate(
            [q_ref[:, g * width + h * HD:g * width + (h + 1) * HD] for h in range(heads)], axis=0
        )
        scores = lax.dot_general(
            stacked, keys, (((1,), (1,)), ((), ())), preferred_element_type=jnp.float32
        ).reshape(heads, rows, window)
        scores = scores + mask_ref[...][None]
        top = jnp.max(scores, axis=2, keepdims=True)
        weights = jnp.exp2((scores - top) * factor)
        total = jnp.sum(weights, axis=2, keepdims=True)
        mixed = jnp.dot(
            weights.astype(jnp.bfloat16).reshape(heads * rows, window),
            values,
            preferred_element_type=jnp.float32,
        ).reshape(heads, rows, HD)
        result = (mixed / total).astype(jnp.bfloat16)
        for h in range(heads):
            out_ref[:, i * width + h * HD:i * width + (h + 1) * HD] = result[h]


def attend(groups, width, queries, mask, keys, values, after):
    rows = queries.shape[0]
    return pl.pallas_call(
        functools.partial(attend_kernel, groups),
        out_shape=jax.ShapeDtypeStruct((rows, len(groups) * width), jnp.bfloat16),
        in_specs=[VMEM] * 10 + [HBM] * len(after),
        out_specs=VMEM,
        compiler_params=pltpu.CompilerParams(vmem_limit_bytes=8 * MIB),
        cost_estimate=pl.CostEstimate(flops=0, bytes_accessed=0, transcendentals=0),
        name=f"attend_{groups[0]}",
    )(queries, mask, *keys, *values, *after)


def lay_out(plan, pieces, column, lhs):
    here = lax.axis_index("ctx")
    core = lax.axis_index("tp")
    first = jnp.where(core == 0, 1, 2)
    owners = [here, here ^ first, here ^ (3 - first), here ^ 3]
    unit_rows = lhs.shape[0] // 16
    swap = jnp.where(core == 0, 8, 0)
    wanted = [plan[slot] for slot in range(16)]
    for owner, piece in zip(owners, pieces):
        for u in range(4):
            slot = jnp.int32(0)
            for s in range(1, 16):
                slot = jnp.where(wanted[s] == owner * 4 + u, s, slot)
            slot = slot ^ swap
            at = pl.ds(pl.multiple_of(slot * unit_rows, unit_rows), unit_rows)
            lhs[at, :] = piece[u * unit_rows:(u + 1) * unit_rows, column:column + lhs.shape[1]]


def step_kernel(index, last, column, first, columns, has_acc, has_after, has_load, *refs):
    refs = list(refs)[has_after:]
    first_half = index % HALVES == 0
    load = None
    if has_load:
        sem = refs.pop()
    token = refs.pop()
    if has_load:
        load = block_copy(refs.pop(0), index + 1, refs.pop(), sem)
        load.start()
    if first_half:
        plan, *pieces = refs[:5]
        del refs[:5]
        lhs = refs.pop()
        lay_out(plan, pieces, column, lhs)
    else:
        lhs = refs.pop(0)
    token[...] = jnp.zeros_like(token)
    w_ref = refs.pop(0)
    acc_ref = refs.pop(0) if has_acc else None
    rows = lhs.shape[0] // 2
    for start in range(0, columns, TILE):
        to = slice(start, start + TILE)
        at = slice(first + start, first + start + TILE)
        product = jnp.dot(lhs[...], w_ref[:, at], preferred_element_type=jnp.float32)
        if has_acc:
            product = product + acc_ref[:, at]
        if last:
            own_ref, sent_ref = refs
            own_ref[:, to] = product[rows:]
            sent_ref[:, to] = product[:rows].astype(jnp.bfloat16)
        else:
            refs[0][:, to] = product
    if load is not None:
        load.wait()


def step(index, last, rows_in, column, block, first, columns, w_out, acc, after):
    first_half = index % HALVES == 0
    has_acc, has_after, has_load = acc is not None, after is not None, w_out is not None
    depth = block.shape[0]
    if first_half:
        plan, pieces = rows_in
        total_rows = 4 * pieces[0].shape[0]
        operands, specs = [plan, *pieces], [SMEM] + [VMEM] * 4
    else:
        total_rows = rows_in.shape[0]
        operands, specs = [rows_in], [VMEM]
    if last:
        part = (total_rows // 2, columns)
        shapes = [jax.ShapeDtypeStruct(part, jnp.float32), jax.ShapeDtypeStruct(part, jnp.bfloat16)]
    else:
        shapes = [jax.ShapeDtypeStruct((total_rows, columns), jnp.float32)]
    if first_half:
        shapes.append(jax.ShapeDtypeStruct((total_rows, depth), jnp.bfloat16))
    if has_load:
        shapes.append(jax.ShapeDtypeStruct(block.shape, jnp.bfloat16))
    shapes.append(TOKEN)
    operands = [after] * has_after + [w_out] * has_load + operands + [block] + [acc] * has_acc
    specs = [HBM] * (has_after + has_load) + specs + [VMEM] * (1 + has_acc)
    results = list(pl.pallas_call(
        functools.partial(
            step_kernel, index, last, column, first, columns, has_acc, has_after, has_load
        ),
        out_shape=shapes,
        in_specs=specs,
        out_specs=[VMEM] * len(shapes),
        scratch_shapes=[pltpu.SemaphoreType.DMA] * has_load,
        input_output_aliases={len(operands) - 1: 0} if has_acc and not last else {},
        compiler_params=pltpu.CompilerParams(vmem_limit_bytes=6 * MIB),
        cost_estimate=pl.CostEstimate(
            flops=2 * total_rows * depth * columns, bytes_accessed=0, transcendentals=0
        ),
        name=f"step_{index}_{first // columns}",
    )(*operands))
    token = results.pop()
    following = results.pop() if has_load else None
    lhs = results.pop() if first_half else rows_in
    return results, lhs, following, token


def total_kernel(first, count, has_out, *refs):
    own_refs, got_refs = refs[:count], refs[count:2 * count]
    out_hbm, buf, sems = refs[2 * count + has_out:]
    writes, at = [], 0
    for own_ref, got_ref in zip(own_refs, got_refs):
        columns = own_ref.shape[1]
        for start in range(0, columns, 2 * TILE):
            to = slice(start, start + 2 * TILE)
            value = own_ref[:, to] + got_ref[:, to].astype(jnp.float32)
            here = slice(at + start, at + start + 2 * TILE)
            there = slice(first + at + start, first + at + start + 2 * TILE)
            buf[:, here] = value.astype(jnp.bfloat16)
            write = pltpu.make_async_copy(buf.at[:, here], out_hbm.at[:, there], sems.at[len(writes)])
            write.start()
            writes.append(write)
        at += columns
    for write in writes:
        write.wait()


def total(first, width, own, got, out):
    rows = own[0].shape[0]
    columns = sum(x.shape[1] for x in own)
    count, has_out = len(own), out is not None
    return pl.pallas_call(
        functools.partial(total_kernel, first, count, has_out),
        out_shape=jax.ShapeDtypeStruct((rows, width), jnp.bfloat16),
        in_specs=[VMEM] * (2 * count) + [HBM] * has_out,
        out_specs=HBM,
        scratch_shapes=[
            pltpu.VMEM((rows, columns), jnp.bfloat16),
            pltpu.SemaphoreType.DMA((columns // (2 * TILE),)),
        ],
        input_output_aliases={2 * count: 0} if has_out else {},
        compiler_params=pltpu.CompilerParams(vmem_limit_bytes=4 * MIB),
        cost_estimate=pl.CostEstimate(
            flops=rows * columns, bytes_accessed=2 * rows * columns, transcendentals=0
        ),
        name=f"total_{first}",
    )(*own, *got, *([out] if has_out else []))


def gate_kernel(x, after, out):
    pass


def gate(x, after):
    return pl.pallas_call(
        gate_kernel,
        out_shape=jax.ShapeDtypeStruct(x.shape, x.dtype),
        in_specs=[HBM, HBM],
        out_specs=HBM,
        input_output_aliases={0: 0},
        compiler_params=pltpu.CompilerParams(vmem_limit_bytes=1 * MIB),
        cost_estimate=pl.CostEstimate(flops=0, bytes_accessed=0, transcendentals=0),
        name="gate",
    )(x, after)


def gather_rows(own):
    def route(first):
        pairs = []
        for chip in range(4):
            for core in range(2):
                axis = 1 if (core == 0) == first else 2
                pairs.append((chip * 2 + core, (chip ^ axis) * 2 + core))
        return pairs

    near = lax.ppermute(own, ("ctx", "tp"), route(True))
    far = lax.ppermute(near, ("ctx", "tp"), route(False))
    own = gate(own, near)
    side = lax.ppermute(own, ("ctx", "tp"), route(False))
    return own, near, side, far


def local(queries, key_rows, value_rows, doc_lengths, unit_source, w_out):
    if lax.axis_size("ctx") != 4 or lax.axis_size("tp") != 2 or key_rows.shape[1] != 4 * HD:
        return general(queries, key_rows, value_rows, doc_lengths, unit_source, w_out)
    w_out = in_hbm(w_out)
    kv_heads = key_rows.shape[1] // HD
    width = queries.shape[1] // kv_heads
    two = [(0, 2), (1, 3)]
    value_two = lax.ppermute(value_rows, "ctx", two)
    key_two = lax.ppermute(key_rows, "ctx", two)
    key_near = lax.ppermute(key_rows, "ctx", [(0, 1), (1, 2), (2, 3)])
    value_near = lax.ppermute(value_rows, "ctx", [(0, 1), (2, 3)])
    own_keys, own_values, held, mask, left, right = prepare(
        doc_lengths, key_rows, value_rows, queries, w_out, kv_heads
    )
    value_two = gate(value_two, mask)
    value_far = lax.ppermute(value_two, "ctx", [(3, 2)])
    keys = (own_keys, key_near, key_near, key_two)
    values = (own_values, value_near, value_far, value_two)
    half_columns = w_out.shape[1] // HALVES
    state = {"left": {0: left}, "right": {0: right}, "totals": [None] * HALVES, "before": None}
    rows, mine, got = {}, [], []

    def rows_of(groups, after):
        own = attend(groups, width, held, mask, keys, values, after)
        pieces = gather_rows(own)
        for i, g in enumerate(groups):
            rows[g] = (pieces, i * width)
        return own

    def load(wanted, after):
        loaded, token = load_blocks([g * HALVES for g in wanted], w_out, kv_heads, after)
        state["left"].update(zip(wanted, loaded))
        return token

    def steps(g):
        last = g == kv_heads - 1
        pieces, column = rows[g]
        loads = g not in state["right"]
        first, lhs, following, state["before"] = step(
            g * HALVES, last, (unit_source, pieces), column, state["left"][g], 0, half_columns,
            w_out if loads else None, state["totals"][0], state["before"],
        )
        if loads:
            state["right"][g] = following
        second, _, _, state["before"] = step(
            g * HALVES + 1, last, lhs, column, state["right"][g], 0, half_columns, None,
            state["totals"][1], state["before"],
        )
        if last:
            for kept, sent in (first, second):
                mine.append(kept)
                got.append(lax.ppermute(sent, "tp", [(0, 1), (1, 0)]))
        else:
            state["totals"] = [first[0], second[0]]
        return state["before"]

    own = rows_of((0,), [])
    own = rows_of((1,), [load((1,), own)])
    own = rows_of((2,), [load((2, 3), own), rows[0][0][1]])
    done = steps(0)
    rows_of((3,), [own, done])
    for g in range(1, kv_heads):
        steps(g)
    out = total(0, w_out.shape[1], mine[:1], got[:1], None)
    return total(half_columns, w_out.shape[1], mine[1:], got[1:], out)


def solution(mesh):
    return jax.shard_map(
        local,
        mesh=mesh,
        in_specs=(
            P(("dp", "ctx"), "tp"),
            P(("dp", "ctx"), "tp"),
            P(("dp", "ctx"), "tp"),
            P("dp"),
            P("dp"),
            P("tp", "ctx"),
        ),
        out_specs=P(("dp", "tp"), "ctx"),
        check_vma=False,
    )
```

```python
import functools
import math

import jax
import jax.numpy as jnp
from jax import lax
from jax.experimental import pallas as pl
from jax.experimental.pallas import tpu as pltpu
from jax.sharding import PartitionSpec as P

HD = 128
MIB = 1 << 20
HALVES = 2


def doc_index(positions, doc_ends):
    return jnp.sum((positions[None, :] >= doc_ends[:, None]).astype(jnp.int32), axis=0)


def general(queries, key_rows, value_rows, doc_lengths, unit_source, w_out):
    ctx_count = lax.axis_size("ctx")
    ctx_index = lax.axis_index("ctx")
    tok_dev, columns = queries.shape
    unit_rows = tok_dev // ctx_count
    head_count = columns // HD
    kv_heads = key_rows.shape[1] // HD
    group_size = head_count // kv_heads
    unit_plan = unit_source.reshape(ctx_count, ctx_count)
    positions = ctx_index * tok_dev + jnp.arange(tok_dev, dtype=jnp.int32)
    doc_ends = jnp.cumsum(doc_lengths)
    query_doc = doc_index(positions, doc_ends)
    grouped = queries.reshape(tok_dev, kv_heads, group_size, HD)
    key_all = lax.all_gather(key_rows, "ctx", axis=0, tiled=True)
    value_all = lax.all_gather(value_rows, "ctx", axis=0, tiled=True)
    extent = key_all.shape[0]
    key_pos = jnp.arange(extent, dtype=jnp.int32)
    key_doc = doc_index(key_pos, doc_ends)
    visible = (key_doc[None, :] == query_doc[:, None]) & (key_pos[None, :] <= positions[:, None])
    scores = jnp.einsum(
        "qkgd,pkd->kgqp",
        grouped,
        key_all.reshape(extent, kv_heads, HD),
        preferred_element_type=jnp.float32,
    ) * (HD ** -0.5)
    scores = jnp.where(visible, scores, -jnp.inf)
    row_max = jnp.max(scores, axis=3, keepdims=True)
    weights = jnp.where(visible, jnp.exp(scores - row_max), 0.0)
    totals = jnp.sum(weights, axis=3)
    blended = jnp.einsum(
        "kgqp,pkd->kgqd",
        weights.astype(jnp.bfloat16),
        value_all.reshape(extent, kv_heads, HD),
        preferred_element_type=jnp.float32,
    )
    attended = (
        (blended / totals[..., None])
        .transpose(2, 0, 1, 3)
        .reshape(tok_dev, columns)
        .astype(jnp.bfloat16)
    )
    gathered = lax.all_gather(attended, "ctx", axis=0, tiled=True)
    units = gathered.reshape(ctx_count * ctx_count, unit_rows, columns)
    balanced = jnp.take(units, unit_plan.reshape(-1), axis=0).reshape(extent, columns)
    partial_value = jnp.dot(balanced, w_out, preferred_element_type=jnp.float32)
    return lax.psum_scatter(
        partial_value.astype(jnp.bfloat16), "tp", scatter_dimension=0, tiled=True
    )


SMEM = pl.BlockSpec(memory_space=pltpu.SMEM)
VMEM = pl.BlockSpec(memory_space=pltpu.VMEM)
HBM = pl.BlockSpec(memory_space=pl.ANY)
TILE = 512


def in_hbm(x):
    return pltpu.with_memory_space_constraint(x, pltpu.HBM)


TOKEN = jax.ShapeDtypeStruct((8, 128), jnp.float32)


def block_shape(w_out, chunks):
    return w_out.shape[0] // chunks, w_out.shape[1] // HALVES


def block_copy(w_hbm, index, w_ref, sem):
    depth, columns = w_ref.shape
    row, column = index // HALVES * depth, index % HALVES * columns
    return pltpu.make_async_copy(
        w_hbm.at[row:row + depth, column:column + columns], w_ref, sem
    )


def prepare_kernel(docs_hbm, k_hbm, v_hbm, q_hbm, w_hbm, after, k_ref, v_ref, q_ref, mask_ref, w_ref, docs, sems):
    lengths = pltpu.make_async_copy(docs_hbm, docs, sems.at[0])
    loads = [
        pltpu.make_async_copy(k_hbm, k_ref, sems.at[1]),
        pltpu.make_async_copy(v_hbm, v_ref, sems.at[2]),
        pltpu.make_async_copy(q_hbm, q_ref, sems.at[3]),
        block_copy(w_hbm, 0, w_ref, sems.at[4]),
    ]
    lengths.start()
    for load in loads:
        load.start()
    lengths.wait()
    rows, window = mask_ref.shape
    base = lax.axis_index("ctx") * rows
    pos = base + lax.broadcasted_iota(jnp.int32, (rows, window), 0)
    start = jnp.zeros((rows, window), jnp.int32)
    end = jnp.int32(0)
    for d in range(docs.shape[0]):
        end = end + docs[d]
        start = jnp.where(pos >= end, end, start)
    key_pos = base + rows - window + lax.broadcasted_iota(jnp.int32, (rows, window), 1)
    mask_ref[...] = jnp.where((key_pos >= start) & (key_pos <= pos), 0.0, -jnp.inf)
    for load in loads:
        load.wait()


def prepare(doc_lengths, key_rows, value_rows, queries, w_out, chunks, after):
    rows = queries.shape[0]
    return pl.pallas_call(
        prepare_kernel,
        out_shape=[
            jax.ShapeDtypeStruct(key_rows.shape, jnp.bfloat16),
            jax.ShapeDtypeStruct(value_rows.shape, jnp.bfloat16),
            jax.ShapeDtypeStruct(queries.shape, jnp.bfloat16),
            jax.ShapeDtypeStruct((rows, 3 * rows), jnp.float32),
            jax.ShapeDtypeStruct(block_shape(w_out, chunks), jnp.bfloat16),
        ],
        in_specs=[HBM] * 6,
        out_specs=[VMEM] * 5,
        scratch_shapes=[
            pltpu.SMEM(doc_lengths.shape, jnp.int32),
            pltpu.SemaphoreType.DMA((5,)),
        ],
        compiler_params=pltpu.CompilerParams(vmem_limit_bytes=4 * MIB),
        cost_estimate=pl.CostEstimate(
            flops=0, bytes_accessed=w_out.size // chunks, transcendentals=0
        ),
        name="prepare",
    )(
        in_hbm(doc_lengths), in_hbm(key_rows), in_hbm(value_rows), in_hbm(queries), w_out, after
    )


def load_kernel(indexes, after, w_hbm, *refs):
    *w_refs, token, sems = refs
    loads = [
        block_copy(w_hbm, index, w_ref, sems.at[i])
        for i, (index, w_ref) in enumerate(zip(indexes, w_refs))
    ]
    for load in loads:
        load.start()
    token[...] = jnp.zeros_like(token)
    for load in loads:
        load.wait()


def load_blocks(indexes, w_out, chunks, after):
    shape = block_shape(w_out, chunks)
    *blocks, token = pl.pallas_call(
        functools.partial(load_kernel, indexes),
        out_shape=[jax.ShapeDtypeStruct(shape, jnp.bfloat16)] * len(indexes) + [TOKEN],
        in_specs=[HBM, HBM],
        out_specs=[VMEM] * (len(indexes) + 1),
        scratch_shapes=[pltpu.SemaphoreType.DMA((len(indexes),))],
        compiler_params=pltpu.CompilerParams(vmem_limit_bytes=1 * MIB),
        cost_estimate=pl.CostEstimate(
            flops=0, bytes_accessed=4 * len(indexes) * shape[0] * shape[1], transcendentals=0
        ),
        name=f"load_{indexes[0]}",
    )(after, w_out)
    return blocks, token


def attend_kernel(groups, q_ref, mask_ref, k0, k2, k_near, k_far, v0, v_near, v_far, v2, *rest):
    out_ref = rest[-1]
    rows = out_ref.shape[0]
    width = out_ref.shape[1] // len(groups)
    heads = width // HD
    window = 3 * rows
    factor = HD ** -0.5 * math.log2(math.e)
    across = lax.axis_index("ctx") == 2
    for i, g in enumerate(groups):
        at = slice(g * HD, (g + 1) * HD)
        k1 = jnp.where(across, k_far[:, at], k_near[:, at])
        v1 = jnp.where(across, v_far[:, at], v_near[:, at])
        keys = jnp.concatenate([k2[:, at], k1, k0[:, at]], axis=0)
        values = jnp.concatenate([v2[:, at], v1, v0[:, at]], axis=0)
        stacked = jnp.concatenate(
            [q_ref[:, g * width + h * HD:g * width + (h + 1) * HD] for h in range(heads)], axis=0
        )
        scores = lax.dot_general(
            stacked, keys, (((1,), (1,)), ((), ())), preferred_element_type=jnp.float32
        ).reshape(heads, rows, window)
        scores = scores + mask_ref[...][None]
        top = jnp.max(scores, axis=2, keepdims=True)
        weights = jnp.exp2((scores - top) * factor)
        total = jnp.sum(weights, axis=2, keepdims=True)
        mixed = jnp.dot(
            weights.astype(jnp.bfloat16).reshape(heads * rows, window),
            values,
            preferred_element_type=jnp.float32,
        ).reshape(heads, rows, HD)
        result = (mixed / total).astype(jnp.bfloat16)
        for h in range(heads):
            out_ref[:, i * width + h * HD:i * width + (h + 1) * HD] = result[h]


def attend(groups, width, queries, mask, keys, values, after):
    rows = queries.shape[0]
    return pl.pallas_call(
        functools.partial(attend_kernel, groups),
        out_shape=jax.ShapeDtypeStruct((rows, len(groups) * width), jnp.bfloat16),
        in_specs=[VMEM] * 10 + [HBM] * len(after),
        out_specs=VMEM,
        compiler_params=pltpu.CompilerParams(vmem_limit_bytes=8 * MIB),
        cost_estimate=pl.CostEstimate(flops=0, bytes_accessed=0, transcendentals=0),
        name=f"attend_{groups[0]}",
    )(queries, mask, *keys, *values, *after)


def lay_out(plan, pieces, column, lhs):
    here = lax.axis_index("ctx")
    core = lax.axis_index("tp")
    first = jnp.where(core == 0, 1, 2)
    owners = [here, here ^ first, here ^ (3 - first), here ^ 3]
    unit_rows = lhs.shape[0] // 16
    swap = jnp.where(core == 0, 8, 0)
    wanted = [plan[slot] for slot in range(16)]
    for owner, piece in zip(owners, pieces):
        for u in range(4):
            slot = jnp.int32(0)
            for s in range(1, 16):
                slot = jnp.where(wanted[s] == owner * 4 + u, s, slot)
            slot = slot ^ swap
            at = pl.ds(pl.multiple_of(slot * unit_rows, unit_rows), unit_rows)
            lhs[at, :] = piece[u * unit_rows:(u + 1) * unit_rows, column:column + lhs.shape[1]]


def step_kernel(index, last, column, first, columns, has_acc, has_after, has_load, *refs):
    refs = list(refs)[has_after:]
    first_half = index % HALVES == 0
    load = None
    if has_load:
        sem = refs.pop()
    token = refs.pop()
    if has_load:
        load = block_copy(refs.pop(0), index + 1, refs.pop(), sem)
        load.start()
    if first_half:
        plan, *pieces = refs[:5]
        del refs[:5]
        lhs = refs.pop()
        lay_out(plan, pieces, column, lhs)
    else:
        lhs = refs.pop(0)
    token[...] = jnp.zeros_like(token)
    w_ref = refs.pop(0)
    acc_ref = refs.pop(0) if has_acc else None
    rows = lhs.shape[0] // 2
    for start in range(0, columns, TILE):
        to = slice(start, start + TILE)
        at = slice(first + start, first + start + TILE)
        product = jnp.dot(lhs[...], w_ref[:, at], preferred_element_type=jnp.float32)
        if has_acc:
            product = product + acc_ref[:, at]
        if last:
            own_ref, sent_ref = refs
            own_ref[:, to] = product[rows:]
            sent_ref[:, to] = product[:rows].astype(jnp.bfloat16)
        else:
            refs[0][:, to] = product
    if load is not None:
        load.wait()


def step(index, last, rows_in, column, block, first, columns, w_out, acc, after):
    first_half = index % HALVES == 0
    has_acc, has_after, has_load = acc is not None, after is not None, w_out is not None
    depth = block.shape[0]
    if first_half:
        plan, pieces = rows_in
        total_rows = 4 * pieces[0].shape[0]
        operands, specs = [plan, *pieces], [SMEM] + [VMEM] * 4
    else:
        total_rows = rows_in.shape[0]
        operands, specs = [rows_in], [VMEM]
    if last:
        part = (total_rows // 2, columns)
        shapes = [jax.ShapeDtypeStruct(part, jnp.float32), jax.ShapeDtypeStruct(part, jnp.bfloat16)]
    else:
        shapes = [jax.ShapeDtypeStruct((total_rows, columns), jnp.float32)]
    if first_half:
        shapes.append(jax.ShapeDtypeStruct((total_rows, depth), jnp.bfloat16))
    if has_load:
        shapes.append(jax.ShapeDtypeStruct(block.shape, jnp.bfloat16))
    shapes.append(TOKEN)
    operands = [after] * has_after + [w_out] * has_load + operands + [block] + [acc] * has_acc
    specs = [HBM] * (has_after + has_load) + specs + [VMEM] * (1 + has_acc)
    results = list(pl.pallas_call(
        functools.partial(
            step_kernel, index, last, column, first, columns, has_acc, has_after, has_load
        ),
        out_shape=shapes,
        in_specs=specs,
        out_specs=[VMEM] * len(shapes),
        scratch_shapes=[pltpu.SemaphoreType.DMA] * has_load,
        input_output_aliases={len(operands) - 1: 0} if has_acc and not last else {},
        compiler_params=pltpu.CompilerParams(vmem_limit_bytes=6 * MIB),
        cost_estimate=pl.CostEstimate(
            flops=2 * total_rows * depth * columns, bytes_accessed=0, transcendentals=0
        ),
        name=f"step_{index}_{first // columns}",
    )(*operands))
    token = results.pop()
    following = results.pop() if has_load else None
    lhs = results.pop() if first_half else rows_in
    return results, lhs, following, token


def total_kernel(first, count, has_out, *refs):
    own_refs, got_refs = refs[:count], refs[count:2 * count]
    out_hbm, buf, sems = refs[2 * count + has_out:]
    writes, at = [], 0
    for own_ref, got_ref in zip(own_refs, got_refs):
        columns = own_ref.shape[1]
        for start in range(0, columns, 2 * TILE):
            to = slice(start, start + 2 * TILE)
            value = own_ref[:, to] + got_ref[:, to].astype(jnp.float32)
            here = slice(at + start, at + start + 2 * TILE)
            there = slice(first + at + start, first + at + start + 2 * TILE)
            buf[:, here] = value.astype(jnp.bfloat16)
            write = pltpu.make_async_copy(buf.at[:, here], out_hbm.at[:, there], sems.at[len(writes)])
            write.start()
            writes.append(write)
        at += columns
    for write in writes:
        write.wait()


def total(first, width, own, got, out):
    rows = own[0].shape[0]
    columns = sum(x.shape[1] for x in own)
    count, has_out = len(own), out is not None
    return pl.pallas_call(
        functools.partial(total_kernel, first, count, has_out),
        out_shape=jax.ShapeDtypeStruct((rows, width), jnp.bfloat16),
        in_specs=[VMEM] * (2 * count) + [HBM] * has_out,
        out_specs=HBM,
        scratch_shapes=[
            pltpu.VMEM((rows, columns), jnp.bfloat16),
            pltpu.SemaphoreType.DMA((columns // (2 * TILE),)),
        ],
        input_output_aliases={2 * count: 0} if has_out else {},
        compiler_params=pltpu.CompilerParams(vmem_limit_bytes=4 * MIB),
        cost_estimate=pl.CostEstimate(
            flops=rows * columns, bytes_accessed=2 * rows * columns, transcendentals=0
        ),
        name=f"total_{first}",
    )(*own, *got, *([out] if has_out else []))


def gate_kernel(x, after, out):
    pass


def gate(x, after):
    return pl.pallas_call(
        gate_kernel,
        out_shape=jax.ShapeDtypeStruct(x.shape, x.dtype),
        in_specs=[HBM, HBM],
        out_specs=HBM,
        input_output_aliases={0: 0},
        compiler_params=pltpu.CompilerParams(vmem_limit_bytes=1 * MIB),
        cost_estimate=pl.CostEstimate(flops=0, bytes_accessed=0, transcendentals=0),
        name="gate",
    )(x, after)


def gather_rows(own):
    def route(first):
        pairs = []
        for chip in range(4):
            for core in range(2):
                axis = 1 if (core == 0) == first else 2
                pairs.append((chip * 2 + core, (chip ^ axis) * 2 + core))
        return pairs

    near = lax.ppermute(own, ("ctx", "tp"), route(True))
    side = lax.ppermute(own, ("ctx", "tp"), route(False))

    def forward(after):
        first = near if after is None else gate(near, after)
        return own, first, side, lax.ppermute(first, ("ctx", "tp"), route(False))

    return near, side, forward


def local(queries, key_rows, value_rows, doc_lengths, unit_source, w_out):
    if lax.axis_size("ctx") != 4 or lax.axis_size("tp") != 2 or key_rows.shape[1] != 4 * HD:
        return general(queries, key_rows, value_rows, doc_lengths, unit_source, w_out)
    w_out = in_hbm(w_out)
    kv_heads = key_rows.shape[1] // HD
    width = queries.shape[1] // kv_heads
    two = [(0, 2), (1, 3)]
    value_two = lax.ppermute(value_rows, "ctx", two)
    key_two = lax.ppermute(key_rows, "ctx", two)
    key_near = lax.ppermute(key_rows, "ctx", [(0, 1), (1, 2), (2, 3)])
    value_near = lax.ppermute(value_rows, "ctx", [(0, 1), (2, 3)])
    value_far = lax.ppermute(value_two, "ctx", [(3, 2)])
    own_keys, own_values, held, mask, block = prepare(
        doc_lengths, key_rows, value_rows, queries, w_out, kv_heads, value_two
    )
    keys = (own_keys, key_two, key_near, key_near)
    values = (own_values, value_near, value_far, value_two)
    half_columns = w_out.shape[1] // HALVES
    state = {"blocks": {0: block}, "totals": [None] * HALVES, "before": None}
    rows, mine, got = {}, [], []

    def rows_of(groups, after):
        own = attend(groups, width, held, mask, keys, values, after)
        near, side, forward = gather_rows(own)

        def arrive(after):
            pieces = forward(after)
            for i, g in enumerate(groups):
                rows[g] = (pieces, i * width)
            return pieces[1]

        return own, arrive

    def load(wanted, after):
        loaded, token = load_blocks(wanted, w_out, kv_heads, after)
        state["blocks"].update(zip(wanted, loaded))
        return token

    def steps(g):
        last = g == kv_heads - 1
        pieces, column = rows[g]
        loads = g * HALVES + 1 not in state["blocks"]
        first, lhs, following, state["before"] = step(
            g * HALVES, last, (unit_source, pieces), column, state["blocks"][g * HALVES], 0,
            half_columns,
            w_out if loads else None, state["totals"][0], state["before"],
        )
        if loads:
            state["blocks"][g * HALVES + 1] = following
        second, _, _, state["before"] = step(
            g * HALVES + 1, last, lhs, column, state["blocks"][g * HALVES + 1], 0,
            half_columns, None,
            state["totals"][1], state["before"],
        )
        if last:
            for kept, sent in (first, second):
                mine.append(kept)
                got.append(lax.ppermute(sent, "tp", [(0, 1), (1, 0)]))
        else:
            state["totals"] = [first[0], second[0]]
        return state["before"]

    own, arrive = rows_of((0,), [])
    near = arrive(None)
    own, arrive = rows_of((1,), [load((1, 2), own)])
    arrive(None)
    own, arrive = rows_of((2, 3), [load((4, 6), own), near])
    arrive(steps(0))
    for g in range(1, kv_heads):
        steps(g)
    out = total(0, w_out.shape[1], mine[:1], got[:1], None)
    return total(half_columns, w_out.shape[1], mine[1:], got[1:], out)


def solution(mesh):
    return jax.shard_map(
        local,
        mesh=mesh,
        in_specs=(
            P(("dp", "ctx"), "tp"),
            P(("dp", "ctx"), "tp"),
            P(("dp", "ctx"), "tp"),
            P("dp"),
            P("dp"),
            P("tp", "ctx"),
        ),
        out_specs=P(("dp", "tp"), "ctx"),
        check_vma=False,
    )
```

```python
import functools
import math

import jax
import jax.numpy as jnp
from jax import lax
from jax.experimental import pallas as pl
from jax.experimental.pallas import tpu as pltpu
from jax.sharding import PartitionSpec as P

HD = 128
MIB = 1 << 20
HALVES = 2


def doc_index(positions, doc_ends):
    return jnp.sum((positions[None, :] >= doc_ends[:, None]).astype(jnp.int32), axis=0)


def general(queries, key_rows, value_rows, doc_lengths, unit_source, w_out):
    ctx_count = lax.axis_size("ctx")
    ctx_index = lax.axis_index("ctx")
    tok_dev, columns = queries.shape
    unit_rows = tok_dev // ctx_count
    head_count = columns // HD
    kv_heads = key_rows.shape[1] // HD
    group_size = head_count // kv_heads
    unit_plan = unit_source.reshape(ctx_count, ctx_count)
    positions = ctx_index * tok_dev + jnp.arange(tok_dev, dtype=jnp.int32)
    doc_ends = jnp.cumsum(doc_lengths)
    query_doc = doc_index(positions, doc_ends)
    grouped = queries.reshape(tok_dev, kv_heads, group_size, HD)
    key_all = lax.all_gather(key_rows, "ctx", axis=0, tiled=True)
    value_all = lax.all_gather(value_rows, "ctx", axis=0, tiled=True)
    extent = key_all.shape[0]
    key_pos = jnp.arange(extent, dtype=jnp.int32)
    key_doc = doc_index(key_pos, doc_ends)
    visible = (key_doc[None, :] == query_doc[:, None]) & (key_pos[None, :] <= positions[:, None])
    scores = jnp.einsum(
        "qkgd,pkd->kgqp",
        grouped,
        key_all.reshape(extent, kv_heads, HD),
        preferred_element_type=jnp.float32,
    ) * (HD ** -0.5)
    scores = jnp.where(visible, scores, -jnp.inf)
    row_max = jnp.max(scores, axis=3, keepdims=True)
    weights = jnp.where(visible, jnp.exp(scores - row_max), 0.0)
    totals = jnp.sum(weights, axis=3)
    blended = jnp.einsum(
        "kgqp,pkd->kgqd",
        weights.astype(jnp.bfloat16),
        value_all.reshape(extent, kv_heads, HD),
        preferred_element_type=jnp.float32,
    )
    attended = (
        (blended / totals[..., None])
        .transpose(2, 0, 1, 3)
        .reshape(tok_dev, columns)
        .astype(jnp.bfloat16)
    )
    gathered = lax.all_gather(attended, "ctx", axis=0, tiled=True)
    units = gathered.reshape(ctx_count * ctx_count, unit_rows, columns)
    balanced = jnp.take(units, unit_plan.reshape(-1), axis=0).reshape(extent, columns)
    partial_value = jnp.dot(balanced, w_out, preferred_element_type=jnp.float32)
    return lax.psum_scatter(
        partial_value.astype(jnp.bfloat16), "tp", scatter_dimension=0, tiled=True
    )


SMEM = pl.BlockSpec(memory_space=pltpu.SMEM)
VMEM = pl.BlockSpec(memory_space=pltpu.VMEM)
HBM = pl.BlockSpec(memory_space=pl.ANY)
TILE = 512


def in_hbm(x):
    return pltpu.with_memory_space_constraint(x, pltpu.HBM)


TOKEN = jax.ShapeDtypeStruct((8, 128), jnp.float32)


def block_shape(w_out, chunks):
    return w_out.shape[0] // chunks, w_out.shape[1] // HALVES


def block_copy(w_hbm, index, w_ref, sem):
    depth, columns = w_ref.shape
    row, column = index // HALVES * depth, index % HALVES * columns
    return pltpu.make_async_copy(
        w_hbm.at[row:row + depth, column:column + columns], w_ref, sem
    )


def prepare_kernel(docs_hbm, k_hbm, v_hbm, q_hbm, w_hbm, after, k_ref, v_ref, q_ref, mask_ref, w_ref, docs, sems):
    lengths = pltpu.make_async_copy(docs_hbm, docs, sems.at[0])
    loads = [
        pltpu.make_async_copy(k_hbm, k_ref, sems.at[1]),
        pltpu.make_async_copy(v_hbm, v_ref, sems.at[2]),
        pltpu.make_async_copy(q_hbm, q_ref, sems.at[3]),
        block_copy(w_hbm, 0, w_ref, sems.at[4]),
    ]
    lengths.start()
    for load in loads:
        load.start()
    lengths.wait()
    rows, window = mask_ref.shape
    base = lax.axis_index("ctx") * rows
    pos = base + lax.broadcasted_iota(jnp.int32, (rows, window), 0)
    start = jnp.zeros((rows, window), jnp.int32)
    end = jnp.int32(0)
    for d in range(docs.shape[0]):
        end = end + docs[d]
        start = jnp.where(pos >= end, end, start)
    key_pos = base + rows - window + lax.broadcasted_iota(jnp.int32, (rows, window), 1)
    mask_ref[...] = jnp.where((key_pos >= start) & (key_pos <= pos), 0.0, -jnp.inf)
    for load in loads:
        load.wait()


def prepare(doc_lengths, key_rows, value_rows, queries, w_out, chunks, after):
    rows = queries.shape[0]
    return pl.pallas_call(
        prepare_kernel,
        out_shape=[
            jax.ShapeDtypeStruct(key_rows.shape, jnp.bfloat16),
            jax.ShapeDtypeStruct(value_rows.shape, jnp.bfloat16),
            jax.ShapeDtypeStruct(queries.shape, jnp.bfloat16),
            jax.ShapeDtypeStruct((rows, 3 * rows), jnp.float32),
            jax.ShapeDtypeStruct(block_shape(w_out, chunks), jnp.bfloat16),
        ],
        in_specs=[HBM] * 6,
        out_specs=[VMEM] * 5,
        scratch_shapes=[
            pltpu.SMEM(doc_lengths.shape, jnp.int32),
            pltpu.SemaphoreType.DMA((5,)),
        ],
        compiler_params=pltpu.CompilerParams(vmem_limit_bytes=4 * MIB),
        cost_estimate=pl.CostEstimate(
            flops=0, bytes_accessed=w_out.size // chunks, transcendentals=0
        ),
        name="prepare",
    )(
        in_hbm(doc_lengths), in_hbm(key_rows), in_hbm(value_rows), in_hbm(queries), w_out, after
    )


def load_kernel(indexes, after, w_hbm, *refs):
    *w_refs, token, sems = refs
    loads = [
        block_copy(w_hbm, index, w_ref, sems.at[i])
        for i, (index, w_ref) in enumerate(zip(indexes, w_refs))
    ]
    for load in loads:
        load.start()
    token[...] = jnp.zeros_like(token)
    for load in loads:
        load.wait()


def load_blocks(indexes, w_out, chunks, after):
    shape = block_shape(w_out, chunks)
    *blocks, token = pl.pallas_call(
        functools.partial(load_kernel, indexes),
        out_shape=[jax.ShapeDtypeStruct(shape, jnp.bfloat16)] * len(indexes) + [TOKEN],
        in_specs=[HBM, HBM],
        out_specs=[VMEM] * (len(indexes) + 1),
        scratch_shapes=[pltpu.SemaphoreType.DMA((len(indexes),))],
        compiler_params=pltpu.CompilerParams(vmem_limit_bytes=1 * MIB),
        cost_estimate=pl.CostEstimate(
            flops=0, bytes_accessed=4 * len(indexes) * shape[0] * shape[1], transcendentals=0
        ),
        name=f"load_{indexes[0]}",
    )(after, w_out)
    return blocks, token


def attend_kernel(groups, q_ref, mask_ref, k0, k2, k_near, k_far, v0, v_near, v_far, v2, *rest):
    out_ref = rest[-1]
    rows = out_ref.shape[0]
    width = out_ref.shape[1] // len(groups)
    heads = width // HD
    window = 3 * rows
    factor = HD ** -0.5 * math.log2(math.e)
    across = lax.axis_index("ctx") == 2
    for i, g in enumerate(groups):
        at = slice(g * HD, (g + 1) * HD)
        k1 = jnp.where(across, k_far[:, at], k_near[:, at])
        v1 = jnp.where(across, v_far[:, at], v_near[:, at])
        keys = jnp.concatenate([k2[:, at], k1, k0[:, at]], axis=0)
        values = jnp.concatenate([v2[:, at], v1, v0[:, at]], axis=0)
        stacked = jnp.concatenate(
            [q_ref[:, g * width + h * HD:g * width + (h + 1) * HD] for h in range(heads)], axis=0
        )
        scores = lax.dot_general(
            stacked, keys, (((1,), (1,)), ((), ())), preferred_element_type=jnp.float32
        ).reshape(heads, rows, window)
        scores = scores + mask_ref[...][None]
        top = jnp.max(scores, axis=2, keepdims=True)
        weights = jnp.exp2((scores - top) * factor)
        total = jnp.sum(weights, axis=2, keepdims=True)
        mixed = jnp.dot(
            weights.astype(jnp.bfloat16).reshape(heads * rows, window),
            values,
            preferred_element_type=jnp.float32,
        ).reshape(heads, rows, HD)
        result = (mixed / total).astype(jnp.bfloat16)
        for h in range(heads):
            out_ref[:, i * width + h * HD:i * width + (h + 1) * HD] = result[h]


def attend(groups, width, queries, mask, keys, values, after):
    rows = queries.shape[0]
    return pl.pallas_call(
        functools.partial(attend_kernel, groups),
        out_shape=jax.ShapeDtypeStruct((rows, len(groups) * width), jnp.bfloat16),
        in_specs=[VMEM] * 10 + [HBM] * len(after),
        out_specs=VMEM,
        compiler_params=pltpu.CompilerParams(vmem_limit_bytes=8 * MIB),
        cost_estimate=pl.CostEstimate(flops=0, bytes_accessed=0, transcendentals=0),
        name=f"attend_{groups[0]}",
    )(queries, mask, *keys, *values, *after)


def lay_out(plan, pieces, column, lhs):
    here = lax.axis_index("ctx")
    core = lax.axis_index("tp")
    first = jnp.where(core == 0, 1, 2)
    owners = [here, here ^ first, here ^ (3 - first), here ^ 3]
    unit_rows = lhs.shape[0] // 16
    swap = jnp.where(core == 0, 8, 0)
    wanted = [plan[slot] for slot in range(16)]
    for owner, piece in zip(owners, pieces):
        for u in range(4):
            slot = jnp.int32(0)
            for s in range(1, 16):
                slot = jnp.where(wanted[s] == owner * 4 + u, s, slot)
            slot = slot ^ swap
            at = pl.ds(pl.multiple_of(slot * unit_rows, unit_rows), unit_rows)
            lhs[at, :] = piece[u * unit_rows:(u + 1) * unit_rows, column:column + lhs.shape[1]]


def step_kernel(index, last, column, first, columns, has_acc, has_after, has_load, *refs):
    refs = list(refs)[has_after:]
    first_half = index % HALVES == 0
    load = None
    if has_load:
        sem = refs.pop()
    token = refs.pop()
    if has_load:
        load = block_copy(refs.pop(0), index + 1, refs.pop(), sem)
        load.start()
    if first_half:
        plan, *pieces = refs[:5]
        del refs[:5]
        lhs = refs.pop()
        lay_out(plan, pieces, column, lhs)
    else:
        lhs = refs.pop(0)
    token[...] = jnp.zeros_like(token)
    w_ref = refs.pop(0)
    acc_ref = refs.pop(0) if has_acc else None
    rows = lhs.shape[0] // 2
    for start in range(0, columns, TILE):
        to = slice(start, start + TILE)
        at = slice(first + start, first + start + TILE)
        product = jnp.dot(lhs[...], w_ref[:, at], preferred_element_type=jnp.float32)
        if has_acc:
            product = product + acc_ref[:, at]
        if last:
            own_ref, sent_ref = refs
            own_ref[:, to] = product[rows:]
            sent_ref[:, to] = product[:rows].astype(jnp.bfloat16)
        else:
            refs[0][:, to] = product
    if load is not None:
        load.wait()


def step(index, last, rows_in, column, block, first, columns, w_out, acc, after):
    first_half = index % HALVES == 0
    has_acc, has_after, has_load = acc is not None, after is not None, w_out is not None
    depth = block.shape[0]
    if first_half:
        plan, pieces = rows_in
        total_rows = 4 * pieces[0].shape[0]
        operands, specs = [plan, *pieces], [SMEM] + [VMEM] * 4
    else:
        total_rows = rows_in.shape[0]
        operands, specs = [rows_in], [VMEM]
    if last:
        part = (total_rows // 2, columns)
        shapes = [jax.ShapeDtypeStruct(part, jnp.float32), jax.ShapeDtypeStruct(part, jnp.bfloat16)]
    else:
        shapes = [jax.ShapeDtypeStruct((total_rows, columns), jnp.float32)]
    if first_half:
        shapes.append(jax.ShapeDtypeStruct((total_rows, depth), jnp.bfloat16))
    if has_load:
        shapes.append(jax.ShapeDtypeStruct(block.shape, jnp.bfloat16))
    shapes.append(TOKEN)
    operands = [after] * has_after + [w_out] * has_load + operands + [block] + [acc] * has_acc
    specs = [HBM] * (has_after + has_load) + specs + [VMEM] * (1 + has_acc)
    results = list(pl.pallas_call(
        functools.partial(
            step_kernel, index, last, column, first, columns, has_acc, has_after, has_load
        ),
        out_shape=shapes,
        in_specs=specs,
        out_specs=[VMEM] * len(shapes),
        scratch_shapes=[pltpu.SemaphoreType.DMA] * has_load,
        input_output_aliases={len(operands) - 1: 0} if has_acc and not last else {},
        compiler_params=pltpu.CompilerParams(vmem_limit_bytes=6 * MIB),
        cost_estimate=pl.CostEstimate(
            flops=2 * total_rows * depth * columns, bytes_accessed=0, transcendentals=0
        ),
        name=f"step_{index}_{first // columns}",
    )(*operands))
    token = results.pop()
    following = results.pop() if has_load else None
    lhs = results.pop() if first_half else rows_in
    return results, lhs, following, token


def total_kernel(first, count, has_out, *refs):
    own_refs, got_refs = refs[:count], refs[count:2 * count]
    out_hbm, buf, sems = refs[2 * count + has_out:]
    writes, at = [], 0
    for own_ref, got_ref in zip(own_refs, got_refs):
        columns = own_ref.shape[1]
        for start in range(0, columns, 2 * TILE):
            to = slice(start, start + 2 * TILE)
            value = own_ref[:, to] + got_ref[:, to].astype(jnp.float32)
            here = slice(at + start, at + start + 2 * TILE)
            there = slice(first + at + start, first + at + start + 2 * TILE)
            buf[:, here] = value.astype(jnp.bfloat16)
            write = pltpu.make_async_copy(buf.at[:, here], out_hbm.at[:, there], sems.at[len(writes)])
            write.start()
            writes.append(write)
        at += columns
    for write in writes:
        write.wait()


def total(first, width, own, got, out):
    rows = own[0].shape[0]
    columns = sum(x.shape[1] for x in own)
    count, has_out = len(own), out is not None
    return pl.pallas_call(
        functools.partial(total_kernel, first, count, has_out),
        out_shape=jax.ShapeDtypeStruct((rows, width), jnp.bfloat16),
        in_specs=[VMEM] * (2 * count) + [HBM] * has_out,
        out_specs=HBM,
        scratch_shapes=[
            pltpu.VMEM((rows, columns), jnp.bfloat16),
            pltpu.SemaphoreType.DMA((columns // (2 * TILE),)),
        ],
        input_output_aliases={2 * count: 0} if has_out else {},
        compiler_params=pltpu.CompilerParams(vmem_limit_bytes=4 * MIB),
        cost_estimate=pl.CostEstimate(
            flops=rows * columns, bytes_accessed=2 * rows * columns, transcendentals=0
        ),
        name=f"total_{first}",
    )(*own, *got, *([out] if has_out else []))


def gate_kernel(x, after, out):
    pass


def gate(x, after):
    return pl.pallas_call(
        gate_kernel,
        out_shape=jax.ShapeDtypeStruct(x.shape, x.dtype),
        in_specs=[HBM, HBM],
        out_specs=HBM,
        input_output_aliases={0: 0},
        compiler_params=pltpu.CompilerParams(vmem_limit_bytes=1 * MIB),
        cost_estimate=pl.CostEstimate(flops=0, bytes_accessed=0, transcendentals=0),
        name="gate",
    )(x, after)


def gather_rows(own):
    def route(first):
        pairs = []
        for chip in range(4):
            for core in range(2):
                axis = 1 if (core == 0) == first else 2
                pairs.append((chip * 2 + core, (chip ^ axis) * 2 + core))
        return pairs

    near = lax.ppermute(own, ("ctx", "tp"), route(True))
    side = lax.ppermute(own, ("ctx", "tp"), route(False))

    def forward(after):
        first = near if after is None else gate(near, after)
        return own, first, side, lax.ppermute(first, ("ctx", "tp"), route(False))

    return near, side, forward


def local(queries, key_rows, value_rows, doc_lengths, unit_source, w_out):
    if lax.axis_size("ctx") != 4 or lax.axis_size("tp") != 2 or key_rows.shape[1] != 4 * HD:
        return general(queries, key_rows, value_rows, doc_lengths, unit_source, w_out)
    w_out = in_hbm(w_out)
    kv_heads = key_rows.shape[1] // HD
    width = queries.shape[1] // kv_heads
    two = [(0, 2), (1, 3)]
    value_two = lax.ppermute(value_rows, "ctx", two)
    key_two = lax.ppermute(key_rows, "ctx", two)
    key_near = lax.ppermute(key_rows, "ctx", [(0, 1), (1, 2), (2, 3)])
    value_near = lax.ppermute(value_rows, "ctx", [(0, 1), (2, 3)])
    value_far = lax.ppermute(value_two, "ctx", [(3, 2)])
    own_keys, own_values, held, mask, block = prepare(
        doc_lengths, key_rows, value_rows, queries, w_out, kv_heads, value_two
    )
    keys = (own_keys, key_two, key_near, key_near)
    values = (own_values, value_near, value_far, value_two)
    half_columns = w_out.shape[1] // HALVES
    state = {"blocks": {0: block}, "totals": [None] * HALVES, "before": None}
    rows, mine, got = {}, [], []

    def rows_of(groups, after):
        own = attend(groups, width, held, mask, keys, values, after)
        near, side, forward = gather_rows(own)

        def arrive(after):
            pieces = forward(after)
            for i, g in enumerate(groups):
                rows[g] = (pieces, i * width)
            return pieces[1]

        return own, arrive

    def load(wanted, after):
        loaded, token = load_blocks(wanted, w_out, kv_heads, after)
        state["blocks"].update(zip(wanted, loaded))
        return token

    def steps(g):
        last = g == kv_heads - 1
        pieces, column = rows[g]
        loads = g * HALVES + 1 not in state["blocks"]
        first, lhs, following, state["before"] = step(
            g * HALVES, last, (unit_source, pieces), column, state["blocks"][g * HALVES], 0,
            half_columns,
            w_out if loads else None, state["totals"][0], state["before"],
        )
        if loads:
            state["blocks"][g * HALVES + 1] = following
        second, _, _, state["before"] = step(
            g * HALVES + 1, last, lhs, column, state["blocks"][g * HALVES + 1], 0,
            half_columns, None,
            state["totals"][1], state["before"],
        )
        if last:
            for kept, sent in (first, second):
                mine.append(kept)
                got.append(lax.ppermute(sent, "tp", [(0, 1), (1, 0)]))
        else:
            state["totals"] = [first[0], second[0]]
        return state["before"]

    own, arrive = rows_of((0,), [])
    near = arrive(None)
    own, arrive = rows_of((1,), [load((1, 2), own)])
    arrive(None)
    own, arrive = rows_of((2,), [load((4, 6), own), near])
    arrive(None)
    own, arrive = rows_of((3,), [own, steps(0)])
    arrive(None)
    for g in range(1, kv_heads):
        steps(g)
    out = total(0, w_out.shape[1], mine[:1], got[:1], None)
    return total(half_columns, w_out.shape[1], mine[1:], got[1:], out)


def solution(mesh):
    return jax.shard_map(
        local,
        mesh=mesh,
        in_specs=(
            P(("dp", "ctx"), "tp"),
            P(("dp", "ctx"), "tp"),
            P(("dp", "ctx"), "tp"),
            P("dp"),
            P("dp"),
            P("tp", "ctx"),
        ),
        out_specs=P(("dp", "tp"), "ctx"),
        check_vma=False,
    )
```

```python
import functools
import math

import jax
import jax.numpy as jnp
from jax import lax
from jax.experimental import pallas as pl
from jax.experimental.pallas import tpu as pltpu
from jax.sharding import PartitionSpec as P

HD = 128
MIB = 1 << 20
HALVES = 2


def doc_index(positions, doc_ends):
    return jnp.sum((positions[None, :] >= doc_ends[:, None]).astype(jnp.int32), axis=0)


def general(queries, key_rows, value_rows, doc_lengths, unit_source, w_out):
    ctx_count = lax.axis_size("ctx")
    ctx_index = lax.axis_index("ctx")
    tok_dev, columns = queries.shape
    unit_rows = tok_dev // ctx_count
    head_count = columns // HD
    kv_heads = key_rows.shape[1] // HD
    group_size = head_count // kv_heads
    unit_plan = unit_source.reshape(ctx_count, ctx_count)
    positions = ctx_index * tok_dev + jnp.arange(tok_dev, dtype=jnp.int32)
    doc_ends = jnp.cumsum(doc_lengths)
    query_doc = doc_index(positions, doc_ends)
    grouped = queries.reshape(tok_dev, kv_heads, group_size, HD)
    key_all = lax.all_gather(key_rows, "ctx", axis=0, tiled=True)
    value_all = lax.all_gather(value_rows, "ctx", axis=0, tiled=True)
    extent = key_all.shape[0]
    key_pos = jnp.arange(extent, dtype=jnp.int32)
    key_doc = doc_index(key_pos, doc_ends)
    visible = (key_doc[None, :] == query_doc[:, None]) & (key_pos[None, :] <= positions[:, None])
    scores = jnp.einsum(
        "qkgd,pkd->kgqp",
        grouped,
        key_all.reshape(extent, kv_heads, HD),
        preferred_element_type=jnp.float32,
    ) * (HD ** -0.5)
    scores = jnp.where(visible, scores, -jnp.inf)
    row_max = jnp.max(scores, axis=3, keepdims=True)
    weights = jnp.where(visible, jnp.exp(scores - row_max), 0.0)
    totals = jnp.sum(weights, axis=3)
    blended = jnp.einsum(
        "kgqp,pkd->kgqd",
        weights.astype(jnp.bfloat16),
        value_all.reshape(extent, kv_heads, HD),
        preferred_element_type=jnp.float32,
    )
    attended = (
        (blended / totals[..., None])
        .transpose(2, 0, 1, 3)
        .reshape(tok_dev, columns)
        .astype(jnp.bfloat16)
    )
    gathered = lax.all_gather(attended, "ctx", axis=0, tiled=True)
    units = gathered.reshape(ctx_count * ctx_count, unit_rows, columns)
    balanced = jnp.take(units, unit_plan.reshape(-1), axis=0).reshape(extent, columns)
    partial_value = jnp.dot(balanced, w_out, preferred_element_type=jnp.float32)
    return lax.psum_scatter(
        partial_value.astype(jnp.bfloat16), "tp", scatter_dimension=0, tiled=True
    )


SMEM = pl.BlockSpec(memory_space=pltpu.SMEM)
VMEM = pl.BlockSpec(memory_space=pltpu.VMEM)
HBM = pl.BlockSpec(memory_space=pl.ANY)
TILE = 512


def in_hbm(x):
    return pltpu.with_memory_space_constraint(x, pltpu.HBM)


TOKEN = jax.ShapeDtypeStruct((8, 128), jnp.float32)


def block_shape(w_out, chunks):
    return w_out.shape[0] // chunks, w_out.shape[1] // HALVES


def block_copy(w_hbm, index, w_ref, sem):
    depth, columns = w_ref.shape
    row, column = index // HALVES * depth, index % HALVES * columns
    return pltpu.make_async_copy(
        w_hbm.at[row:row + depth, column:column + columns], w_ref, sem
    )


def prepare_kernel(docs_hbm, k_hbm, v_hbm, q_hbm, w_hbm, after, k_ref, v_ref, q_ref, mask_ref, w_ref, docs, sems):
    lengths = pltpu.make_async_copy(docs_hbm, docs, sems.at[0])
    loads = [
        pltpu.make_async_copy(k_hbm, k_ref, sems.at[1]),
        pltpu.make_async_copy(v_hbm, v_ref, sems.at[2]),
        pltpu.make_async_copy(q_hbm, q_ref, sems.at[3]),
        block_copy(w_hbm, 0, w_ref, sems.at[4]),
    ]
    lengths.start()
    for load in loads:
        load.start()
    lengths.wait()
    rows, window = mask_ref.shape
    base = lax.axis_index("ctx") * rows
    pos = base + lax.broadcasted_iota(jnp.int32, (rows, window), 0)
    start = jnp.zeros((rows, window), jnp.int32)
    end = jnp.int32(0)
    for d in range(docs.shape[0]):
        end = end + docs[d]
        start = jnp.where(pos >= end, end, start)
    key_pos = base + rows - window + lax.broadcasted_iota(jnp.int32, (rows, window), 1)
    mask_ref[...] = jnp.where((key_pos >= start) & (key_pos <= pos), 0.0, -jnp.inf)
    for load in loads:
        load.wait()


def prepare(doc_lengths, key_rows, value_rows, queries, w_out, chunks, after):
    rows = queries.shape[0]
    return pl.pallas_call(
        prepare_kernel,
        out_shape=[
            jax.ShapeDtypeStruct(key_rows.shape, jnp.bfloat16),
            jax.ShapeDtypeStruct(value_rows.shape, jnp.bfloat16),
            jax.ShapeDtypeStruct(queries.shape, jnp.bfloat16),
            jax.ShapeDtypeStruct((rows, 3 * rows), jnp.float32),
            jax.ShapeDtypeStruct(block_shape(w_out, chunks), jnp.bfloat16),
        ],
        in_specs=[HBM] * 6,
        out_specs=[VMEM] * 5,
        scratch_shapes=[
            pltpu.SMEM(doc_lengths.shape, jnp.int32),
            pltpu.SemaphoreType.DMA((5,)),
        ],
        compiler_params=pltpu.CompilerParams(vmem_limit_bytes=4 * MIB),
        cost_estimate=pl.CostEstimate(
            flops=0, bytes_accessed=w_out.size // chunks, transcendentals=0
        ),
        name="prepare",
    )(
        in_hbm(doc_lengths), in_hbm(key_rows), in_hbm(value_rows), in_hbm(queries), w_out, after
    )


def load_kernel(indexes, after, w_hbm, *refs):
    *w_refs, token, sems = refs
    loads = [
        block_copy(w_hbm, index, w_ref, sems.at[i])
        for i, (index, w_ref) in enumerate(zip(indexes, w_refs))
    ]
    for load in loads:
        load.start()
    token[...] = jnp.zeros_like(token)
    for load in loads:
        load.wait()


def load_blocks(indexes, w_out, chunks, after):
    shape = block_shape(w_out, chunks)
    *blocks, token = pl.pallas_call(
        functools.partial(load_kernel, indexes),
        out_shape=[jax.ShapeDtypeStruct(shape, jnp.bfloat16)] * len(indexes) + [TOKEN],
        in_specs=[HBM, HBM],
        out_specs=[VMEM] * (len(indexes) + 1),
        scratch_shapes=[pltpu.SemaphoreType.DMA((len(indexes),))],
        compiler_params=pltpu.CompilerParams(vmem_limit_bytes=1 * MIB),
        cost_estimate=pl.CostEstimate(
            flops=0, bytes_accessed=4 * len(indexes) * shape[0] * shape[1], transcendentals=0
        ),
        name=f"load_{indexes[0]}",
    )(after, w_out)
    return blocks, token


def attend_kernel(groups, q_ref, mask_ref, k0, k2, k_near, k_far, v0, v_near, v_far, v2, *rest):
    out_ref = rest[-1]
    rows = out_ref.shape[0]
    width = out_ref.shape[1] // len(groups)
    heads = width // HD
    window = 3 * rows
    factor = HD ** -0.5 * math.log2(math.e)
    across = lax.axis_index("ctx") == 2
    for i, g in enumerate(groups):
        at = slice(g * HD, (g + 1) * HD)
        k1 = jnp.where(across, k_far[:, at], k_near[:, at])
        v1 = jnp.where(across, v_far[:, at], v_near[:, at])
        keys = jnp.concatenate([k2[:, at], k1, k0[:, at]], axis=0)
        values = jnp.concatenate([v2[:, at], v1, v0[:, at]], axis=0)
        stacked = jnp.concatenate(
            [q_ref[:, g * width + h * HD:g * width + (h + 1) * HD] for h in range(heads)], axis=0
        )
        scores = lax.dot_general(
            stacked, keys, (((1,), (1,)), ((), ())), preferred_element_type=jnp.float32
        ).reshape(heads, rows, window)
        scores = scores + mask_ref[...][None]
        top = jnp.max(scores, axis=2, keepdims=True)
        weights = jnp.exp2((scores - top) * factor)
        total = jnp.sum(weights, axis=2, keepdims=True)
        mixed = jnp.dot(
            weights.astype(jnp.bfloat16).reshape(heads * rows, window),
            values,
            preferred_element_type=jnp.float32,
        ).reshape(heads, rows, HD)
        result = (mixed / total).astype(jnp.bfloat16)
        for h in range(heads):
            out_ref[:, i * width + h * HD:i * width + (h + 1) * HD] = result[h]


def attend(groups, width, queries, mask, keys, values, after):
    rows = queries.shape[0]
    return pl.pallas_call(
        functools.partial(attend_kernel, groups),
        out_shape=jax.ShapeDtypeStruct((rows, len(groups) * width), jnp.bfloat16),
        in_specs=[VMEM] * 10 + [HBM] * len(after),
        out_specs=VMEM,
        compiler_params=pltpu.CompilerParams(vmem_limit_bytes=8 * MIB),
        cost_estimate=pl.CostEstimate(flops=0, bytes_accessed=0, transcendentals=0),
        name=f"attend_{groups[0]}",
    )(queries, mask, *keys, *values, *after)


def lay_out(plan, pieces, column, lhs):
    here = lax.axis_index("ctx")
    core = lax.axis_index("tp")
    first = jnp.where(core == 0, 1, 2)
    owners = [here, here ^ first, here ^ (3 - first), here ^ 3]
    unit_rows = lhs.shape[0] // 16
    swap = jnp.where(core == 0, 8, 0)
    wanted = [plan[slot] for slot in range(16)]
    for owner, piece in zip(owners, pieces):
        for u in range(4):
            slot = jnp.int32(0)
            for s in range(1, 16):
                slot = jnp.where(wanted[s] == owner * 4 + u, s, slot)
            slot = slot ^ swap
            at = pl.ds(pl.multiple_of(slot * unit_rows, unit_rows), unit_rows)
            lhs[at, :] = piece[u * unit_rows:(u + 1) * unit_rows, column:column + lhs.shape[1]]


def step_kernel(index, last, column, first, columns, has_acc, has_after, has_load, *refs):
    refs = list(refs)[has_after:]
    first_half = index % HALVES == 0
    load = None
    if has_load:
        sem = refs.pop()
    token = refs.pop()
    if has_load:
        load = block_copy(refs.pop(0), index + 1, refs.pop(), sem)
        load.start()
    if first_half:
        plan, *pieces = refs[:5]
        del refs[:5]
        lhs = refs.pop()
        lay_out(plan, pieces, column, lhs)
    else:
        lhs = refs.pop(0)
    token[...] = jnp.zeros_like(token)
    w_ref = refs.pop(0)
    acc_ref = refs.pop(0) if has_acc else None
    rows = lhs.shape[0] // 2
    for start in range(0, columns, TILE):
        to = slice(start, start + TILE)
        at = slice(first + start, first + start + TILE)
        product = jnp.dot(lhs[...], w_ref[:, at], preferred_element_type=jnp.float32)
        if has_acc:
            product = product + acc_ref[:, at]
        if last:
            own_ref, sent_ref = refs
            own_ref[:, to] = product[rows:]
            sent_ref[:, to] = product[:rows].astype(jnp.bfloat16)
        else:
            refs[0][:, to] = product
    if load is not None:
        load.wait()


def step(index, last, rows_in, column, block, first, columns, w_out, acc, after):
    first_half = index % HALVES == 0
    has_acc, has_after, has_load = acc is not None, after is not None, w_out is not None
    depth = block.shape[0]
    if first_half:
        plan, pieces = rows_in
        total_rows = 4 * pieces[0].shape[0]
        operands, specs = [plan, *pieces], [SMEM] + [VMEM] * 4
    else:
        total_rows = rows_in.shape[0]
        operands, specs = [rows_in], [VMEM]
    if last:
        part = (total_rows // 2, columns)
        shapes = [jax.ShapeDtypeStruct(part, jnp.float32), jax.ShapeDtypeStruct(part, jnp.bfloat16)]
    else:
        shapes = [jax.ShapeDtypeStruct((total_rows, columns), jnp.float32)]
    if first_half:
        shapes.append(jax.ShapeDtypeStruct((total_rows, depth), jnp.bfloat16))
    if has_load:
        shapes.append(jax.ShapeDtypeStruct(block.shape, jnp.bfloat16))
    shapes.append(TOKEN)
    operands = [after] * has_after + [w_out] * has_load + operands + [block] + [acc] * has_acc
    specs = [HBM] * (has_after + has_load) + specs + [VMEM] * (1 + has_acc)
    results = list(pl.pallas_call(
        functools.partial(
            step_kernel, index, last, column, first, columns, has_acc, has_after, has_load
        ),
        out_shape=shapes,
        in_specs=specs,
        out_specs=[VMEM] * len(shapes),
        scratch_shapes=[pltpu.SemaphoreType.DMA] * has_load,
        input_output_aliases={len(operands) - 1: 0} if has_acc and not last else {},
        compiler_params=pltpu.CompilerParams(vmem_limit_bytes=6 * MIB),
        cost_estimate=pl.CostEstimate(
            flops=2 * total_rows * depth * columns, bytes_accessed=0, transcendentals=0
        ),
        name=f"step_{index}_{first // columns}",
    )(*operands))
    token = results.pop()
    following = results.pop() if has_load else None
    lhs = results.pop() if first_half else rows_in
    return results, lhs, following, token


def total_kernel(first, count, has_out, *refs):
    own_refs, got_refs = refs[:count], refs[count:2 * count]
    out_hbm, buf, sems = refs[2 * count + has_out:]
    writes, at = [], 0
    for own_ref, got_ref in zip(own_refs, got_refs):
        columns = own_ref.shape[1]
        for start in range(0, columns, 2 * TILE):
            to = slice(start, start + 2 * TILE)
            value = own_ref[:, to] + got_ref[:, to].astype(jnp.float32)
            here = slice(at + start, at + start + 2 * TILE)
            there = slice(first + at + start, first + at + start + 2 * TILE)
            buf[:, here] = value.astype(jnp.bfloat16)
            write = pltpu.make_async_copy(buf.at[:, here], out_hbm.at[:, there], sems.at[len(writes)])
            write.start()
            writes.append(write)
        at += columns
    for write in writes:
        write.wait()


def total(first, width, own, got, out):
    rows = own[0].shape[0]
    columns = sum(x.shape[1] for x in own)
    count, has_out = len(own), out is not None
    return pl.pallas_call(
        functools.partial(total_kernel, first, count, has_out),
        out_shape=jax.ShapeDtypeStruct((rows, width), jnp.bfloat16),
        in_specs=[VMEM] * (2 * count) + [HBM] * has_out,
        out_specs=HBM,
        scratch_shapes=[
            pltpu.VMEM((rows, columns), jnp.bfloat16),
            pltpu.SemaphoreType.DMA((columns // (2 * TILE),)),
        ],
        input_output_aliases={2 * count: 0} if has_out else {},
        compiler_params=pltpu.CompilerParams(vmem_limit_bytes=4 * MIB),
        cost_estimate=pl.CostEstimate(
            flops=rows * columns, bytes_accessed=2 * rows * columns, transcendentals=0
        ),
        name=f"total_{first}",
    )(*own, *got, *([out] if has_out else []))


def gate_kernel(x, after, out):
    pass


def gate(x, after):
    return pl.pallas_call(
        gate_kernel,
        out_shape=jax.ShapeDtypeStruct(x.shape, x.dtype),
        in_specs=[HBM, HBM],
        out_specs=HBM,
        input_output_aliases={0: 0},
        compiler_params=pltpu.CompilerParams(vmem_limit_bytes=1 * MIB),
        cost_estimate=pl.CostEstimate(flops=0, bytes_accessed=0, transcendentals=0),
        name="gate",
    )(x, after)


def gather_rows(own):
    def route(first):
        pairs = []
        for chip in range(4):
            for core in range(2):
                axis = 1 if (core == 0) == first else 2
                pairs.append((chip * 2 + core, (chip ^ axis) * 2 + core))
        return pairs

    near = lax.ppermute(own, ("ctx", "tp"), route(True))
    side = lax.ppermute(own, ("ctx", "tp"), route(False))

    def forward(after):
        first = near if after is None else gate(near, after)
        return own, first, side, lax.ppermute(first, ("ctx", "tp"), route(False))

    return near, side, forward


def local(queries, key_rows, value_rows, doc_lengths, unit_source, w_out):
    if lax.axis_size("ctx") != 4 or lax.axis_size("tp") != 2 or key_rows.shape[1] != 4 * HD:
        return general(queries, key_rows, value_rows, doc_lengths, unit_source, w_out)
    w_out = in_hbm(w_out)
    kv_heads = key_rows.shape[1] // HD
    width = queries.shape[1] // kv_heads
    two = [(0, 2), (1, 3)]
    value_two = lax.ppermute(value_rows, "ctx", two)
    key_two = lax.ppermute(key_rows, "ctx", two)
    key_near = lax.ppermute(key_rows, "ctx", [(0, 1), (1, 2), (2, 3)])
    value_near = lax.ppermute(value_rows, "ctx", [(0, 1), (2, 3)])
    value_far = lax.ppermute(value_two, "ctx", [(3, 2)])
    own_keys, own_values, held, mask, block = prepare(
        doc_lengths, key_rows, value_rows, queries, w_out, kv_heads, value_two
    )
    keys = (own_keys, key_two, key_near, key_near)
    values = (own_values, value_near, value_far, value_two)
    half_columns = w_out.shape[1] // HALVES
    state = {"blocks": {0: block}, "totals": [None] * HALVES, "before": None}
    rows, mine, got = {}, [], []

    def rows_of(groups, after):
        own = attend(groups, width, held, mask, keys, values, after)
        near, side, forward = gather_rows(own)

        def arrive(after):
            pieces = forward(after)
            for i, g in enumerate(groups):
                rows[g] = (pieces, i * width)
            return pieces[1]

        return own, arrive

    def load(wanted, after):
        loaded, token = load_blocks(wanted, w_out, kv_heads, after)
        state["blocks"].update(zip(wanted, loaded))
        return token

    def steps(g):
        last = g == kv_heads - 1
        pieces, column = rows[g]
        loads = g * HALVES + 1 not in state["blocks"]
        first, lhs, following, state["before"] = step(
            g * HALVES, last, (unit_source, pieces), column, state["blocks"][g * HALVES], 0,
            half_columns,
            w_out if loads else None, state["totals"][0], state["before"],
        )
        if loads:
            state["blocks"][g * HALVES + 1] = following
        second, _, _, state["before"] = step(
            g * HALVES + 1, last, lhs, column, state["blocks"][g * HALVES + 1], 0,
            half_columns, None,
            state["totals"][1], state["before"],
        )
        if last:
            for kept, sent in (first, second):
                mine.append(kept)
                got.append(lax.ppermute(sent, "tp", [(0, 1), (1, 0)]))
        else:
            state["totals"] = [first[0], second[0]]
        return state["before"]

    own, arrive = rows_of((0,), [])
    near = arrive(None)
    own, arrive = rows_of((1,), [load((1, 2), own)])
    arrive(None)
    own, arrive = rows_of((2,), [own, near])
    near = arrive(None)
    own, arrive = rows_of((3,), [own, steps(0)])
    arrive(None)
    state["before"] = load((4, 6), near)
    for g in range(1, kv_heads):
        steps(g)
    out = total(0, w_out.shape[1], mine[:1], got[:1], None)
    return total(half_columns, w_out.shape[1], mine[1:], got[1:], out)


def solution(mesh):
    return jax.shard_map(
        local,
        mesh=mesh,
        in_specs=(
            P(("dp", "ctx"), "tp"),
            P(("dp", "ctx"), "tp"),
            P(("dp", "ctx"), "tp"),
            P("dp"),
            P("dp"),
            P("tp", "ctx"),
        ),
        out_specs=P(("dp", "tp"), "ctx"),
        check_vma=False,
    )
```

```python
import functools
import math

import jax
import jax.numpy as jnp
from jax import lax
from jax.experimental import pallas as pl
from jax.experimental.pallas import tpu as pltpu
from jax.sharding import PartitionSpec as P

HD = 128
MIB = 1 << 20
HALVES = 2


def doc_index(positions, doc_ends):
    return jnp.sum((positions[None, :] >= doc_ends[:, None]).astype(jnp.int32), axis=0)


def general(queries, key_rows, value_rows, doc_lengths, unit_source, w_out):
    ctx_count = lax.axis_size("ctx")
    ctx_index = lax.axis_index("ctx")
    tok_dev, columns = queries.shape
    unit_rows = tok_dev // ctx_count
    head_count = columns // HD
    kv_heads = key_rows.shape[1] // HD
    group_size = head_count // kv_heads
    unit_plan = unit_source.reshape(ctx_count, ctx_count)
    positions = ctx_index * tok_dev + jnp.arange(tok_dev, dtype=jnp.int32)
    doc_ends = jnp.cumsum(doc_lengths)
    query_doc = doc_index(positions, doc_ends)
    grouped = queries.reshape(tok_dev, kv_heads, group_size, HD)
    key_all = lax.all_gather(key_rows, "ctx", axis=0, tiled=True)
    value_all = lax.all_gather(value_rows, "ctx", axis=0, tiled=True)
    extent = key_all.shape[0]
    key_pos = jnp.arange(extent, dtype=jnp.int32)
    key_doc = doc_index(key_pos, doc_ends)
    visible = (key_doc[None, :] == query_doc[:, None]) & (key_pos[None, :] <= positions[:, None])
    scores = jnp.einsum(
        "qkgd,pkd->kgqp",
        grouped,
        key_all.reshape(extent, kv_heads, HD),
        preferred_element_type=jnp.float32,
    ) * (HD ** -0.5)
    scores = jnp.where(visible, scores, -jnp.inf)
    row_max = jnp.max(scores, axis=3, keepdims=True)
    weights = jnp.where(visible, jnp.exp(scores - row_max), 0.0)
    totals = jnp.sum(weights, axis=3)
    blended = jnp.einsum(
        "kgqp,pkd->kgqd",
        weights.astype(jnp.bfloat16),
        value_all.reshape(extent, kv_heads, HD),
        preferred_element_type=jnp.float32,
    )
    attended = (
        (blended / totals[..., None])
        .transpose(2, 0, 1, 3)
        .reshape(tok_dev, columns)
        .astype(jnp.bfloat16)
    )
    gathered = lax.all_gather(attended, "ctx", axis=0, tiled=True)
    units = gathered.reshape(ctx_count * ctx_count, unit_rows, columns)
    balanced = jnp.take(units, unit_plan.reshape(-1), axis=0).reshape(extent, columns)
    partial_value = jnp.dot(balanced, w_out, preferred_element_type=jnp.float32)
    return lax.psum_scatter(
        partial_value.astype(jnp.bfloat16), "tp", scatter_dimension=0, tiled=True
    )


SMEM = pl.BlockSpec(memory_space=pltpu.SMEM)
VMEM = pl.BlockSpec(memory_space=pltpu.VMEM)
HBM = pl.BlockSpec(memory_space=pl.ANY)
TILE = 512


def in_hbm(x):
    return pltpu.with_memory_space_constraint(x, pltpu.HBM)


TOKEN = jax.ShapeDtypeStruct((8, 128), jnp.float32)


def block_copy(w_hbm, row, half, w_ref, sem):
    depth, columns = w_ref.shape
    return pltpu.make_async_copy(
        w_hbm.at[row:row + depth, half * columns:(half + 1) * columns], w_ref, sem
    )


def prepare_kernel(docs_hbm, k_hbm, v_hbm, q_hbm, w_hbm, after, k_ref, v_ref, q_ref, mask_ref, w_ref, docs, sems):
    lengths = pltpu.make_async_copy(docs_hbm, docs, sems.at[0])
    loads = [
        pltpu.make_async_copy(k_hbm, k_ref, sems.at[1]),
        pltpu.make_async_copy(v_hbm, v_ref, sems.at[2]),
        pltpu.make_async_copy(q_hbm, q_ref, sems.at[3]),
        block_copy(w_hbm, 0, 0, w_ref, sems.at[4]),
    ]
    lengths.start()
    for load in loads:
        load.start()
    lengths.wait()
    rows, window = mask_ref.shape
    base = lax.axis_index("ctx") * rows
    pos = base + lax.broadcasted_iota(jnp.int32, (rows, window), 0)
    start = jnp.zeros((rows, window), jnp.int32)
    end = jnp.int32(0)
    for d in range(docs.shape[0]):
        end = end + docs[d]
        start = jnp.where(pos >= end, end, start)
    key_pos = base + rows - window + lax.broadcasted_iota(jnp.int32, (rows, window), 1)
    mask_ref[...] = jnp.where((key_pos >= start) & (key_pos <= pos), 0.0, -jnp.inf)
    for load in loads:
        load.wait()


def prepare(doc_lengths, key_rows, value_rows, queries, w_out, depth, after):
    rows = queries.shape[0]
    return pl.pallas_call(
        prepare_kernel,
        out_shape=[
            jax.ShapeDtypeStruct(key_rows.shape, jnp.bfloat16),
            jax.ShapeDtypeStruct(value_rows.shape, jnp.bfloat16),
            jax.ShapeDtypeStruct(queries.shape, jnp.bfloat16),
            jax.ShapeDtypeStruct((rows, 3 * rows), jnp.float32),
            jax.ShapeDtypeStruct((depth, w_out.shape[1] // HALVES), jnp.bfloat16),
        ],
        in_specs=[HBM] * 6,
        out_specs=[VMEM] * 5,
        scratch_shapes=[
            pltpu.SMEM(doc_lengths.shape, jnp.int32),
            pltpu.SemaphoreType.DMA((5,)),
        ],
        compiler_params=pltpu.CompilerParams(vmem_limit_bytes=4 * MIB),
        cost_estimate=pl.CostEstimate(
            flops=0, bytes_accessed=depth * w_out.shape[1], transcendentals=0
        ),
        name="prepare",
    )(
        in_hbm(doc_lengths), in_hbm(key_rows), in_hbm(value_rows), in_hbm(queries), w_out, after
    )


def load_kernel(wanted, after, w_hbm, *refs):
    *w_refs, token, sems = refs
    loads = [
        block_copy(w_hbm, row, half, w_ref, sems.at[i])
        for i, ((row, depth, half), w_ref) in enumerate(zip(wanted, w_refs))
    ]
    for load in loads:
        load.start()
    token[...] = jnp.zeros_like(token)
    for load in loads:
        load.wait()


def load_blocks(wanted, w_out, after):
    columns = w_out.shape[1] // HALVES
    *blocks, token = pl.pallas_call(
        functools.partial(load_kernel, wanted),
        out_shape=[
            jax.ShapeDtypeStruct((depth, columns), jnp.bfloat16) for _, depth, _ in wanted
        ] + [TOKEN],
        in_specs=[HBM, HBM],
        out_specs=[VMEM] * (len(wanted) + 1),
        scratch_shapes=[pltpu.SemaphoreType.DMA((len(wanted),))],
        compiler_params=pltpu.CompilerParams(vmem_limit_bytes=1 * MIB),
        cost_estimate=pl.CostEstimate(
            flops=0,
            bytes_accessed=4 * columns * sum(depth for _, depth, _ in wanted),
            transcendentals=0,
        ),
        name=f"load_{wanted[0][0]}",
    )(after, w_out)
    return blocks, token


def attend_kernel(groups, q_ref, mask_ref, k0, k2, k_near, k_far, v0, v_near, v_far, v2, *rest):
    out_ref = rest[-1]
    rows = out_ref.shape[0]
    width = out_ref.shape[1] // len(groups)
    heads = width // HD
    window = 3 * rows
    factor = HD ** -0.5 * math.log2(math.e)
    across = lax.axis_index("ctx") == 2
    for i, g in enumerate(groups):
        at = slice(g * HD, (g + 1) * HD)
        k1 = jnp.where(across, k_far[:, at], k_near[:, at])
        v1 = jnp.where(across, v_far[:, at], v_near[:, at])
        keys = jnp.concatenate([k2[:, at], k1, k0[:, at]], axis=0)
        values = jnp.concatenate([v2[:, at], v1, v0[:, at]], axis=0)
        stacked = jnp.concatenate(
            [q_ref[:, g * width + h * HD:g * width + (h + 1) * HD] for h in range(heads)], axis=0
        )
        scores = lax.dot_general(
            stacked, keys, (((1,), (1,)), ((), ())), preferred_element_type=jnp.float32
        ).reshape(heads, rows, window)
        scores = scores + mask_ref[...][None]
        top = jnp.max(scores, axis=2, keepdims=True)
        weights = jnp.exp2((scores - top) * factor)
        total = jnp.sum(weights, axis=2, keepdims=True)
        mixed = jnp.dot(
            weights.astype(jnp.bfloat16).reshape(heads * rows, window),
            values,
            preferred_element_type=jnp.float32,
        ).reshape(heads, rows, HD)
        result = (mixed / total).astype(jnp.bfloat16)
        for h in range(heads):
            out_ref[:, i * width + h * HD:i * width + (h + 1) * HD] = result[h]


def attend(groups, width, queries, mask, keys, values, after):
    rows = queries.shape[0]
    return pl.pallas_call(
        functools.partial(attend_kernel, groups),
        out_shape=jax.ShapeDtypeStruct((rows, len(groups) * width), jnp.bfloat16),
        in_specs=[VMEM] * 10 + [HBM] * len(after),
        out_specs=VMEM,
        compiler_params=pltpu.CompilerParams(vmem_limit_bytes=8 * MIB),
        cost_estimate=pl.CostEstimate(flops=0, bytes_accessed=0, transcendentals=0),
        name=f"attend_{groups[0]}",
    )(queries, mask, *keys, *values, *after)


def lay_out(plan, pieces, lhs):
    here = lax.axis_index("ctx")
    core = lax.axis_index("tp")
    first = jnp.where(core == 0, 1, 2)
    owners = [here, here ^ first, here ^ (3 - first), here ^ 3]
    unit_rows = lhs.shape[0] // 16
    swap = jnp.where(core == 0, 8, 0)
    wanted = [plan[slot] for slot in range(16)]
    for owner, piece in zip(owners, pieces):
        for u in range(4):
            slot = jnp.int32(0)
            for s in range(1, 16):
                slot = jnp.where(wanted[s] == owner * 4 + u, s, slot)
            slot = slot ^ swap
            at = pl.ds(pl.multiple_of(slot * unit_rows, unit_rows), unit_rows)
            lhs[at, :] = piece[u * unit_rows:(u + 1) * unit_rows, :]


def step_kernel(row, half, last, has_acc, has_after, has_load, *refs):
    refs = list(refs)[has_after:]
    load = None
    if has_load:
        sem = refs.pop()
    token = refs.pop()
    if has_load:
        load = block_copy(refs.pop(0), row, half + 1, refs.pop(), sem)
        load.start()
    if half == 0:
        plan, *pieces = refs[:5]
        del refs[:5]
        lhs = refs.pop()
        lay_out(plan, pieces, lhs)
    else:
        lhs = refs.pop(0)
    token[...] = jnp.zeros_like(token)
    w_ref = refs.pop(0)
    acc_ref = refs.pop(0) if has_acc else None
    rows = lhs.shape[0] // 2
    for start in range(0, w_ref.shape[1], TILE):
        at = slice(start, start + TILE)
        product = jnp.dot(lhs[...], w_ref[:, at], preferred_element_type=jnp.float32)
        if has_acc:
            product = product + acc_ref[:, at]
        if last:
            own_ref, sent_ref = refs
            own_ref[:, at] = product[rows:]
            sent_ref[:, at] = product[:rows].astype(jnp.bfloat16)
        else:
            refs[0][:, at] = product
    if load is not None:
        load.wait()


def step(row, half, last, rows_in, block, w_out, acc, after):
    has_acc, has_after, has_load = acc is not None, after is not None, w_out is not None
    depth, columns = block.shape
    if half == 0:
        plan, pieces = rows_in
        total_rows = 4 * pieces[0].shape[0]
        operands, specs = [plan, *pieces], [SMEM] + [VMEM] * 4
    else:
        total_rows = rows_in.shape[0]
        operands, specs = [rows_in], [VMEM]
    if last:
        part = (total_rows // 2, columns)
        shapes = [jax.ShapeDtypeStruct(part, jnp.float32), jax.ShapeDtypeStruct(part, jnp.bfloat16)]
    else:
        shapes = [jax.ShapeDtypeStruct((total_rows, columns), jnp.float32)]
    if half == 0:
        shapes.append(jax.ShapeDtypeStruct((total_rows, depth), jnp.bfloat16))
    if has_load:
        shapes.append(jax.ShapeDtypeStruct(block.shape, jnp.bfloat16))
    shapes.append(TOKEN)
    operands = [after] * has_after + [w_out] * has_load + operands + [block] + [acc] * has_acc
    specs = [HBM] * (has_after + has_load) + specs + [VMEM] * (1 + has_acc)
    results = list(pl.pallas_call(
        functools.partial(step_kernel, row, half, last, has_acc, has_after, has_load),
        out_shape=shapes,
        in_specs=specs,
        out_specs=[VMEM] * len(shapes),
        scratch_shapes=[pltpu.SemaphoreType.DMA] * has_load,
        input_output_aliases={len(operands) - 1: 0} if has_acc and not last else {},
        compiler_params=pltpu.CompilerParams(vmem_limit_bytes=6 * MIB),
        cost_estimate=pl.CostEstimate(
            flops=2 * total_rows * depth * columns, bytes_accessed=0, transcendentals=0
        ),
        name=f"step_{row}_{half}",
    )(*operands))
    token = results.pop()
    following = results.pop() if has_load else None
    lhs = results.pop() if half == 0 else rows_in
    return results, lhs, following, token


def total_kernel(first, count, has_out, *refs):
    own_refs, got_refs = refs[:count], refs[count:2 * count]
    out_hbm, buf, sems = refs[2 * count + has_out:]
    writes, at = [], 0
    for own_ref, got_ref in zip(own_refs, got_refs):
        columns = own_ref.shape[1]
        for start in range(0, columns, 2 * TILE):
            to = slice(start, start + 2 * TILE)
            value = own_ref[:, to] + got_ref[:, to].astype(jnp.float32)
            here = slice(at + start, at + start + 2 * TILE)
            there = slice(first + at + start, first + at + start + 2 * TILE)
            buf[:, here] = value.astype(jnp.bfloat16)
            write = pltpu.make_async_copy(buf.at[:, here], out_hbm.at[:, there], sems.at[len(writes)])
            write.start()
            writes.append(write)
        at += columns
    for write in writes:
        write.wait()


def total(first, width, own, got, out):
    rows = own[0].shape[0]
    columns = sum(x.shape[1] for x in own)
    count, has_out = len(own), out is not None
    return pl.pallas_call(
        functools.partial(total_kernel, first, count, has_out),
        out_shape=jax.ShapeDtypeStruct((rows, width), jnp.bfloat16),
        in_specs=[VMEM] * (2 * count) + [HBM] * has_out,
        out_specs=HBM,
        scratch_shapes=[
            pltpu.VMEM((rows, columns), jnp.bfloat16),
            pltpu.SemaphoreType.DMA((columns // (2 * TILE),)),
        ],
        input_output_aliases={2 * count: 0} if has_out else {},
        compiler_params=pltpu.CompilerParams(vmem_limit_bytes=4 * MIB),
        cost_estimate=pl.CostEstimate(
            flops=rows * columns, bytes_accessed=2 * rows * columns, transcendentals=0
        ),
        name=f"total_{first}",
    )(*own, *got, *([out] if has_out else []))


def gate_kernel(x, after, out):
    pass


def gate(x, after):
    return pl.pallas_call(
        gate_kernel,
        out_shape=jax.ShapeDtypeStruct(x.shape, x.dtype),
        in_specs=[HBM, HBM],
        out_specs=HBM,
        input_output_aliases={0: 0},
        compiler_params=pltpu.CompilerParams(vmem_limit_bytes=1 * MIB),
        cost_estimate=pl.CostEstimate(flops=0, bytes_accessed=0, transcendentals=0),
        name="gate",
    )(x, after)


def gather_rows(own):
    def route(first):
        pairs = []
        for chip in range(4):
            for core in range(2):
                axis = 1 if (core == 0) == first else 2
                pairs.append((chip * 2 + core, (chip ^ axis) * 2 + core))
        return pairs

    near = lax.ppermute(own, ("ctx", "tp"), route(True))
    side = lax.ppermute(own, ("ctx", "tp"), route(False))

    def forward(after):
        first = near if after is None else gate(near, after)
        return own, first, side, lax.ppermute(first, ("ctx", "tp"), route(False))

    return near, side, forward


def local(queries, key_rows, value_rows, doc_lengths, unit_source, w_out):
    if lax.axis_size("ctx") != 4 or lax.axis_size("tp") != 2 or key_rows.shape[1] != 4 * HD:
        return general(queries, key_rows, value_rows, doc_lengths, unit_source, w_out)
    w_out = in_hbm(w_out)
    kv_heads = key_rows.shape[1] // HD
    width = queries.shape[1] // kv_heads
    two = [(0, 2), (1, 3)]
    value_two = lax.ppermute(value_rows, "ctx", two)
    key_two = lax.ppermute(key_rows, "ctx", two)
    key_near = lax.ppermute(key_rows, "ctx", [(0, 1), (1, 2), (2, 3)])
    value_near = lax.ppermute(value_rows, "ctx", [(0, 1), (2, 3)])
    value_far = lax.ppermute(value_two, "ctx", [(3, 2)])
    own_keys, own_values, held, mask, block = prepare(
        doc_lengths, key_rows, value_rows, queries, w_out, width, value_two
    )
    keys = (own_keys, key_two, key_near, key_near)
    values = (own_values, value_near, value_far, value_two)
    state = {"blocks": {(0, 0): block}, "totals": [None] * HALVES, "before": None}
    rows, mine, got = {}, [], []

    def rows_of(groups, after):
        own = attend(groups, width, held, mask, keys, values, after)
        _, _, forward = gather_rows(own)

        def arrive(after):
            rows[groups] = forward(after)
            return rows[groups]

        return own, arrive

    def load(wanted, after):
        blocks, token = load_blocks(
            [(groups[0] * width, len(groups) * width, half) for groups, half in wanted], w_out, after
        )
        for (groups, half), loaded in zip(wanted, blocks):
            state["blocks"][groups[0], half] = loaded
        return token

    def steps(groups, between=None):
        last = groups[-1] == kv_heads - 1
        row = groups[0] * width
        second_block = state["blocks"].get((groups[0], 1))
        first, lhs, following, state["before"] = step(
            row, 0, last, (unit_source, rows[groups]), state["blocks"][groups[0], 0],
            w_out if second_block is None else None, state["totals"][0], state["before"],
        )
        if between is not None:
            between(state["before"])
        second, _, _, state["before"] = step(
            row, 1, last, lhs, following if second_block is None else second_block, None,
            state["totals"][1], state["before"],
        )
        if last:
            for kept, sent in (first, second):
                mine.append(kept)
                got.append(lax.ppermute(sent, "tp", [(0, 1), (1, 0)]))
        else:
            state["totals"] = [first[0], second[0]]
        return state["before"]

    one, two, rest = (0,), (1,), (2, 3)
    own, arrive = rows_of(one, [])
    pieces = arrive(None)
    own, arrive = rows_of(two, [load([(one, 1), (two, 0)], own)])
    arrive(None)
    token = load([(rest, 0)], own)
    _, arrive = rows_of(rest, [token, pieces[3]])
    steps(one)
    steps(two, arrive)
    steps(rest)
    half_columns = w_out.shape[1] // HALVES
    out = total(0, w_out.shape[1], mine[:1], got[:1], None)
    return total(half_columns, w_out.shape[1], mine[1:], got[1:], out)


def solution(mesh):
    return jax.shard_map(
        local,
        mesh=mesh,
        in_specs=(
            P(("dp", "ctx"), "tp"),
            P(("dp", "ctx"), "tp"),
            P(("dp", "ctx"), "tp"),
            P("dp"),
            P("dp"),
            P("tp", "ctx"),
        ),
        out_specs=P(("dp", "tp"), "ctx"),
        check_vma=False,
    )
```

```python
import functools
import math

import jax
import jax.numpy as jnp
from jax import lax
from jax.experimental import pallas as pl
from jax.experimental.pallas import tpu as pltpu
from jax.sharding import PartitionSpec as P

HD = 128
MIB = 1 << 20
HALVES = 2


def doc_index(positions, doc_ends):
    return jnp.sum((positions[None, :] >= doc_ends[:, None]).astype(jnp.int32), axis=0)


def general(queries, key_rows, value_rows, doc_lengths, unit_source, w_out):
    ctx_count = lax.axis_size("ctx")
    ctx_index = lax.axis_index("ctx")
    tok_dev, columns = queries.shape
    unit_rows = tok_dev // ctx_count
    head_count = columns // HD
    kv_heads = key_rows.shape[1] // HD
    group_size = head_count // kv_heads
    unit_plan = unit_source.reshape(ctx_count, ctx_count)
    positions = ctx_index * tok_dev + jnp.arange(tok_dev, dtype=jnp.int32)
    doc_ends = jnp.cumsum(doc_lengths)
    query_doc = doc_index(positions, doc_ends)
    grouped = queries.reshape(tok_dev, kv_heads, group_size, HD)
    key_all = lax.all_gather(key_rows, "ctx", axis=0, tiled=True)
    value_all = lax.all_gather(value_rows, "ctx", axis=0, tiled=True)
    extent = key_all.shape[0]
    key_pos = jnp.arange(extent, dtype=jnp.int32)
    key_doc = doc_index(key_pos, doc_ends)
    visible = (key_doc[None, :] == query_doc[:, None]) & (key_pos[None, :] <= positions[:, None])
    scores = jnp.einsum(
        "qkgd,pkd->kgqp",
        grouped,
        key_all.reshape(extent, kv_heads, HD),
        preferred_element_type=jnp.float32,
    ) * (HD ** -0.5)
    scores = jnp.where(visible, scores, -jnp.inf)
    row_max = jnp.max(scores, axis=3, keepdims=True)
    weights = jnp.where(visible, jnp.exp(scores - row_max), 0.0)
    totals = jnp.sum(weights, axis=3)
    blended = jnp.einsum(
        "kgqp,pkd->kgqd",
        weights.astype(jnp.bfloat16),
        value_all.reshape(extent, kv_heads, HD),
        preferred_element_type=jnp.float32,
    )
    attended = (
        (blended / totals[..., None])
        .transpose(2, 0, 1, 3)
        .reshape(tok_dev, columns)
        .astype(jnp.bfloat16)
    )
    gathered = lax.all_gather(attended, "ctx", axis=0, tiled=True)
    units = gathered.reshape(ctx_count * ctx_count, unit_rows, columns)
    balanced = jnp.take(units, unit_plan.reshape(-1), axis=0).reshape(extent, columns)
    partial_value = jnp.dot(balanced, w_out, preferred_element_type=jnp.float32)
    return lax.psum_scatter(
        partial_value.astype(jnp.bfloat16), "tp", scatter_dimension=0, tiled=True
    )


SMEM = pl.BlockSpec(memory_space=pltpu.SMEM)
VMEM = pl.BlockSpec(memory_space=pltpu.VMEM)
HBM = pl.BlockSpec(memory_space=pl.ANY)
TILE = 512


def in_hbm(x):
    return pltpu.with_memory_space_constraint(x, pltpu.HBM)


TOKEN = jax.ShapeDtypeStruct((8, 128), jnp.float32)


def block_copy(w_hbm, row, half, w_ref, sem):
    depth, columns = w_ref.shape
    return pltpu.make_async_copy(
        w_hbm.at[row:row + depth, half * columns:(half + 1) * columns], w_ref, sem
    )


def prepare_kernel(docs_hbm, k_hbm, v_hbm, q_hbm, w_hbm, after, k_ref, v_ref, q_ref, mask_ref, w_ref, docs, sems):
    lengths = pltpu.make_async_copy(docs_hbm, docs, sems.at[0])
    loads = [
        pltpu.make_async_copy(k_hbm, k_ref, sems.at[1]),
        pltpu.make_async_copy(v_hbm, v_ref, sems.at[2]),
        pltpu.make_async_copy(q_hbm, q_ref, sems.at[3]),
        block_copy(w_hbm, 0, 0, w_ref, sems.at[4]),
    ]
    lengths.start()
    for load in loads:
        load.start()
    lengths.wait()
    rows, window = mask_ref.shape
    base = lax.axis_index("ctx") * rows
    pos = base + lax.broadcasted_iota(jnp.int32, (rows, window), 0)
    start = jnp.zeros((rows, window), jnp.int32)
    end = jnp.int32(0)
    for d in range(docs.shape[0]):
        end = end + docs[d]
        start = jnp.where(pos >= end, end, start)
    key_pos = base + rows - window + lax.broadcasted_iota(jnp.int32, (rows, window), 1)
    mask_ref[...] = jnp.where((key_pos >= start) & (key_pos <= pos), 0.0, -jnp.inf)
    for load in loads:
        load.wait()


def prepare(doc_lengths, key_rows, value_rows, queries, w_out, depth, after):
    rows = queries.shape[0]
    return pl.pallas_call(
        prepare_kernel,
        out_shape=[
            jax.ShapeDtypeStruct(key_rows.shape, jnp.bfloat16),
            jax.ShapeDtypeStruct(value_rows.shape, jnp.bfloat16),
            jax.ShapeDtypeStruct(queries.shape, jnp.bfloat16),
            jax.ShapeDtypeStruct((rows, 3 * rows), jnp.float32),
            jax.ShapeDtypeStruct((depth, w_out.shape[1] // HALVES), jnp.bfloat16),
        ],
        in_specs=[HBM] * 6,
        out_specs=[VMEM] * 5,
        scratch_shapes=[
            pltpu.SMEM(doc_lengths.shape, jnp.int32),
            pltpu.SemaphoreType.DMA((5,)),
        ],
        compiler_params=pltpu.CompilerParams(vmem_limit_bytes=4 * MIB),
        cost_estimate=pl.CostEstimate(
            flops=0, bytes_accessed=depth * w_out.shape[1], transcendentals=0
        ),
        name="prepare",
    )(
        in_hbm(doc_lengths), in_hbm(key_rows), in_hbm(value_rows), in_hbm(queries), w_out, after
    )


def load_kernel(wanted, after, w_hbm, *refs):
    *w_refs, token, sems = refs
    loads = [
        block_copy(w_hbm, row, half, w_ref, sems.at[i])
        for i, ((row, depth, half), w_ref) in enumerate(zip(wanted, w_refs))
    ]
    for load in loads:
        load.start()
    token[...] = jnp.zeros_like(token)
    for load in loads:
        load.wait()


def load_blocks(wanted, w_out, after):
    columns = w_out.shape[1] // HALVES
    *blocks, token = pl.pallas_call(
        functools.partial(load_kernel, wanted),
        out_shape=[
            jax.ShapeDtypeStruct((depth, columns), jnp.bfloat16) for _, depth, _ in wanted
        ] + [TOKEN],
        in_specs=[HBM, HBM],
        out_specs=[VMEM] * (len(wanted) + 1),
        scratch_shapes=[pltpu.SemaphoreType.DMA((len(wanted),))],
        compiler_params=pltpu.CompilerParams(vmem_limit_bytes=1 * MIB),
        cost_estimate=pl.CostEstimate(
            flops=0,
            bytes_accessed=4 * columns * sum(depth for _, depth, _ in wanted),
            transcendentals=0,
        ),
        name=f"load_{wanted[0][0]}",
    )(after, w_out)
    return blocks, token


def attend_kernel(groups, q_ref, mask_ref, k0, k_near, k_far, k2, v0, v_near, v_far, v2, *rest):
    out_ref = rest[-1]
    rows = out_ref.shape[0]
    width = out_ref.shape[1] // len(groups)
    heads = width // HD
    window = 3 * rows
    factor = HD ** -0.5 * math.log2(math.e)
    across = lax.axis_index("ctx") == 2
    for i, g in enumerate(groups):
        at = slice(g * HD, (g + 1) * HD)
        k1 = jnp.where(across, k_far[:, at], k_near[:, at])
        v1 = jnp.where(across, v_far[:, at], v_near[:, at])
        keys = jnp.concatenate([k2[:, at], k1, k0[:, at]], axis=0)
        values = jnp.concatenate([v2[:, at], v1, v0[:, at]], axis=0)
        stacked = jnp.concatenate(
            [q_ref[:, g * width + h * HD:g * width + (h + 1) * HD] for h in range(heads)], axis=0
        )
        scores = lax.dot_general(
            stacked, keys, (((1,), (1,)), ((), ())), preferred_element_type=jnp.float32
        ).reshape(heads, rows, window)
        scores = scores + mask_ref[...][None]
        top = jnp.max(scores, axis=2, keepdims=True)
        weights = jnp.exp2((scores - top) * factor)
        total = jnp.sum(weights, axis=2, keepdims=True)
        mixed = jnp.dot(
            weights.astype(jnp.bfloat16).reshape(heads * rows, window),
            values,
            preferred_element_type=jnp.float32,
        ).reshape(heads, rows, HD)
        result = (mixed / total).astype(jnp.bfloat16)
        for h in range(heads):
            out_ref[:, i * width + h * HD:i * width + (h + 1) * HD] = result[h]


def attend(groups, width, queries, mask, keys, values, after):
    rows = queries.shape[0]
    return pl.pallas_call(
        functools.partial(attend_kernel, groups),
        out_shape=jax.ShapeDtypeStruct((rows, len(groups) * width), jnp.bfloat16),
        in_specs=[VMEM] * 10 + [HBM] * len(after),
        out_specs=VMEM,
        compiler_params=pltpu.CompilerParams(vmem_limit_bytes=8 * MIB),
        cost_estimate=pl.CostEstimate(flops=0, bytes_accessed=0, transcendentals=0),
        name=f"attend_{groups[0]}",
    )(queries, mask, *keys, *values, *after)


def lay_out(plan, pieces, column, lhs):
    here = lax.axis_index("ctx")
    core = lax.axis_index("tp")
    first = jnp.where(core == 0, 1, 2)
    owners = [here, here ^ first, here ^ (3 - first), here ^ 3]
    unit_rows = lhs.shape[0] // 16
    swap = jnp.where(core == 0, 8, 0)
    wanted = [plan[slot] for slot in range(16)]
    for owner, piece in zip(owners, pieces):
        for u in range(4):
            slot = jnp.int32(0)
            for s in range(1, 16):
                slot = jnp.where(wanted[s] == owner * 4 + u, s, slot)
            slot = slot ^ swap
            at = pl.ds(pl.multiple_of(slot * unit_rows, unit_rows), unit_rows)
            lhs[at, column:column + piece.shape[1]] = piece[u * unit_rows:(u + 1) * unit_rows, :]


def step_kernel(row, half, last, pieces_in, has_acc, has_after, has_load, *refs):
    refs = list(refs)[has_after:]
    load = None
    if has_load:
        sem = refs.pop()
    token = refs.pop()
    if has_load:
        load = block_copy(refs.pop(0), row, half + 1, refs.pop(), sem)
        load.start()
    if half == 0:
        plan, *pieces = refs[:1 + pieces_in]
        del refs[:1 + pieces_in]
        lhs = refs.pop()
        width = pieces[0].shape[1]
        for i in range(0, pieces_in, 4):
            lay_out(plan, pieces[i:i + 4], i // 4 * width, lhs)
    else:
        lhs = refs.pop(0)
    token[...] = jnp.zeros_like(token)
    w_ref = refs.pop(0)
    acc_ref = refs.pop(0) if has_acc else None
    rows = lhs.shape[0] // 2
    for start in range(0, w_ref.shape[1], TILE):
        at = slice(start, start + TILE)
        product = jnp.dot(lhs[...], w_ref[:, at], preferred_element_type=jnp.float32)
        if has_acc:
            product = product + acc_ref[:, at]
        if last:
            own_ref, sent_ref = refs
            own_ref[:, at] = product[rows:]
            sent_ref[:, at] = product[:rows].astype(jnp.bfloat16)
        else:
            refs[0][:, at] = product
    if load is not None:
        load.wait()


def step(row, half, last, rows_in, block, w_out, acc, after):
    has_acc, has_after, has_load = acc is not None, len(after), w_out is not None
    depth, columns = block.shape
    if half == 0:
        plan, pieces = rows_in
        pieces_in = len(pieces)
        total_rows = 4 * pieces[0].shape[0]
        operands, specs = [plan, *pieces], [SMEM] + [VMEM] * pieces_in
    else:
        pieces_in = 0
        total_rows = rows_in.shape[0]
        operands, specs = [rows_in], [VMEM]
    if last:
        part = (total_rows // 2, columns)
        shapes = [jax.ShapeDtypeStruct(part, jnp.float32), jax.ShapeDtypeStruct(part, jnp.bfloat16)]
    else:
        shapes = [jax.ShapeDtypeStruct((total_rows, columns), jnp.float32)]
    if half == 0:
        shapes.append(jax.ShapeDtypeStruct((total_rows, depth), jnp.bfloat16))
    if has_load:
        shapes.append(jax.ShapeDtypeStruct(block.shape, jnp.bfloat16))
    shapes.append(TOKEN)
    operands = [*after] + [w_out] * has_load + operands + [block] + [acc] * has_acc
    specs = [HBM] * (has_after + has_load) + specs + [VMEM] * (1 + has_acc)
    results = list(pl.pallas_call(
        functools.partial(step_kernel, row, half, last, pieces_in, has_acc, has_after, has_load),
        out_shape=shapes,
        in_specs=specs,
        out_specs=[VMEM] * len(shapes),
        scratch_shapes=[pltpu.SemaphoreType.DMA] * has_load,
        input_output_aliases={len(operands) - 1: 0} if has_acc and not last else {},
        compiler_params=pltpu.CompilerParams(vmem_limit_bytes=6 * MIB),
        cost_estimate=pl.CostEstimate(
            flops=2 * total_rows * depth * columns, bytes_accessed=0, transcendentals=0
        ),
        name=f"step_{row}_{half}",
    )(*operands))
    token = results.pop()
    following = results.pop() if has_load else None
    lhs = results.pop() if half == 0 else rows_in
    return results, lhs, following, token


def total_kernel(first, count, has_out, *refs):
    own_refs, got_refs = refs[:count], refs[count:2 * count]
    out_hbm, buf, sems = refs[2 * count + has_out:]
    writes, at = [], 0
    for own_ref, got_ref in zip(own_refs, got_refs):
        columns = own_ref.shape[1]
        for start in range(0, columns, 2 * TILE):
            to = slice(start, start + 2 * TILE)
            value = own_ref[:, to] + got_ref[:, to].astype(jnp.float32)
            here = slice(at + start, at + start + 2 * TILE)
            there = slice(first + at + start, first + at + start + 2 * TILE)
            buf[:, here] = value.astype(jnp.bfloat16)
            write = pltpu.make_async_copy(buf.at[:, here], out_hbm.at[:, there], sems.at[len(writes)])
            write.start()
            writes.append(write)
        at += columns
    for write in writes:
        write.wait()


def total(first, width, own, got, out):
    rows = own[0].shape[0]
    columns = sum(x.shape[1] for x in own)
    count, has_out = len(own), out is not None
    return pl.pallas_call(
        functools.partial(total_kernel, first, count, has_out),
        out_shape=jax.ShapeDtypeStruct((rows, width), jnp.bfloat16),
        in_specs=[VMEM] * (2 * count) + [HBM] * has_out,
        out_specs=HBM,
        scratch_shapes=[
            pltpu.VMEM((rows, columns), jnp.bfloat16),
            pltpu.SemaphoreType.DMA((columns // (2 * TILE),)),
        ],
        input_output_aliases={2 * count: 0} if has_out else {},
        compiler_params=pltpu.CompilerParams(vmem_limit_bytes=4 * MIB),
        cost_estimate=pl.CostEstimate(
            flops=rows * columns, bytes_accessed=2 * rows * columns, transcendentals=0
        ),
        name=f"total_{first}",
    )(*own, *got, *([out] if has_out else []))


def gate_kernel(x, after, out):
    pass


def gate(x, after):
    return pl.pallas_call(
        gate_kernel,
        out_shape=jax.ShapeDtypeStruct(x.shape, x.dtype),
        in_specs=[HBM, HBM],
        out_specs=HBM,
        input_output_aliases={0: 0},
        compiler_params=pltpu.CompilerParams(vmem_limit_bytes=1 * MIB),
        cost_estimate=pl.CostEstimate(flops=0, bytes_accessed=0, transcendentals=0),
        name="gate",
    )(x, after)


def gather_rows(own):
    def route(first):
        pairs = []
        for chip in range(4):
            for core in range(2):
                axis = 1 if (core == 0) == first else 2
                pairs.append((chip * 2 + core, (chip ^ axis) * 2 + core))
        return pairs

    near = lax.ppermute(own, ("ctx", "tp"), route(True))
    side = lax.ppermute(own, ("ctx", "tp"), route(False))

    def forward(after):
        first = near if after is None else gate(near, after)
        return own, first, side, lax.ppermute(first, ("ctx", "tp"), route(False))

    return near, side, forward


def local(queries, key_rows, value_rows, doc_lengths, unit_source, w_out):
    if lax.axis_size("ctx") != 4 or lax.axis_size("tp") != 2 or key_rows.shape[1] != 4 * HD:
        return general(queries, key_rows, value_rows, doc_lengths, unit_source, w_out)
    w_out = in_hbm(w_out)
    kv_heads = key_rows.shape[1] // HD
    width = queries.shape[1] // kv_heads
    two = [(0, 2), (1, 3)]
    value_two = lax.ppermute(value_rows, "ctx", two)
    key_two = lax.ppermute(key_rows, "ctx", two)
    key_near = lax.ppermute(key_rows, "ctx", [(0, 1), (1, 2), (2, 3)])
    value_near = lax.ppermute(value_rows, "ctx", [(0, 1), (2, 3)])
    value_far = lax.ppermute(value_two, "ctx", [(3, 2)])
    own_keys, own_values, held, mask, block = prepare(
        doc_lengths, key_rows, value_rows, queries, w_out, width, value_two
    )
    keys = (own_keys, key_near, key_near, key_two)
    values = (own_values, value_near, value_far, value_two)
    state = {"blocks": {(0, 0): block}, "totals": [None] * HALVES, "before": []}
    rows, mine, got = {}, [], []

    def rows_of(groups, after):
        own = attend(groups, width, held, mask, keys, values, after)
        _, _, forward = gather_rows(own)

        def arrive(after):
            rows[groups] = forward(after)
            return rows[groups]

        return own, arrive

    def load(wanted, after):
        blocks, token = load_blocks(
            [(groups[0] * width, len(groups) * width, half) for groups, half in wanted], w_out, after
        )
        for (groups, half), loaded in zip(wanted, blocks):
            state["blocks"][groups[0], half] = loaded
        return token

    def steps(groups, between=None):
        last = groups[-1] == kv_heads - 1
        row = groups[0] * width
        second_block = state["blocks"].get((groups[0], 1))
        first, lhs, following, token = step(
            row, 0, last, (unit_source, rows[groups]), state["blocks"][groups[0], 0],
            w_out if second_block is None else None, state["totals"][0], state["before"],
        )
        if between is not None:
            between(token)
        second, _, _, token = step(
            row, 1, last, lhs, following if second_block is None else second_block, None,
            state["totals"][1], [token],
        )
        state["before"] = [token]
        if last:
            for kept, sent in (first, second):
                mine.append(kept)
                got.append(lax.ppermute(sent, "tp", [(0, 1), (1, 0)]))
        else:
            state["totals"] = [first[0], second[0]]
        return token

    one, two, three, four = (0,), (1,), (2,), (3,)
    rest = three + four
    own, arrive = rows_of(one, [])
    pieces = arrive(None)
    own, arrive = rows_of(two, [load([(one, 1), (two, 0)], own)])
    arrive(None)
    own, arrive = rows_of(three, [load([(rest, 0)], own), pieces[1]])
    side = arrive(None)[2]
    _, arrive = rows_of(four, [own, steps(one)])
    state["before"].append(side)
    steps(two, arrive)
    rows[rest] = rows[three] + rows[four]
    steps(rest)
    half_columns = w_out.shape[1] // HALVES
    out = total(0, w_out.shape[1], mine[:1], got[:1], None)
    return total(half_columns, w_out.shape[1], mine[1:], got[1:], out)


def solution(mesh):
    return jax.shard_map(
        local,
        mesh=mesh,
        in_specs=(
            P(("dp", "ctx"), "tp"),
            P(("dp", "ctx"), "tp"),
            P(("dp", "ctx"), "tp"),
            P("dp"),
            P("dp"),
            P("tp", "ctx"),
        ),
        out_specs=P(("dp", "tp"), "ctx"),
        check_vma=False,
    )
```

```python
import functools
import math

import jax
import jax.numpy as jnp
from jax import lax
from jax.experimental import pallas as pl
from jax.experimental.pallas import tpu as pltpu
from jax.sharding import PartitionSpec as P

HD = 128
MIB = 1 << 20
HALVES = 2


def doc_index(positions, doc_ends):
    return jnp.sum((positions[None, :] >= doc_ends[:, None]).astype(jnp.int32), axis=0)


def general(queries, key_rows, value_rows, doc_lengths, unit_source, w_out):
    ctx_count = lax.axis_size("ctx")
    ctx_index = lax.axis_index("ctx")
    tok_dev, columns = queries.shape
    unit_rows = tok_dev // ctx_count
    head_count = columns // HD
    kv_heads = key_rows.shape[1] // HD
    group_size = head_count // kv_heads
    unit_plan = unit_source.reshape(ctx_count, ctx_count)
    positions = ctx_index * tok_dev + jnp.arange(tok_dev, dtype=jnp.int32)
    doc_ends = jnp.cumsum(doc_lengths)
    query_doc = doc_index(positions, doc_ends)
    grouped = queries.reshape(tok_dev, kv_heads, group_size, HD)
    key_all = lax.all_gather(key_rows, "ctx", axis=0, tiled=True)
    value_all = lax.all_gather(value_rows, "ctx", axis=0, tiled=True)
    extent = key_all.shape[0]
    key_pos = jnp.arange(extent, dtype=jnp.int32)
    key_doc = doc_index(key_pos, doc_ends)
    visible = (key_doc[None, :] == query_doc[:, None]) & (key_pos[None, :] <= positions[:, None])
    scores = jnp.einsum(
        "qkgd,pkd->kgqp",
        grouped,
        key_all.reshape(extent, kv_heads, HD),
        preferred_element_type=jnp.float32,
    ) * (HD ** -0.5)
    scores = jnp.where(visible, scores, -jnp.inf)
    row_max = jnp.max(scores, axis=3, keepdims=True)
    weights = jnp.where(visible, jnp.exp(scores - row_max), 0.0)
    totals = jnp.sum(weights, axis=3)
    blended = jnp.einsum(
        "kgqp,pkd->kgqd",
        weights.astype(jnp.bfloat16),
        value_all.reshape(extent, kv_heads, HD),
        preferred_element_type=jnp.float32,
    )
    attended = (
        (blended / totals[..., None])
        .transpose(2, 0, 1, 3)
        .reshape(tok_dev, columns)
        .astype(jnp.bfloat16)
    )
    gathered = lax.all_gather(attended, "ctx", axis=0, tiled=True)
    units = gathered.reshape(ctx_count * ctx_count, unit_rows, columns)
    balanced = jnp.take(units, unit_plan.reshape(-1), axis=0).reshape(extent, columns)
    partial_value = jnp.dot(balanced, w_out, preferred_element_type=jnp.float32)
    return lax.psum_scatter(
        partial_value.astype(jnp.bfloat16), "tp", scatter_dimension=0, tiled=True
    )


SMEM = pl.BlockSpec(memory_space=pltpu.SMEM)
VMEM = pl.BlockSpec(memory_space=pltpu.VMEM)
HBM = pl.BlockSpec(memory_space=pl.ANY)
TILE = 256


def in_hbm(x):
    return pltpu.with_memory_space_constraint(x, pltpu.HBM)


TOKEN = jax.ShapeDtypeStruct((8, 128), jnp.float32)


def block_shape(w_out, chunks):
    return w_out.shape[0] // chunks, w_out.shape[1] // HALVES


def block_copy(w_hbm, index, w_ref, sem):
    depth, columns = w_ref.shape
    row, column = index // HALVES * depth, index % HALVES * columns
    return pltpu.make_async_copy(
        w_hbm.at[row:row + depth, column:column + columns], w_ref, sem
    )


def prepare_kernel(docs_hbm, k_hbm, v_hbm, q_hbm, w_hbm, after, k_ref, v_ref, q_ref, mask_ref, w_ref, docs, sems):
    lengths = pltpu.make_async_copy(docs_hbm, docs, sems.at[0])
    loads = [
        pltpu.make_async_copy(k_hbm, k_ref, sems.at[1]),
        pltpu.make_async_copy(v_hbm, v_ref, sems.at[2]),
        pltpu.make_async_copy(q_hbm, q_ref, sems.at[3]),
        block_copy(w_hbm, 0, w_ref, sems.at[4]),
    ]
    lengths.start()
    for load in loads:
        load.start()
    lengths.wait()
    rows, window = mask_ref.shape
    base = lax.axis_index("ctx") * rows
    pos = base + lax.broadcasted_iota(jnp.int32, (rows, window), 0)
    start = jnp.zeros((rows, window), jnp.int32)
    end = jnp.int32(0)
    for d in range(docs.shape[0]):
        end = end + docs[d]
        start = jnp.where(pos >= end, end, start)
    key_pos = base + rows - window + lax.broadcasted_iota(jnp.int32, (rows, window), 1)
    mask_ref[...] = jnp.where((key_pos >= start) & (key_pos <= pos), 0.0, -jnp.inf)
    for load in loads:
        load.wait()


def prepare(doc_lengths, key_rows, value_rows, queries, w_out, chunks, after):
    rows = queries.shape[0]
    return pl.pallas_call(
        prepare_kernel,
        out_shape=[
            jax.ShapeDtypeStruct(key_rows.shape, jnp.bfloat16),
            jax.ShapeDtypeStruct(value_rows.shape, jnp.bfloat16),
            jax.ShapeDtypeStruct(queries.shape, jnp.bfloat16),
            jax.ShapeDtypeStruct((rows, 3 * rows), jnp.float32),
            jax.ShapeDtypeStruct(block_shape(w_out, chunks), jnp.bfloat16),
        ],
        in_specs=[HBM] * 6,
        out_specs=[VMEM] * 5,
        scratch_shapes=[
            pltpu.SMEM(doc_lengths.shape, jnp.int32),
            pltpu.SemaphoreType.DMA((5,)),
        ],
        compiler_params=pltpu.CompilerParams(vmem_limit_bytes=4 * MIB),
        cost_estimate=pl.CostEstimate(
            flops=0, bytes_accessed=w_out.size // chunks, transcendentals=0
        ),
        name="prepare",
    )(
        in_hbm(doc_lengths), in_hbm(key_rows), in_hbm(value_rows), in_hbm(queries), w_out, after
    )


def load_kernel(indexes, after, w_hbm, *refs):
    *w_refs, token, sems = refs
    loads = [
        block_copy(w_hbm, index, w_ref, sems.at[i])
        for i, (index, w_ref) in enumerate(zip(indexes, w_refs))
    ]
    for load in loads:
        load.start()
    token[...] = jnp.zeros_like(token)
    for load in loads:
        load.wait()


def load_blocks(indexes, w_out, chunks, after):
    shape = block_shape(w_out, chunks)
    *blocks, token = pl.pallas_call(
        functools.partial(load_kernel, indexes),
        out_shape=[jax.ShapeDtypeStruct(shape, jnp.bfloat16)] * len(indexes) + [TOKEN],
        in_specs=[HBM, HBM],
        out_specs=[VMEM] * (len(indexes) + 1),
        scratch_shapes=[pltpu.SemaphoreType.DMA((len(indexes),))],
        compiler_params=pltpu.CompilerParams(vmem_limit_bytes=1 * MIB),
        cost_estimate=pl.CostEstimate(
            flops=0, bytes_accessed=4 * len(indexes) * shape[0] * shape[1], transcendentals=0
        ),
        name=f"load_{indexes[0]}",
    )(after, w_out)
    return blocks, token


def attend_kernel(groups, q_ref, mask_ref, k0, k2, k_near, k_far, v0, v_near, v_far, v2, *rest):
    out_ref = rest[-1]
    rows = out_ref.shape[0]
    width = out_ref.shape[1] // len(groups)
    heads = width // HD
    window = 3 * rows
    factor = HD ** -0.5 * math.log2(math.e)
    across = lax.axis_index("ctx") == 2
    for i, g in enumerate(groups):
        at = slice(g * HD, (g + 1) * HD)
        k1 = jnp.where(across, k_far[:, at], k_near[:, at])
        v1 = jnp.where(across, v_far[:, at], v_near[:, at])
        keys = jnp.concatenate([k2[:, at], k1, k0[:, at]], axis=0)
        values = jnp.concatenate([v2[:, at], v1, v0[:, at]], axis=0)
        stacked = jnp.concatenate(
            [q_ref[:, g * width + h * HD:g * width + (h + 1) * HD] for h in range(heads)], axis=0
        )
        scores = lax.dot_general(
            stacked, keys, (((1,), (1,)), ((), ())), preferred_element_type=jnp.float32
        ).reshape(heads, rows, window)
        scores = scores + mask_ref[...][None]
        top = jnp.max(scores, axis=2, keepdims=True)
        weights = jnp.exp2((scores - top) * factor)
        total = jnp.sum(weights, axis=2, keepdims=True)
        mixed = jnp.dot(
            weights.astype(jnp.bfloat16).reshape(heads * rows, window),
            values,
            preferred_element_type=jnp.float32,
        ).reshape(heads, rows, HD)
        result = (mixed / total).astype(jnp.bfloat16)
        for h in range(heads):
            out_ref[:, i * width + h * HD:i * width + (h + 1) * HD] = result[h]


def attend(groups, width, queries, mask, keys, values, after):
    rows = queries.shape[0]
    return pl.pallas_call(
        functools.partial(attend_kernel, groups),
        out_shape=jax.ShapeDtypeStruct((rows, len(groups) * width), jnp.bfloat16),
        in_specs=[VMEM] * 10 + [HBM] * len(after),
        out_specs=VMEM,
        compiler_params=pltpu.CompilerParams(vmem_limit_bytes=8 * MIB),
        cost_estimate=pl.CostEstimate(flops=0, bytes_accessed=0, transcendentals=0),
        name=f"attend_{groups[0]}",
    )(queries, mask, *keys, *values, *after)


def lay_out(plan, pieces, column, lhs):
    here = lax.axis_index("ctx")
    core = lax.axis_index("tp")
    first = jnp.where(core == 0, 1, 2)
    owners = [here, here ^ first, here ^ (3 - first), here ^ 3]
    unit_rows = lhs.shape[0] // 16
    swap = jnp.where(core == 0, 8, 0)
    wanted = [plan[slot] for slot in range(16)]
    for owner, piece in zip(owners, pieces):
        for u in range(4):
            slot = jnp.int32(0)
            for s in range(1, 16):
                slot = jnp.where(wanted[s] == owner * 4 + u, s, slot)
            slot = slot ^ swap
            at = pl.ds(pl.multiple_of(slot * unit_rows, unit_rows), unit_rows)
            lhs[at, :] = piece[u * unit_rows:(u + 1) * unit_rows, column:column + lhs.shape[1]]


def step_kernel(index, last, column, first, columns, has_acc, has_after, has_load, *refs):
    refs = list(refs)[has_after:]
    first_half = index % HALVES == 0
    load = None
    if has_load:
        sem = refs.pop()
    token = refs.pop()
    if has_load:
        load = block_copy(refs.pop(0), index + 1, refs.pop(), sem)
        load.start()
    if first_half:
        plan, *pieces = refs[:5]
        del refs[:5]
        lhs = refs.pop()
        lay_out(plan, pieces, column, lhs)
    else:
        lhs = refs.pop(0)
    token[...] = jnp.zeros_like(token)
    w_ref = refs.pop(0)
    acc_ref = refs.pop(0) if has_acc else None
    rows = lhs.shape[0] // 2
    for start in range(0, columns, TILE):
        to = slice(start, start + TILE)
        at = slice(first + start, first + start + TILE)
        product = jnp.dot(lhs[...], w_ref[:, at], preferred_element_type=jnp.float32)
        if has_acc:
            product = product + acc_ref[:, at]
        if last:
            own_ref, sent_ref = refs
            own_ref[:, to] = product[rows:]
            sent_ref[:, to] = product[:rows].astype(jnp.bfloat16)
        else:
            refs[0][:, to] = product
    if load is not None:
        load.wait()


def step(index, last, rows_in, column, block, first, columns, w_out, acc, after):
    first_half = index % HALVES == 0
    has_acc, has_after, has_load = acc is not None, after is not None, w_out is not None
    depth = block.shape[0]
    if first_half:
        plan, pieces = rows_in
        total_rows = 4 * pieces[0].shape[0]
        operands, specs = [plan, *pieces], [SMEM] + [VMEM] * 4
    else:
        total_rows = rows_in.shape[0]
        operands, specs = [rows_in], [VMEM]
    if last:
        part = (total_rows // 2, columns)
        shapes = [jax.ShapeDtypeStruct(part, jnp.float32), jax.ShapeDtypeStruct(part, jnp.bfloat16)]
    else:
        shapes = [jax.ShapeDtypeStruct((total_rows, columns), jnp.float32)]
    if first_half:
        shapes.append(jax.ShapeDtypeStruct((total_rows, depth), jnp.bfloat16))
    if has_load:
        shapes.append(jax.ShapeDtypeStruct(block.shape, jnp.bfloat16))
    shapes.append(TOKEN)
    operands = [after] * has_after + [w_out] * has_load + operands + [block] + [acc] * has_acc
    specs = [HBM] * (has_after + has_load) + specs + [VMEM] * (1 + has_acc)
    results = list(pl.pallas_call(
        functools.partial(
            step_kernel, index, last, column, first, columns, has_acc, has_after, has_load
        ),
        out_shape=shapes,
        in_specs=specs,
        out_specs=[VMEM] * len(shapes),
        scratch_shapes=[pltpu.SemaphoreType.DMA] * has_load,
        input_output_aliases={len(operands) - 1: 0} if has_acc and not last else {},
        compiler_params=pltpu.CompilerParams(vmem_limit_bytes=6 * MIB),
        cost_estimate=pl.CostEstimate(
            flops=2 * total_rows * depth * columns, bytes_accessed=0, transcendentals=0
        ),
        name=f"step_{index}_{first // columns}",
    )(*operands))
    token = results.pop()
    following = results.pop() if has_load else None
    lhs = results.pop() if first_half else rows_in
    return results, lhs, following, token


def total_kernel(first, count, has_out, *refs):
    own_refs, got_refs = refs[:count], refs[count:2 * count]
    out_hbm, buf, sems = refs[2 * count + has_out:]
    writes, at = [], 0
    for own_ref, got_ref in zip(own_refs, got_refs):
        columns = own_ref.shape[1]
        for start in range(0, columns, 2 * TILE):
            to = slice(start, start + 2 * TILE)
            value = own_ref[:, to] + got_ref[:, to].astype(jnp.float32)
            here = slice(at + start, at + start + 2 * TILE)
            there = slice(first + at + start, first + at + start + 2 * TILE)
            buf[:, here] = value.astype(jnp.bfloat16)
            write = pltpu.make_async_copy(buf.at[:, here], out_hbm.at[:, there], sems.at[len(writes)])
            write.start()
            writes.append(write)
        at += columns
    for write in writes:
        write.wait()


def total(first, width, own, got, out):
    rows = own[0].shape[0]
    columns = sum(x.shape[1] for x in own)
    count, has_out = len(own), out is not None
    return pl.pallas_call(
        functools.partial(total_kernel, first, count, has_out),
        out_shape=jax.ShapeDtypeStruct((rows, width), jnp.bfloat16),
        in_specs=[VMEM] * (2 * count) + [HBM] * has_out,
        out_specs=HBM,
        scratch_shapes=[
            pltpu.VMEM((rows, columns), jnp.bfloat16),
            pltpu.SemaphoreType.DMA((columns // (2 * TILE),)),
        ],
        input_output_aliases={2 * count: 0} if has_out else {},
        compiler_params=pltpu.CompilerParams(vmem_limit_bytes=4 * MIB),
        cost_estimate=pl.CostEstimate(
            flops=rows * columns, bytes_accessed=2 * rows * columns, transcendentals=0
        ),
        name=f"total_{first}",
    )(*own, *got, *([out] if has_out else []))


def gate_kernel(x, after, out):
    pass


def gate(x, after):
    return pl.pallas_call(
        gate_kernel,
        out_shape=jax.ShapeDtypeStruct(x.shape, x.dtype),
        in_specs=[HBM, HBM],
        out_specs=HBM,
        input_output_aliases={0: 0},
        compiler_params=pltpu.CompilerParams(vmem_limit_bytes=1 * MIB),
        cost_estimate=pl.CostEstimate(flops=0, bytes_accessed=0, transcendentals=0),
        name="gate",
    )(x, after)


def gather_rows(own):
    def route(first):
        pairs = []
        for chip in range(4):
            for core in range(2):
                axis = 1 if (core == 0) == first else 2
                pairs.append((chip * 2 + core, (chip ^ axis) * 2 + core))
        return pairs

    near = lax.ppermute(own, ("ctx", "tp"), route(True))
    side = lax.ppermute(own, ("ctx", "tp"), route(False))

    def forward(after):
        first = near if after is None else gate(near, after)
        return own, first, side, lax.ppermute(first, ("ctx", "tp"), route(False))

    return near, side, forward


def local(queries, key_rows, value_rows, doc_lengths, unit_source, w_out):
    if lax.axis_size("ctx") != 4 or lax.axis_size("tp") != 2 or key_rows.shape[1] != 4 * HD:
        return general(queries, key_rows, value_rows, doc_lengths, unit_source, w_out)
    w_out = in_hbm(w_out)
    kv_heads = key_rows.shape[1] // HD
    width = queries.shape[1] // kv_heads
    two = [(0, 2), (1, 3)]
    value_two = lax.ppermute(value_rows, "ctx", two)
    key_two = lax.ppermute(key_rows, "ctx", two)
    key_near = lax.ppermute(key_rows, "ctx", [(0, 1), (1, 2), (2, 3)])
    value_near = lax.ppermute(value_rows, "ctx", [(0, 1), (2, 3)])
    value_far = lax.ppermute(value_two, "ctx", [(3, 2)])
    own_keys, own_values, held, mask, block = prepare(
        doc_lengths, key_rows, value_rows, queries, w_out, kv_heads, value_two
    )
    keys = (own_keys, key_two, key_near, key_near)
    values = (own_values, value_near, value_far, value_two)
    half_columns = w_out.shape[1] // HALVES
    state = {"blocks": {0: block}, "totals": [None] * HALVES, "before": None}
    rows, mine, got = {}, [], []

    def rows_of(groups, after):
        own = attend(groups, width, held, mask, keys, values, after)
        near, side, forward = gather_rows(own)

        def arrive(after):
            pieces = forward(after)
            for i, g in enumerate(groups):
                rows[g] = (pieces, i * width)
            return pieces[1]

        return own, arrive

    def load(wanted, after):
        loaded, token = load_blocks(wanted, w_out, kv_heads, after)
        state["blocks"].update(zip(wanted, loaded))
        return token

    def steps(g):
        last = g == kv_heads - 1
        pieces, column = rows[g]
        loads = g * HALVES + 1 not in state["blocks"]
        first, lhs, following, state["before"] = step(
            g * HALVES, last, (unit_source, pieces), column, state["blocks"][g * HALVES], 0,
            half_columns,
            w_out if loads else None, state["totals"][0], state["before"],
        )
        if loads:
            state["blocks"][g * HALVES + 1] = following
        second, _, _, state["before"] = step(
            g * HALVES + 1, last, lhs, column, state["blocks"][g * HALVES + 1], 0,
            half_columns, None,
            state["totals"][1], state["before"],
        )
        if last:
            for kept, sent in (first, second):
                mine.append(kept)
                got.append(lax.ppermute(sent, "tp", [(0, 1), (1, 0)]))
        else:
            state["totals"] = [first[0], second[0]]
        return state["before"]

    own, arrive = rows_of((0,), [])
    near = arrive(None)
    own, arrive = rows_of((1,), [load((1, 2), own)])
    arrive(None)
    own, arrive = rows_of((2,), [load((4, 6), own), near])
    arrive(None)
    own, arrive = rows_of((3,), [own, steps(0)])
    arrive(None)
    for g in range(1, kv_heads):
        steps(g)
    out = total(0, w_out.shape[1], mine[:1], got[:1], None)
    return total(half_columns, w_out.shape[1], mine[1:], got[1:], out)


def solution(mesh):
    return jax.shard_map(
        local,
        mesh=mesh,
        in_specs=(
            P(("dp", "ctx"), "tp"),
            P(("dp", "ctx"), "tp"),
            P(("dp", "ctx"), "tp"),
            P("dp"),
            P("dp"),
            P("tp", "ctx"),
        ),
        out_specs=P(("dp", "tp"), "ctx"),
        check_vma=False,
    )
```
